128 devices in a mesh: seq: 16 (over x_hi, z, core), fsdp: 8 (over y, x_lo).
Axes of the slice: x: 4 (x_hi: 2, x_lo: 2; x = x_hi * 2 + x_lo), y: 4, z: 4, core: 2. Of those that a mesh axis runs over, the one named last changes fastest.
Arguments:
- inputs: bfloat16 [16, 1024, 1024], P('seq', 'fsdp'), may hold values from -6 to 6
- doc_ids: int32 [16, 1024], replicated, may hold values from 0 to 1, as said below
- positions: int32 [16, 1024], P('seq', 'fsdp'), may hold values from 0 to 1023, as said below
- attn_gain: bfloat16 [1024], P('fsdp'), may hold values from 0.5 to 1.5
- query_weight: bfloat16 [1024, 1024], P('fsdp'), may hold values from -0.1875 to 0.1875
- key_weight: bfloat16 [1024, 1024], P('fsdp'), may hold values from -0.1875 to 0.1875
- value_weight: bfloat16 [1024, 1024], P('fsdp'), may hold values from -0.1875 to 0.1875
- query_bias: bfloat16 [1024], P('fsdp'), may hold values from -3 to 3
- key_bias: bfloat16 [1024], P('fsdp'), may hold values from -3 to 3
- value_bias: bfloat16 [1024], P('fsdp'), may hold values from -3 to 3
- out_weight: bfloat16 [1024, 1024], P('fsdp'), may hold values from -0.75 to 0.75
- mlp_gain: bfloat16 [1024], P('fsdp'), may hold values from 0.5 to 1.5
- gate_weight: bfloat16 [1024, 2816], P('fsdp'), may hold values from -0.1875 to 0.1875
- up_weight: bfloat16 [1024, 2816], P('fsdp'), may hold values from -0.1875 to 0.1875
- down_weight: bfloat16 [2816, 1024], P(None, 'fsdp'), may hold values from -0.109375 to 0.109375
- cotangent: bfloat16 [16, 1024, 1024], P('seq', 'fsdp'), may hold values from -6 to 6
Outputs:
- layer_out: bfloat16 [16, 1024, 1024], P('seq', 'fsdp')
- input_grad: float32 [16, 1024, 1024], P('seq', 'fsdp')
- attn_gain_grad: float32 [1024], P('fsdp')
- query_weight_grad: float32 [1024, 1024], P('fsdp')
- key_weight_grad: float32 [1024, 1024], P('fsdp')
- value_weight_grad: float32 [1024, 1024], P('fsdp')
- query_bias_grad: float32 [1024], P('fsdp')
- key_bias_grad: float32 [1024], P('fsdp')
- value_bias_grad: float32 [1024], P('fsdp')
- out_weight_grad: float32 [1024, 1024], P('fsdp')
- mlp_gain_grad: float32 [1024], P('fsdp')
- gate_weight_grad: float32 [1024, 2816], P('fsdp')
- up_weight_grad: float32 [1024, 2816], P('fsdp')
- down_weight_grad: float32 [2816, 1024], P(None, 'fsdp')
The draws below stay inside these ranges and needn't reach their ends.
Inputs may be any that keep to these rules, and one draw needn't show every extreme that they name: `doc_ids`: in each sequence the document number is 0 on a leading run of positions and 1 on the rest; in some sequences the run covers the whole sequence. Within a document the positions rise by one from token to token; the first document of each sequence starts at 0, the second at a position below the first's length.
All inputs are finite; a program needn't handle non-finite values.
Results may differ from the reference program's by a relative error of at most 0.023.
Values may be sent and summed in bfloat16 or wider, within the bound.
A program may use at most 256 MiB of HBM per device.

```python
import math
import jax
import jax.numpy as jnp
from jax import lax

D = 1024
HEADS = 16
HEAD_DIM = 64
FF = 2816
LEN = 1024
BATCH = 16


def packing(key):
    key_bound, key_single, key_offset = jax.random.split(key, 3)
    doc_bound = jax.random.randint(key_bound, (BATCH,), 1, LEN)
    chosen = jax.random.randint(key_single, (), 0, 4)
    seq_index = jnp.arange(BATCH, dtype=jnp.int32)
    doc_bound = jnp.where(seq_index % 4 == chosen, LEN, doc_bound)
    offset = jax.random.randint(key_offset, (BATCH,), 0, doc_bound)
    return (doc_bound, offset)


def draw_doc_ids(key, part):
    doc_bound, offset = packing(key)
    token_place = jnp.arange(LEN, dtype=jnp.int32)[None, :]
    return (token_place >= doc_bound[:, None]).astype(jnp.int32)


def draw_positions(key, part):
    doc_bound, offset = packing(key)
    token_place = jnp.arange(LEN, dtype=jnp.int32)[None, :]
    later = offset[:, None] + token_place - doc_bound[:, None]
    return jnp.where(token_place < doc_bound[:, None], token_place, later).astype(jnp.int32)


def with_spikes(values, key, source, target, blocks, factor):
    def block_of(axis_at):
        return (jnp.arange(values.shape[axis_at]) // (values.shape[axis_at] // blocks)).reshape((-1,) + (1,) * (values.ndim - 1 - axis_at))

    one_side = jax.random.permutation(key, blocks)[block_of(target)]
    far = (block_of(target) + blocks // 2) % blocks
    return jnp.where((block_of(source) == one_side) | (block_of(source) == far), factor * values, values)


def level_of(own_key, dims, cuts, smallest, high):
    gain = 1.0
    for axis_at, parts in cuts:
        draws = jax.random.uniform(jax.random.fold_in(jax.random.fold_in(own_key, 6), axis_at), (parts,), jnp.float32, smallest / len(cuts), high / len(cuts))
        gain = gain * jnp.repeat(jnp.exp(draws), dims[axis_at] // parts).reshape((-1,) + (1,) * (len(dims) - 1 - axis_at))
    return gain


def centred(own_key, dims, spread, reach, shards=(), kind=jnp.bfloat16):
    values = jax.random.normal(own_key, dims, jnp.float32) * spread
    if len(shards) > 0:
        values = level_of(own_key, dims, shards, -0.22, 0.18) * values
    return jnp.clip(values, min=-reach, max=reach).astype(kind)


def heavy_noise(own_key, shape, width, bound, cuts, heavy, kind=jnp.bfloat16):
    array = width * jax.random.normal(own_key, shape, jnp.float32)
    if cuts:
        array = array * level_of(own_key, shape, cuts, -0.22, 0.18)
    return jnp.clip(with_spikes(array, jax.random.fold_in(own_key, 3), *heavy), -bound, bound).astype(kind)


def setup_inputs(seed: int = 0) -> dict:
    keys = jax.random.split(jax.random.key(seed), 17)
    inputs = centred(keys[0], (BATCH, LEN, D), 1.0, 6.0, ((0, 16), (1, 8)))
    doc_ids = draw_doc_ids(jax.random.fold_in(keys[16], 71), 0)
    positions = draw_positions(jax.random.fold_in(keys[16], 71), 0)
    attn_gain = jnp.clip(1.0 + 0.1 * jax.random.normal(keys[3], (D,), jnp.float32), 0.5, 1.5).astype(jnp.bfloat16)
    query_weight = centred(keys[4], (D, D), D ** -0.5, 0.1875, ((0, 8),))
    key_weight = centred(keys[5], (D, D), D ** -0.5, 0.1875, ((0, 8),))
    value_weight = centred(keys[6], (D, D), D ** -0.5, 0.1875, ((0, 8),))
    query_bias = centred(keys[7], (D,), 0.5, 3.0, ((0, 8),))
    key_bias = centred(keys[8], (D,), 0.5, 3.0, ((0, 8),))
    value_bias = centred(keys[9], (D,), 0.5, 3.0, ((0, 8),))
    out_weight = centred(keys[10], (D, D), HEAD_DIM ** -0.5, 0.75, ((0, 8),))
    mlp_gain = jnp.clip(1.0 + 0.1 * jax.random.normal(keys[11], (D,), jnp.float32), 0.5, 1.5).astype(jnp.bfloat16)
    gate_weight = centred(keys[12], (D, FF), D ** -0.5, 0.1875, ((0, 8),))
    up_weight = centred(keys[13], (D, FF), D ** -0.5, 0.1875, ((0, 8),))
    down_weight = centred(keys[14], (FF, D), FF ** -0.5, 0.109375, ((1, 8),))
    cotangent = heavy_noise(keys[15], (BATCH, LEN, D), 1.0, 6.0, ((0, 16), (1, 8)), (0, 2, 16, 2.0))
    return {"inputs": inputs, "doc_ids": doc_ids, "positions": positions, "attn_gain": attn_gain, "query_weight": query_weight, "key_weight": key_weight, "value_weight": value_weight, "query_bias": query_bias, "key_bias": key_bias, "value_bias": value_bias, "out_weight": out_weight, "mlp_gain": mlp_gain, "gate_weight": gate_weight, "up_weight": up_weight, "down_weight": down_weight, "cotangent": cotangent}


EPS = 1e-06
THETA = 1000000.0
NEG = -1000000000.0

@jax.custom_vjp
def low(v):
    return lax.optimization_barrier(v.astype(jnp.bfloat16)).astype(jnp.float32)

@jax.custom_vjp
def low_back(v):
    return v

def low_keep(v):
    return (low(v), None)

def low_pass(kept, grad):
    return (grad,)

def back_keep(v):
    return (v, None)

def back_low(kept, grad):
    return (low(grad),)
low.defvjp(low_keep, low_pass)
low_back.defvjp(back_keep, back_low)

def product(left_op, right_op):
    return jnp.dot(left_op, right_op, precision=lax.Precision.HIGHEST)

def rms_scale(tensor):
    return lax.rsqrt(lax.optimization_barrier(jnp.mean(tensor * tensor, axis=-1, keepdims=True)) + EPS)

def turn_half(tensor):
    half_dim = tensor.shape[-1] // 2
    return jnp.concatenate([-tensor[..., half_dim:], tensor[..., :half_dim]], axis=-1)

def rotary_tables(positions):
    exponent = jnp.arange(HEAD_DIM // 2, dtype=jnp.float32) * (2.0 / HEAD_DIM)
    inverse = jnp.exp(-math.log(THETA) * exponent)
    angles = positions.astype(jnp.float32)[..., None] * inverse
    angles = jnp.concatenate([angles, angles], axis=-1)
    return (jnp.cos(angles)[..., None, :], jnp.sin(angles)[..., None, :])

def head_attention(query_rows, key_rows, value_rows, same_doc):
    scaling_factor = 1.0 / math.sqrt(HEAD_DIM)
    logit_scores = low_back(jnp.einsum('pfi,pzi->pfz', query_rows, key_rows, precision=lax.Precision.HIGHEST) * scaling_factor)
    logit_scores = jnp.where(same_doc, logit_scores, NEG)
    row_max = lax.optimization_barrier(jnp.max(logit_scores, axis=-1, keepdims=True))
    weights = jnp.exp(logit_scores - row_max)
    attention_weights = low(weights / lax.optimization_barrier(jnp.sum(weights, axis=-1, keepdims=True)))
    return jnp.einsum('rfo,rop->rfp', attention_weights, value_rows, precision=lax.Precision.HIGHEST)

def full_layer(weights, inputs, same_doc, cos_table, sin_table):
    attn_gain, query_w, key_w, value_w, query_b, key_b, value_b, out_w, mlp_gain, gate_w, up_w, down_w = weights
    seq_count, length, model_width = inputs.shape
    flat_in = inputs.reshape(seq_count * length, model_width)
    normed = low(flat_in * rms_scale(flat_in) * attn_gain)

    def project(matrix, bias_vec):
        return (product(normed, matrix) + bias_vec).reshape(seq_count, length, HEADS, HEAD_DIM)

    def rotated(matrix, bias_vec):
        unrotated = low_back(project(matrix, bias_vec))
        return low(low_back(unrotated * cos_table + turn_half(unrotated) * sin_table))
    query_rows = rotated(query_w, query_b)
    key_rows = rotated(key_w, key_b)
    value_rows = low(low_back(project(value_w, value_b)))
    attend = jax.checkpoint(lambda block_in: head_attention(block_in[0], block_in[1], block_in[2], same_doc))
    mixed_out = lax.map(attend, (jnp.moveaxis(query_rows, 2, 0), jnp.moveaxis(key_rows, 2, 0), jnp.moveaxis(value_rows, 2, 0)))
    mixed_out = low(low_back(jnp.moveaxis(mixed_out, 0, 2).reshape(seq_count * length, model_width)))
    hidden = flat_in + low_back(product(mixed_out, out_w))
    normed_mlp = low(hidden * rms_scale(hidden) * mlp_gain)
    gate_val = low_back(product(normed_mlp, gate_w))
    up_val = low_back(product(normed_mlp, up_w))
    active = low(jax.nn.silu(gate_val) * up_val)
    result = hidden + product(active, down_w)
    return result.reshape(seq_count, length, model_width)

def reference(inputs, doc_ids, positions, attn_gain, query_weight, key_weight, value_weight, query_bias, key_bias, value_bias, out_weight, mlp_gain, gate_weight, up_weight, down_weight, cotangent):
    weights = tuple((tensor.astype(jnp.float32) for tensor in (attn_gain, query_weight, key_weight, value_weight, query_bias, key_bias, value_bias, out_weight, mlp_gain, gate_weight, up_weight, down_weight)))
    group_size = math.gcd(BATCH, max(1, 4096 // LEN))
    step_count = BATCH // group_size
    token_index = jnp.arange(LEN, dtype=jnp.int32)
    causal = token_index[:, None] >= token_index[None, :]

    def grouped(tensor):
        return tensor.reshape((step_count, group_size) + tensor.shape[1:])

    def one_group(totals, block_in):
        inputs_b, docs_b, positions_b, cot_b = block_in
        same_doc = (docs_b[:, :, None] == docs_b[:, None, :]) & causal
        cos_table, sin_table = rotary_tables(positions_b)

        def forward(weights_in, inputs_in):
            return full_layer(weights_in, inputs_in, same_doc, cos_table, sin_table)
        result, pullback = jax.vjp(forward, weights, inputs_b.astype(jnp.float32))
        grads_w, grads_x = pullback(cot_b.astype(jnp.float32))
        totals = jax.tree.map(lambda first_part, second: first_part + second, totals, grads_w)
        return (totals, (result.astype(jnp.bfloat16), grads_x))
    zero_grads = jax.tree.map(jnp.zeros_like, weights)
    totals, (outputs, grads_in) = lax.scan(one_group, zero_grads, (grouped(inputs), grouped(doc_ids), grouped(positions), grouped(cotangent)))
    return (outputs.reshape(inputs.shape), grads_in.reshape(inputs.shape), totals[0], totals[1], totals[2], totals[3], totals[4], totals[5], totals[6], totals[7], totals[8], totals[9], totals[10], totals[11])
```

```python
import math

import jax
import jax.numpy as jnp
from jax import lax
from jax.experimental import pallas as pl
from jax.experimental.pallas import tpu as pltpu
from jax.sharding import PartitionSpec as P

MESH = pl.DeviceIdType.MESH
HEAD_DIM = 64
EPS = 1e-06
THETA = 1000000.0
NEG = -1000000000.0
D = 1024
PIECE = 128
BLOCK = 256
FB = 384
F32 = jnp.float32
BF16 = jnp.bfloat16


def nn(a, b):
    return lax.dot_general(a, b, (((1,), (0,)), ((), ())), preferred_element_type=F32)


def nt(a, b):
    return lax.dot_general(a, b, (((1,), (1,)), ((), ())), preferred_element_type=F32)


def tn(a, b):
    return lax.dot_general(a, b, (((0,), (0,)), ((), ())), preferred_element_type=F32)


def rms_scale(value):
    return lax.rsqrt(jnp.mean(value * value, axis=-1, keepdims=True) + EPS)


def rows(start, size):
    return pl.ds(pl.multiple_of(start, size), size)


def half_turn(value):
    lane = lax.broadcasted_iota(jnp.int32, value.shape, 1)
    ahead = pltpu.roll(value, 96, 1)
    behind = pltpu.roll(value, 32, 1)
    return jnp.where(lane % 64 < 32, ahead, behind)


def layer_kernel(
    x_in, cot_in, wq_in, wk_in, wv_in, wo_in, wg_in, wu_in, wd_in,
    vec_in, cos_ref, sin_ref, start_ref,
    layer_out, in_grad, grads_a, grads_b, vec_out,
    x_own, cot_own, hidden, g_hidden, wo, wqkv, wgu, wdn, vall,
    normed_all, cot_all, mlp_all, branch_all,
    q_h, k_h, v_h, k_t, v_t, p_t, mixed_t, mixed,
    g_act, active, g_gu, g_mixed, gk_acc, gv_acc, g_qkv,
    part, sib, far_s, far_r, fin_s, fin_r,
    dgu, ddn, dwo, dqkv, rgu, rdn, rwo, rqkv, wo_send, wo_recv,
    lo_send, ig_send, lo_recv, ig_recv,
    vs, vr, v2s, v2r,
    sem_load, swap_s, swap_r, vec_s, vec_r, w_s, w_r, ag_s, ag_r,
    sib_ss, sib_rs, far_ss, far_rs, fin_ss, fin_rs,
    pl_s, pl_r, ga_s, ga_r, v1_ss, v1_rs, v2_ss, v2_rs,
):
    s = lax.axis_index("seq")
    f = lax.axis_index("fsdp")
    xh = s // 8
    j = s % 8
    z = j // 2
    c = j % 2
    y = f // 2
    x = xh * 2 + f % 2

    def dev(x_, y_, z_, c_):
        x_, y_, z_ = (x_ + 4) % 4, (y_ + 4) % 4, (z_ + 4) % 4
        return ((x_ // 2) * 8 + z_ * 2 + c_, y_ * 2 + x_ % 2)

    sibling = dev(x, y, z, 1 - c)
    z_up = dev(x, y, z + 1, c)
    z_dn = dev(x, y, z + 3, c)
    partner = (xh * 8 + f, j)
    x_to = dev(x + 1 + 2 * c, y, z, c)
    win = (3 * j - 2 * (j // 7)) * 128

    def remote(src, dst, ss, rs, to):
        return pltpu.make_async_remote_copy(
            src_ref=src, dst_ref=dst, send_sem=ss, recv_sem=rs, device_id=to, device_id_type=MESH
        )

    loads = [
        pltpu.make_async_copy(wq_in.at[:, rows(j * 128, 128)], wqkv.at[rows(f * 128, 128), pl.ds(0, 128)], sem_load.at[0]),
        pltpu.make_async_copy(wk_in.at[:, rows(j * 128, 128)], wqkv.at[rows(f * 128, 128), pl.ds(128, 128)], sem_load.at[1]),
        pltpu.make_async_copy(wv_in.at[:, rows(j * 128, 128)], wqkv.at[rows(f * 128, 128), pl.ds(256, 128)], sem_load.at[2]),
        pltpu.make_async_copy(wg_in.at[:, pl.ds(pl.multiple_of(win, 128), FB)], wgu.at[rows(f * 128, 128), pl.ds(0, FB)], sem_load.at[3]),
        pltpu.make_async_copy(wu_in.at[:, pl.ds(pl.multiple_of(win, 128), FB)], wgu.at[rows(f * 128, 128), pl.ds(FB, FB)], sem_load.at[4]),
        pltpu.make_async_copy(wd_in.at[pl.ds(pl.multiple_of(win, 128), FB), :], wdn.at[:, rows(f * 128, 128)], sem_load.at[5]),
    ]
    for load in loads:
        load.start()

    barrier = pltpu.get_barrier_semaphore()

    def greet_plane(r, carry):
        pl.semaphore_signal(barrier, inc=1, device_id=dev(x + r // 4, y + r % 4, z, c), device_id_type=MESH)
        return carry

    def greet_seq(r, carry):
        pl.semaphore_signal(barrier, inc=1, device_id=((s + r) % 16, f), device_id_type=MESH)
        return carry

    lax.fori_loop(1, 16, greet_plane, 0)
    lax.fori_loop(1, 16, greet_seq, 0)

    @pl.when(j != f)
    def _():
        pl.semaphore_signal(barrier, inc=1, device_id=partner, device_id_type=MESH)
        pl.semaphore_wait(barrier, 31)

    @pl.when(j == f)
    def _():
        pl.semaphore_wait(barrier, 30)

    def swap_start(src, dst, n):
        @pl.when(j != f)
        def _():
            remote(src, dst, swap_s.at[n], swap_r.at[n], partner).start()

        @pl.when(j == f)
        def _():
            pltpu.make_async_copy(src, dst, swap_r.at[n]).start()

    def swap_wait(src, dst, n):
        @pl.when(j != f)
        def _():
            remote(src, dst, swap_s.at[n], swap_r.at[n], partner).wait()

        @pl.when(j == f)
        def _():
            pltpu.make_async_copy(src, dst, swap_r.at[n]).wait()

    x_src = x_in
    cot_src = cot_in
    swap_start(x_src, x_own, 0)

    def vec_copy(r):
        return remote(vec_in, vall.at[f], vec_s.at[r], vec_r.at[r], (s, (f + r) % 8))

    def vec_start(r, carry):
        vec_copy(r).start()
        return carry

    def vec_wait(r, carry):
        vec_copy(r).wait()
        return carry

    lax.fori_loop(1, 8, vec_start, 0)
    vall[pl.ds(f, 1)] = vec_in[...][None]

    def w_slice(n, f_):
        if n == 0:
            return wqkv.at[rows(f_ * 128, 128)]
        if n == 1:
            return wgu.at[rows(f_ * 128, 128)]
        return wdn.at[:, rows(f_ * 128, 128)]

    def w_y(n, r):
        ref = w_slice(n, f)
        return remote(ref, ref, w_s.at[n, r], w_r.at[n, r], dev(x, y + r, z, c))

    def w_x(n, r):
        ref = w_slice(n, ((y + 4 - r) % 4) * 2 + f % 2)
        return remote(ref, ref, w_s.at[n, 4 + r], w_r.at[n, 4 + r], x_to)

    def w_x_in(n, r):
        ref = w_slice(n, ((y + 4 - r) % 4) * 2 + 1 - f % 2)
        return remote(ref, ref, w_s.at[n, 4 + r], w_r.at[n, 4 + r], x_to)

    def w_y_in(n, r):
        ref = w_slice(n, ((y + 4 - r) % 4) * 2 + f % 2)
        return remote(ref, ref, w_s.at[n, r], w_r.at[n, r], dev(x, y + r, z, c))

    def w_start(n):
        for r in (1, 3, 2):
            w_y(n, r).start()
        w_x(n, 0).start()

    def w_forward(n):
        for r in (1, 3, 2):
            w_y_in(n, r).wait_recv()
            w_x(n, r).start()

    def w_finish(n):
        for r in range(4):
            w_x_in(n, r).wait_recv()

    for load in loads[:3]:
        load.wait()
    w_start(0)
    swap_start(wo_in, wo, 1)
    swap_start(cot_src, cot_own, 2)

    def piece(buf, z_, c_):
        return buf.at[rows((((z_ + 4) % 4) * 2 + c_) * PIECE, PIECE)]

    def half(buf, z_, c_, h):
        return buf.at[rows((((z_ + 4) % 4) * 2 + c_) * PIECE + h * 64, 64)]

    def ag(buf, k, n, recv=False):
        if n == 0:
            ref, to = (piece(buf, z - 1, c) if recv else piece(buf, z, c)), z_up
        elif n == 1:
            ref, to = (piece(buf, z + 1, c) if recv else piece(buf, z, c)), z_dn
        elif n == 2:
            ref, to = (piece(buf, z, 1 - c) if recv else piece(buf, z, c)), sibling
        elif n == 3:
            ref, to = (half(buf, z - 2, c, 0) if recv else half(buf, z - 1, c, 0)), z_up
        elif n == 4:
            ref, to = (piece(buf, z - 1, 1 - c) if recv else piece(buf, z - 1, c)), sibling
        elif n == 5:
            ref, to = (half(buf, z + 2, c, 1) if recv else half(buf, z + 1, c, 1)), z_dn
        elif n == 6:
            ref, to = (piece(buf, z + 1, 1 - c) if recv else piece(buf, z + 1, c)), sibling
        else:
            ref, to = (piece(buf, z + 2, 1 - c) if recv else piece(buf, z + 2, c)), sibling
        return remote(ref, ref, ag_s.at[k, n], ag_r.at[k, n], to)

    def ag_start(buf, k):
        for n in range(3):
            ag(buf, k, n).start()

    def ag_near(buf, k):
        ag(buf, k, 0, True).wait_recv()
        ag(buf, k, 3).start()
        ag(buf, k, 4).start()
        ag(buf, k, 1, True).wait_recv()
        ag(buf, k, 5).start()
        ag(buf, k, 6).start()

    def ag_far(buf, k):
        ag(buf, k, 3, True).wait_recv()
        ag(buf, k, 5, True).wait_recv()
        ag(buf, k, 7).start()

    def ag_run(buf, k, consume):
        def step(i, carry):
            @pl.when(i == 0)
            def _():
                ag(buf, k, 2, True).wait_recv()

            @pl.when(i == 1)
            def _():
                ag_near(buf, k)
                ag(buf, k, 4, True).wait_recv()

            @pl.when(i == 2)
            def _():
                ag(buf, k, 6, True).wait_recv()

            @pl.when(i == 3)
            def _():
                ag_far(buf, k)
                ag(buf, k, 7, True).wait_recv()

            consume((z + (3 * ((i * (i + 1)) // 2)) % 4) % 4)
            return carry

        lax.fori_loop(0, 4, step, 0)

    def other(i):
        return part.at[i, rows((1 - c) * PIECE, PIECE)]

    def own_part(i):
        return part[i, rows(c * PIECE, PIECE), :].astype(F32)

    def c_sib(k, i):
        return remote(other(i), sib.at[k, i], sib_ss.at[k, i], sib_rs.at[k, i], sibling)

    def c_far(k, n):
        return remote(far_s.at[k, pl.ds(64 * n, 64)], far_r.at[k, n], far_ss.at[k, n], far_rs.at[k, n], z_up if n == 0 else z_dn)

    def c_fin(k, n, h):
        cut = pl.ds(64 * h, 64)
        return remote(fin_s.at[k, n, cut], fin_r.at[k, n, cut], fin_ss.at[k, n, h], fin_rs.at[k, n, h], z_up if n == 0 else z_dn)

    def rs_start(k, produce):
        def step(i, carry):
            if k > 0:
                c_sib(k - 1, i).wait_send()
            part[i] = produce((z + (2 - (i * (i + 1)) // 2 + 8) % 4) % 4).astype(BF16)
            c_sib(k, i).start()

            @pl.when(i == 1)
            def _():
                c_sib(k, 0).wait_recv()
                far_s[k] = (own_part(0) + sib[k, 0].astype(F32)).astype(BF16)
                c_far(k, 0).start()
                c_far(k, 1).start()

            @pl.when(i == 2)
            def _():
                c_sib(k, 1).wait_recv()
                fin_s[k, 0] = (own_part(1) + sib[k, 1].astype(F32)).astype(BF16)
                c_fin(k, 0, 1).start()

            @pl.when(i == 3)
            def _():
                c_sib(k, 2).wait_recv()
                fin_s[k, 1] = (own_part(2) + sib[k, 2].astype(F32)).astype(BF16)
                c_fin(k, 1, 0).start()

            return carry

        lax.fori_loop(0, 4, step, 0)

    def rs_mid(k):
        for n in (0, 1):
            c_far(k, n).wait_recv()
            cut = pl.ds(64 * n, 64)
            fin_s[k, n, cut] = (fin_s[k, n, cut].astype(F32) + far_r[k, n].astype(F32)).astype(BF16)
            c_fin(k, n, n).start()

    def rs_finish(k):
        c_sib(k, 3).wait_recv()
        total = own_part(3) + sib[k, 3].astype(F32)
        for n in (0, 1):
            for h in (0, 1):
                c_fin(k, n, h).wait_recv()
        return total + fin_r[k, 0].astype(F32) + fin_r[k, 1].astype(F32)

    lax.fori_loop(1, 8, vec_wait, 0)

    def gathered(row):
        return jnp.concatenate([vall[i, row : row + 1, :] for i in range(8)], axis=1)

    swap_wait(x_src, x_own, 0)
    x32 = x_own[...].astype(F32)
    normed_all[rows(j * PIECE, PIECE), :] = (x32 * rms_scale(x32) * gathered(0)).astype(BF16)
    ag_start(normed_all, 0)
    w_forward(0)
    for load in loads[3:]:
        load.wait()
    w_start(1)
    w_start(2)
    swap_wait(cot_src, cot_own, 2)
    cot_all[rows(j * PIECE, PIECE), :] = cot_own[...]
    w_finish(0)

    def project(zz):
        cut = rows(zz * BLOCK, BLOCK)
        lin = nn(normed_all[cut, :], wqkv[...])
        cos = cos_ref[cut, :]
        sin = sin_ref[cut, :]
        bias = vall[pl.ds(j, 1)][0]
        q_lin = lin[:, :128] + bias[2:3, :]
        k_lin = lin[:, 128:256] + bias[3:4, :]
        v_lin = lin[:, 256:] + bias[4:5, :]
        q = (q_lin * cos + half_turn(q_lin) * sin).astype(BF16) * 0.125
        k32 = k_lin * cos + half_turn(k_lin) * sin
        k = k32.astype(BF16)
        v = v_lin.astype(BF16)
        for h in range(2):
            lanes = slice(64 * h, 64 * h + 64)
            q_h[h, cut, :] = q[:, lanes]
            k_h[h, cut, :] = k[:, lanes]
            v_h[h, cut, :] = v[:, lanes]
        k_t[:, cut] = k32.T.astype(BF16)
        v_t[:, cut] = v_lin.T.astype(BF16)

    ag_run(normed_all, 0, project)
    ag_start(cot_all, 1)

    def attend(i):
        width = (i + 1) * BLOCK
        cut = slice(i * BLOCK, (i + 1) * BLOCK)
        key_at = lax.broadcasted_iota(jnp.int32, (width, BLOCK), 0)
        query_at = lax.broadcasted_iota(jnp.int32, (width, BLOCK), 1) + i * BLOCK
        allowed = (key_at >= start_ref[0:1, cut]) & (key_at <= query_at)
        for h in range(2):
            scores = nt(k_h[h, :width, :], q_h[h, cut, :])
            scores = jnp.where(allowed, scores, NEG)
            weights = jnp.exp(scores - jnp.max(scores, axis=0, keepdims=True))
            inverse = 1.0 / jnp.sum(weights, axis=0, keepdims=True)
            probs = (weights * inverse).astype(BF16)
            p_t[h, i, :width, :] = probs
            mixed_t[64 * h : 64 * h + 64, cut] = nn(v_t[64 * h : 64 * h + 64, :width], probs)
        mixed[cut, :] = mixed_t[:, cut].T.astype(BF16)

    attend(0)
    attend(1)
    w_forward(1)
    w_forward(2)
    attend(2)
    ag_near(cot_all, 1)
    attend(3)
    ag_far(cot_all, 1)
    swap_wait(wo_in, wo, 1)

    rs_start(0, lambda zz: nn(mixed[rows(zz * BLOCK, BLOCK), :], wo[...]))
    w_finish(1)
    w_finish(2)
    for n in (2, 4, 6, 7):
        ag(cot_all, 1, n, True).wait_recv()
    rs_mid(0)

    def active_back(i, carry):
        cut = rows(i * BLOCK, BLOCK)
        g_act[cut, :] = nt(cot_all[cut, :], wdn[...])
        return carry

    lax.fori_loop(0, 4, active_back, 0)
    hidden[...] = x_own[...].astype(F32) + rs_finish(0)
    hid = hidden[...]
    mlp_all[rows(j * PIECE, PIECE), :] = (hid * rms_scale(hid) * gathered(1)).astype(BF16)
    ag_start(mlp_all, 2)

    unit = lax.broadcasted_iota(jnp.int32, (1, FB), 1)
    low_edge = 128 * (j // 7)
    high_edge = FB - 128 * ((j // 6) * (1 - j // 7))
    live = (unit >= low_edge) & (unit < high_edge)

    def feed(zz):
        cut = rows(zz * BLOCK, BLOCK)
        both = nn(mlp_all[cut, :], wgu[...])
        gate = both[:, :FB]
        up = both[:, FB:]
        sig = 1.0 / (1.0 + jnp.exp(-gate))
        silu = gate * sig
        back = jnp.where(live, g_act[cut, :], 0.0)
        active[cut, :] = jnp.where(live, silu * up, 0.0).astype(BF16)
        g_gu[cut, :FB] = (back * up * sig * (1.0 + gate * (1.0 - sig))).astype(BF16)
        g_gu[cut, FB:] = (back * silu).astype(BF16)

    ag_run(mlp_all, 2, feed)
    rs_start(1, lambda zz: nt(g_gu[rows(zz * BLOCK, BLOCK), :], wgu[...]))
    rs_mid(1)

    def plane_to(r):
        x_ = (x + r // 4) % 4
        y_ = (y + r % 4) % 4
        return x_ // 2, y_ * 2 + x_ % 2, dev(x_, y_, z, c)

    def p_gu(r):
        h_, f_, to = plane_to(r)
        return remote(dgu.at[rows(f_ * 128 + h_ * 64, 64)], rgu.at[r - 1], pl_s.at[0, r - 1], pl_r.at[0, r - 1], to)

    def p_dn(r):
        h_, f_, to = plane_to(r)
        return remote(ddn.at[rows(h_ * 192, 64 * 3), rows(f_ * 128, 128)], rdn.at[r - 1], pl_s.at[1, r - 1], pl_r.at[1, r - 1], to)

    def p_wo(r):
        h_, f_, to = plane_to(r)
        return remote(dwo.at[rows(h_ * 64, 64), rows(f_ * 128, 128)], rwo.at[r - 1], pl_s.at[2, r - 1], pl_r.at[2, r - 1], to)

    def p_qkv(r):
        h_, f_, to = plane_to(r)
        return remote(dqkv.at[rows(f_ * 128 + h_ * 64, 64)], rqkv.at[r - 1], pl_s.at[3, r - 1], pl_r.at[3, r - 1], to)

    def plane_start(copy):
        def go(r, carry):
            copy(r).start()
            return carry

        lax.fori_loop(1, 16, go, 0)

    def plane_wait(copy):
        def go(r, carry):
            copy(r).wait()
            return carry

        lax.fori_loop(1, 16, go, 0)

    def plane_sum(own, recv):
        return lax.fori_loop(0, 15, lambda r, total: total + recv[r].astype(F32), own.astype(F32))

    def grad_gu(i, carry):
        cut = rows(i * BLOCK, BLOCK)
        dgu[cut, :] = tn(mlp_all[:, cut], g_gu[...]).astype(BF16)
        return carry

    def grad_dn(i, carry):
        cut = rows(i * 128, 128)
        ddn[cut, :] = tn(active[:, cut], cot_all[...]).astype(BF16)
        return carry

    lax.fori_loop(0, 4, grad_gu, 0)
    plane_start(p_gu)

    grad = rs_finish(1)
    hid = hidden[...]
    scale = rms_scale(hid)
    scaled = grad * gathered(1)
    back = scale * scaled - hid * (scale * scale * scale) * jnp.mean(scaled * hid, axis=-1, keepdims=True)
    gain_two = jnp.sum(grad * hid * scale, axis=0, keepdims=True)
    g_hidden[...] = cot_own[...].astype(F32) + back
    branch_all[rows(j * PIECE, PIECE), :] = g_hidden[...].astype(BF16)
    ag_start(branch_all, 3)
    lax.fori_loop(0, 3, grad_dn, 0)
    plane_start(p_dn)

    def mixed_back(zz):
        cut = rows(zz * BLOCK, BLOCK)
        g_mixed[cut, :] = nt(branch_all[cut, :], wo[...])

    ag_run(branch_all, 3, mixed_back)
    rs_start(2, lambda zz: nn(active[rows(zz * BLOCK, BLOCK), :], wdn[...]))
    dwo[...] = tn(mixed[...], branch_all[...]).astype(BF16)
    plane_start(p_wo)

    gk_acc[...] = jnp.zeros_like(gk_acc)
    gv_acc[...] = jnp.zeros_like(gv_acc)

    def unturn(value, cut):
        value = value.astype(BF16).astype(F32)
        return (value * cos_ref[cut, :] - half_turn(value) * sin_ref[cut, :]).astype(BF16)

    def attend_back(i):
        width = (i + 1) * BLOCK
        cut = slice(i * BLOCK, (i + 1) * BLOCK)
        grad_t = g_mixed[cut, :].T
        grad_bf = g_mixed[cut, :].astype(BF16)
        products = grad_t * mixed_t[:, cut]
        queries_t = []
        for h in range(2):
            lanes = slice(64 * h, 64 * h + 64)
            grad_h = grad_bf[:, lanes]
            delta = jnp.sum(products[lanes, :], axis=0, keepdims=True)
            probs = p_t[h, i, :width, :]
            gv_acc[h, :width, :] += nn(probs, grad_h)
            g_probs = nt(v_h[h, :width, :], grad_h)
            g_scores = (probs.astype(F32) * (g_probs - delta)).astype(BF16)
            gk_acc[h, :width, :] += nn(g_scores, q_h[h, cut, :])
            queries_t.append(nn(k_t[lanes, :width], g_scores))
        g_query = (jnp.concatenate(queries_t, axis=0) * 0.125).T
        g_qkv[cut, :128] = unturn(g_query, cut)

    attend_back(0)
    attend_back(1)
    rs_mid(2)
    attend_back(2)
    attend_back(3)
    for i in range(4):
        cut = slice(i * BLOCK, (i + 1) * BLOCK)
        g_qkv[cut, 128:256] = unturn(jnp.concatenate([gk_acc[0, cut, :], gk_acc[1, cut, :]], axis=1), cut)
        g_qkv[cut, 256:] = jnp.concatenate([gv_acc[0, cut, :], gv_acc[1, cut, :]], axis=1).astype(BF16)

    lo_send[...] = (hidden[...] + rs_finish(2)).astype(BF16)
    swap_start(lo_send, lo_recv, 3)
    rs_start(3, lambda zz: nt(g_qkv[rows(zz * BLOCK, BLOCK), :], wqkv[...]))

    def grad_qkv(i, carry):
        cut = rows(i * BLOCK, BLOCK)
        dqkv[cut, :] = tn(normed_all[:, cut], g_qkv[...]).astype(BF16)
        return carry

    lax.fori_loop(0, 4, grad_qkv, 0)
    plane_start(p_qkv)
    rs_mid(3)

    mine = f * 128 + xh * 64
    plane_wait(p_wo)
    wo_send[...] = plane_sum(dwo[rows(xh * 64, 64), rows(f * 128, 128)], rwo).astype(BF16)
    swap_start(wo_send, wo_recv, 4)
    slot = j * 2 + xh
    plane_wait(p_gu)
    grads_a[pl.ds(slot, 1), :, 128:896] = plane_sum(dgu[rows(mine, 64), :], rgu).astype(BF16)[None]
    plane_wait(p_dn)
    total_dn = plane_sum(ddn[rows(xh * 192, 192), rows(f * 128, 128)], rdn).astype(BF16)
    for t in range(3):
        grads_a[pl.ds(slot, 1), :, 896 + 128 * t : 1024 + 128 * t] = total_dn[64 * t : 64 * t + 64][None]
    swap_wait(wo_send, wo_recv, 4)
    grads_a[pl.ds(slot, 1), :, :128] = wo_recv[...][None]

    def pair(buf, z_, c_):
        return buf.at[pl.ds((((z_ + 4) % 4) * 2 + c_) * 2, 2)]

    def single(buf, z_, c_, h):
        return buf.at[pl.ds((((z_ + 4) % 4) * 2 + c_) * 2 + h, 1)]

    def gg(buf, k, n, recv=False):
        if n == 0:
            ref = single(buf, z, c, (1 - xh) if recv else xh)
            to = dev(x + 2, y, z, c)
        elif n == 1:
            ref, to = pair(buf, z - 1 if recv else z, c), z_up
        elif n == 2:
            ref, to = pair(buf, z + 1 if recv else z, c), z_dn
        elif n == 3:
            ref, to = single(buf, z - 2 if recv else z - 1, c, 0), z_up
        elif n == 4:
            ref, to = single(buf, z + 2 if recv else z + 1, c, 1), z_dn
        else:
            ref, to = pair(buf, z + (n - 5), (1 - c) if recv else c), sibling
        return remote(ref, ref, ga_s.at[k, n], ga_r.at[k, n], to)

    def gg_one(buf, k):
        gg(buf, k, 0).start()

    def gg_two(buf, k):
        gg(buf, k, 0, True).wait_recv()
        gg(buf, k, 1).start()
        gg(buf, k, 2).start()
        gg(buf, k, 5).start()

    def gg_three(buf, k):
        gg(buf, k, 1, True).wait_recv()
        gg(buf, k, 3).start()
        gg(buf, k, 8).start()
        gg(buf, k, 2, True).wait_recv()
        gg(buf, k, 4).start()
        gg(buf, k, 6).start()

    def gg_four(buf, k):
        gg(buf, k, 3, True).wait_recv()
        gg(buf, k, 4, True).wait_recv()
        gg(buf, k, 7).start()

    def gg_five(buf, k):
        for n in (5, 6, 7, 8):
            gg(buf, k, n, True).wait_recv()

    gg_one(grads_a, 0)

    grad = rs_finish(3)
    gg_two(grads_a, 0)
    scale = rms_scale(x32)
    scaled = grad * gathered(0)
    back = scale * scaled - x32 * (scale * scale * scale) * jnp.mean(scaled * x32, axis=-1, keepdims=True)
    gain_one = jnp.sum(grad * x32 * scale, axis=0, keepdims=True)
    ig_send[...] = (g_hidden[...] + back).astype(BF16)
    swap_start(ig_send, ig_recv, 5)

    vs[...] = jnp.zeros_like(vs)
    for i in range(8):
        vs[i, 0:1, :] = gain_one[:, 128 * i : 128 * i + 128]
        vs[i, 1:2, :] = gain_two[:, 128 * i : 128 * i + 128]
    bias_sum = jnp.sum(g_qkv[...].astype(F32), axis=0, keepdims=True)
    for i in range(3):
        vs[pl.ds(j, 1), 2 + i : 3 + i, :] = bias_sum[:, 128 * i : 128 * i + 128][None]

    def v1_copy(r):
        return remote(vs.at[(f + r) % 8], vr.at[r - 1], v1_ss.at[r - 1], v1_rs.at[r - 1], (s, (f + r) % 8))

    def v1_start(r, carry):
        v1_copy(r).start()
        return carry

    def v1_wait(r, carry):
        v1_copy(r).wait()
        return carry

    lax.fori_loop(1, 8, v1_start, 0)

    plane_wait(p_qkv)
    grads_b[pl.ds(slot, 1)] = plane_sum(dqkv[rows(mine, 64), :], rqkv).astype(BF16)[None]
    gg_one(grads_b, 1)
    lax.fori_loop(1, 8, v1_wait, 0)
    v2s[...] = jnp.sum(vr[...], axis=0) + vs[pl.ds(f, 1)][0]

    def v2_copy(r):
        return remote(v2s, v2r.at[r - 1], v2_ss.at[r - 1], v2_rs.at[r - 1], ((s + r) % 16, f))

    def v2_start(r, carry):
        v2_copy(r).start()
        return carry

    def v2_wait(r, carry):
        v2_copy(r).wait()
        return carry

    lax.fori_loop(1, 16, v2_start, 0)
    gg_three(grads_a, 0)
    gg_two(grads_b, 1)
    gg_four(grads_a, 0)
    gg_three(grads_b, 1)
    lax.fori_loop(1, 16, v2_wait, 0)
    vec_out[...] = jnp.sum(v2r[...], axis=0) + v2s[...]
    gg_four(grads_b, 1)
    swap_wait(lo_send, lo_recv, 3)
    layer_out[...] = lo_recv[...]
    swap_wait(ig_send, ig_recv, 5)
    in_grad[...] = ig_recv[...]
    gg_five(grads_a, 0)
    gg_five(grads_b, 1)

    for n in range(3):
        for r in (1, 2, 3):
            w_y(n, r).wait_send()
        for r in range(4):
            w_x(n, r).wait_send()
    for k, buf in enumerate((normed_all, cot_all, mlp_all, branch_all)):
        for n in range(8):
            ag(buf, k, n).wait_send()
    for k in range(4):
        if k == 3:
            for i in range(4):
                c_sib(k, i).wait_send()
        for n in (0, 1):
            c_far(k, n).wait_send()
            for h in (0, 1):
                c_fin(k, n, h).wait_send()
    for k, buf in enumerate((grads_a, grads_b)):
        for n in range(9):
            gg(buf, k, n).wait_send()


def fused_layer(x, cot, wq, wk, wv, wo, wg, wu, wd, vec, cos, sin, start):
    def vmem(*shape, dtype=BF16):
        return pltpu.VMEM(shape, dtype)

    def dma(*shape):
        return pltpu.SemaphoreType.DMA(shape)

    full = vmem(D, D)
    scratch = [
        vmem(PIECE, D), vmem(PIECE, D), vmem(PIECE, D, dtype=F32), vmem(PIECE, D, dtype=F32),
        vmem(PIECE, D), vmem(D, FB), vmem(D, 2 * FB), vmem(FB, D), vmem(8, 8, 128, dtype=F32),
        full, full, full, full,
        vmem(2, D, 64), vmem(2, D, 64), vmem(2, D, 64), vmem(128, D), vmem(128, D),
        vmem(2, 4, D, BLOCK), vmem(128, D, dtype=F32), vmem(D, 128),
        vmem(D, FB, dtype=F32), vmem(D, FB), vmem(D, 2 * FB), vmem(D, 128, dtype=F32),
        vmem(2, D, 64, dtype=F32), vmem(2, D, 64, dtype=F32), vmem(D, FB),
        vmem(4, BLOCK, D), vmem(4, 4, PIECE, D), vmem(4, PIECE, D), vmem(4, 2, 64, D), vmem(4, 2, PIECE, D), vmem(4, 2, PIECE, D),
        vmem(D, 2 * FB), vmem(FB, D), vmem(128, D), vmem(D, FB),
        vmem(15, 64, 2 * FB), vmem(15, 192, 128), vmem(15, 64, 128), vmem(15, 64, FB), vmem(64, 128), vmem(64, 128),
        vmem(PIECE, D), vmem(PIECE, D), vmem(PIECE, D), vmem(PIECE, D),
        vmem(8, 8, 128, dtype=F32), vmem(7, 8, 128, dtype=F32), vmem(8, 128, dtype=F32), vmem(15, 8, 128, dtype=F32),
        dma(6), dma(6), dma(6), dma(8), dma(8), dma(3, 8), dma(3, 8), dma(4, 8), dma(4, 8),
        dma(4, 4), dma(4, 4), dma(4, 2), dma(4, 2), dma(4, 2, 2), dma(4, 2, 2),
        dma(4, 15), dma(4, 15), dma(2, 9), dma(2, 9), dma(7), dma(7), dma(15), dma(15),
    ]
    anywhere = pl.BlockSpec(memory_space=pl.ANY)
    inside = pl.BlockSpec(memory_space=pltpu.VMEM)
    return pl.pallas_call(
        layer_kernel,
        out_shape=(
            jax.ShapeDtypeStruct((PIECE, D), BF16),
            jax.ShapeDtypeStruct((PIECE, D), BF16),
            jax.ShapeDtypeStruct((16, 64, 1280), BF16),
            jax.ShapeDtypeStruct((16, 64, FB), BF16),
            jax.ShapeDtypeStruct((8, 128), F32),
        ),
        in_specs=[anywhere] * 9 + [inside] * 4,
        out_specs=[inside] * 5,
        scratch_shapes=scratch,
        compiler_params=pltpu.CompilerParams(
            collective_id=0, has_side_effects=True, vmem_limit_bytes=63 * 1024 * 1024
        ),
        name="layer",
    )(x, cot, wq, wk, wv, wo, wg, wu, wd, vec, cos, sin, start)


def per_device(
    inputs, doc_ids, positions, attn_gain, query_weight, key_weight, value_weight,
    query_bias, key_bias, value_bias, out_weight, mlp_gain, gate_weight, up_weight,
    down_weight, cotangent,
):
    del positions
    exponent = jnp.arange(HEAD_DIM // 2, dtype=F32) * (2.0 / HEAD_DIM)
    inverse = jnp.exp(-math.log(THETA) * exponent)
    angles = jnp.arange(D, dtype=F32)[:, None] * inverse
    cos_half, sin_half = jnp.cos(angles), jnp.sin(angles)
    cos = jnp.concatenate([cos_half] * 4, axis=1)
    sin = jnp.concatenate([-sin_half, sin_half] * 2, axis=1)
    seq_here = (lax.axis_index("seq") // 8) * 8 + lax.axis_index("fsdp")
    docs = lax.dynamic_slice_in_dim(doc_ids, seq_here, 1, 0)
    start = jnp.where(docs == 1, jnp.sum(1 - docs, axis=1, keepdims=True), 0)
    zero = jnp.zeros((128,), F32)
    vec = jnp.stack(
        [v.astype(F32) for v in (attn_gain, mlp_gain, query_bias, key_bias, value_bias)] + [zero] * 3
    )
    layer_out, in_grad, grads_a, grads_b, vec_out = fused_layer(
        inputs.reshape(PIECE, D), cotangent.reshape(PIECE, D),
        query_weight, key_weight, value_weight, out_weight, gate_weight, up_weight, down_weight,
        vec, cos, sin, start,
    )
    def rowwise(block):
        return block.reshape(8, 2, 64, -1).transpose(1, 2, 0, 3).reshape(128, -1).astype(F32)

    def cut_windows(block):
        return jnp.concatenate([block[:, : 6 * FB], block[:, 6 * FB : 6 * FB + 256], block[:, 7 * FB + 128 :]], axis=1)

    down = grads_a[:, :, 896:].reshape(8, 2, 64, 3, 128).transpose(0, 1, 3, 2, 4).reshape(8 * FB, 128).astype(F32)
    down = jnp.concatenate([down[: 6 * FB], down[6 * FB : 6 * FB + 256], down[7 * FB + 128 :]], axis=0)
    return (
        layer_out.reshape(inputs.shape),
        in_grad.astype(F32).reshape(inputs.shape),
        vec_out[0],
        rowwise(grads_b[:, :, :128]),
        rowwise(grads_b[:, :, 128:256]),
        rowwise(grads_b[:, :, 256:]),
        vec_out[2],
        vec_out[3],
        vec_out[4],
        rowwise(grads_a[:, :, :128]),
        vec_out[1],
        cut_windows(rowwise(grads_a[:, :, 128:512])),
        cut_windows(rowwise(grads_a[:, :, 512:896])),
        down,
    )


def solution(mesh):
    rows_spec = P("fsdp", None)
    act = P("seq", "fsdp", None)
    vec = P("fsdp")
    return jax.shard_map(
        per_device,
        mesh=mesh,
        in_specs=(
            act, P(), P("seq", "fsdp"), vec, rows_spec, rows_spec, rows_spec, vec, vec, vec,
            rows_spec, vec, rows_spec, rows_spec, P(None, "fsdp"), act,
        ),
        out_specs=(
            act, act, vec, rows_spec, rows_spec, rows_spec, vec, vec, vec, rows_spec, vec,
            rows_spec, rows_spec, P(None, "fsdp"),
        ),
        check_vma=False,
    )
```

```python
import math

import jax
import jax.numpy as jnp
import numpy as np
from jax import lax
from jax.experimental import pallas as pl
from jax.experimental.pallas import tpu as pltpu
from jax.sharding import PartitionSpec as P

MESH = pl.DeviceIdType.MESH
HEAD_DIM = 64
EPS = 1e-06
THETA = 1000000.0
NEG = -1000000000.0
D = 1024
PIECE = 128
BLOCK = 256
FB = 384
F32 = jnp.float32
BF16 = jnp.bfloat16


def nn(a, b):
    return lax.dot_general(a, b, (((1,), (0,)), ((), ())), preferred_element_type=F32)


def nt(a, b):
    return lax.dot_general(a, b, (((1,), (1,)), ((), ())), preferred_element_type=F32)


def tn(a, b):
    return lax.dot_general(a, b, (((0,), (0,)), ((), ())), preferred_element_type=F32)


def rms_scale(value):
    return lax.rsqrt(jnp.mean(value * value, axis=-1, keepdims=True) + EPS)


def rows(start, size):
    return pl.ds(pl.multiple_of(start, size), size)


def half_turn(value):
    lane = lax.broadcasted_iota(jnp.int32, value.shape, 1)
    ahead = pltpu.roll(value, 96, 1)
    behind = pltpu.roll(value, 32, 1)
    return jnp.where(lane % 64 < 32, ahead, behind)


def layer_kernel(
    x_in, cot_in, wq_in, wk_in, wv_in, wo_in, wg_in, wu_in, wd_in, cos_in, sin_in,
    gain_a, gain_m, bias_q, bias_k, bias_v, docs,
    layer_out, in_grad, all_gu, all_dn, all_wo, all_qkv, vec_out,
    cos_ref, sin_ref, start_ref, vec_in,
    x_own, cot_own, hidden, g_hidden, wo_all, wqkv, wgu, wdn, vall,
    normed_all, cot_all, mlp_all, branch_all,
    q_h, k_h, v_h, k_t, v_t, p_t, mixed_t, mixed, mixed_own,
    g_act, active, active_t, g_gu, g_mixed, gk_acc, gv_acc, g_qkv,
    part, sib, far_s, far_r, fin_s, fin_r,
    dga, dgb, ddn, dwo, dqkv, ra, rb, rd, ha, hb, hd, sa, sb, sd, rwo, rqkv, wo_send, sum_gu, sum_dn, sum_qkv,
    lo_send, ig_send,
    vs, vr, v2s, v2r, v3s, v3r,
    sem_load, swap_s, swap_r, vec_s, vec_r, wy_s, wy_r, wz_s, wz_r, wx_s, wx_r, wp_s, wp_r, mx_s, mx_r, ag_s, ag_r,
    sib_ss, sib_rs, far_ss, far_rs, fin_ss, fin_rs,
    pl_s, pl_r, f1_s, f1_r, f2_s, f2_r, ya_s, ya_r, rg_s, rg_r, gd_s, gd_r, gp_s, gp_r, v1_ss, v1_rs, v2_ss, v2_rs, v3_ss, v3_rs,
):
    s = lax.axis_index("seq")
    f = lax.axis_index("fsdp")
    xh = s // 8
    z = (s % 8) // 2
    c = s % 2
    y = f // 2
    xl = f % 2
    x = xh * 2 + xl
    j = y * 2 + c
    place = z * 2 + xh

    def dev(x_, y_, z_, c_):
        x_, y_, z_ = (x_ + 4) % 4, (y_ + 4) % 4, (z_ + 4) % 4
        return ((x_ // 2) * 8 + z_ * 2 + c_, y_ * 2 + x_ % 2)

    sibling = dev(x, y, z, 1 - c)
    y_up = dev(x, y + 1, z, c)
    y_dn = dev(x, y + 3, z, c)
    moves = (c + xl) % 2
    partner = dev(xh * 2 + 1 - xl, y, z, 1 - c)
    x_to = dev(x + 1 + 2 * c, y, z, c)

    def window(m):
        return (3 * m - 2 * (m // 7)) * 128

    def remote(src, dst, ss, rs, to):
        return pltpu.make_async_remote_copy(
            src_ref=src, dst_ref=dst, send_sem=ss, recv_sem=rs, device_id=to, device_id_type=MESH
        )

    def at(start, size, unit):
        return pl.ds(pl.multiple_of(start, unit), size)

    own_rows = rows(f * 128, 128)
    own_win = at(window(j), FB, 128)
    loads = [
        pltpu.make_async_copy(wq_in.at[:, rows(j * 128, 128)], wqkv.at[own_rows, pl.ds(0, 128)], sem_load.at[0]),
        pltpu.make_async_copy(wk_in.at[:, rows(j * 128, 128)], wqkv.at[own_rows, pl.ds(128, 128)], sem_load.at[1]),
        pltpu.make_async_copy(wv_in.at[:, rows(j * 128, 128)], wqkv.at[own_rows, pl.ds(256, 128)], sem_load.at[2]),
        pltpu.make_async_copy(wo_in, wo_all.at[own_rows], sem_load.at[3]),
        pltpu.make_async_copy(wg_in.at[:, own_win], wgu.at[own_rows, pl.ds(0, FB)], sem_load.at[4]),
        pltpu.make_async_copy(wu_in.at[:, own_win], wgu.at[own_rows, pl.ds(FB, FB)], sem_load.at[5]),
        pltpu.make_async_copy(wd_in.at[own_win, :], wdn.at[:, own_rows], sem_load.at[6]),
        pltpu.make_async_copy(cos_in, cos_ref, sem_load.at[7]),
        pltpu.make_async_copy(sin_in, sin_ref, sem_load.at[8]),
    ]
    for load in loads:
        load.start()

    barrier = pltpu.get_barrier_semaphore()

    def greet(to):
        pl.semaphore_signal(barrier, inc=1, device_id=to, device_id_type=MESH)

    def greet_plane(r, carry):
        greet(dev(x + r // 4, y, z + r % 4, c))
        return carry

    def greet_fsdp(r, carry):
        greet((s, (f + r) % 8))
        return carry

    def greet_cross(r, carry):
        greet(dev(x, y + r, z, 1 - c))
        return carry

    lax.fori_loop(1, 16, greet_plane, 0)
    lax.fori_loop(1, 8, greet_fsdp, 0)
    lax.fori_loop(0, 4, greet_cross, 0)

    @pl.when(moves == 1)
    def _():
        greet(partner)
        pl.semaphore_wait(barrier, 27)

    @pl.when(moves == 0)
    def _():
        pl.semaphore_wait(barrier, 26)

    def swap_start(src, dst, n):
        @pl.when(moves == 1)
        def _():
            remote(src, dst, swap_s.at[n], swap_r.at[n], partner).start()

        @pl.when(moves == 0)
        def _():
            pltpu.make_async_copy(src, dst, swap_r.at[n]).start()

    def swap_wait(src, dst, n):
        @pl.when(moves == 1)
        def _():
            remote(src, dst, swap_s.at[n], swap_r.at[n], partner).wait()

        @pl.when(moves == 0)
        def _():
            pltpu.make_async_copy(src, dst, swap_r.at[n]).wait()

    def vec_copy(r):
        return remote(vec_in, vall.at[f], vec_s.at[r], vec_r.at[r], (s, (f + r) % 8))

    def vec_start(r, carry):
        vec_copy(r).start()
        return carry

    def vec_wait(r, carry):
        vec_copy(r).wait()
        return carry

    vec_in[...] = jnp.zeros_like(vec_in)
    for i, ref in enumerate((gain_a, gain_m, bias_q, bias_k, bias_v)):
        vec_in[i : i + 1, :] = ref[...].astype(F32)
    lax.fori_loop(1, 8, vec_start, 0)
    swap_start(x_in, x_own, 0)
    vall[pl.ds(f, 1)] = vec_in[...][None]
    doc_row = docs[pl.ds(xh * 8 + z * 2 + xl, 1), :]
    start_ref[...] = jnp.where(doc_row == 1, jnp.sum(1 - doc_row, axis=1, keepdims=True), 0)

    PARTS = (3, 2, 1, 1)

    def shard(r):
        return ((y + 4 - r) % 4) * 2 + xl

    def w_quarter(n, f_, q, p=None):
        if n == 0:
            return wqkv.at[at(f_ * 128 + q * 32, 32, 32), slice(None) if p is None else pl.ds(p * 128, 128)]
        if n == 1:
            return wgu.at[at(f_ * 128 + q * 32, 32, 32), slice(None) if p is None else pl.ds(p * FB, FB)]
        if n == 2:
            return wdn.at[at(q * 96, 96, 32), rows(f_ * 128, 128)]
        return wo_all.at[at(f_ * 128 + c * 64 + q * 16, 16, 16)]

    def w_rows(n, f_):
        if n == 0:
            return wqkv.at[rows(f_ * 128, 128)]
        if n == 1:
            return wgu.at[rows(f_ * 128, 128)]
        if n == 2:
            return wdn.at[:, rows(f_ * 128, 128)]
        return wo_all.at[rows(f_ * 128 + c * 64, 64)]

    def w_y(n, p, r, recv=False):
        m = ((y + r) % 4) * 2 + c
        if n == 0:
            src = (wq_in, wk_in, wv_in)[p].at[at(z * 32, 32, 32), rows(m * 128, 128)]
        elif n == 1:
            src = (wg_in, wu_in)[p].at[at(z * 32, 32, 32), at(window(m), FB, 128)]
        elif n == 2:
            src = wd_in.at[at(window(m) + z * 96, 96, 32), :]
        else:
            src = wo_in.at[at(c * 64 + z * 16, 16, 16)]
        dst = w_quarter(n, shard(r) if recv else f, z, p)
        return remote(src, dst, wy_s.at[n, p, r], wy_r.at[n, p, r], dev(x, y + r, z, c))

    def w_z(n, r, dz, recv=False):
        src = w_quarter(n, shard(r), z)
        dst = w_quarter(n, shard(r), (z + 4 - dz) % 4) if recv else src
        return remote(src, dst, wz_s.at[n, r, dz], wz_r.at[n, r, dz], dev(x, y, z + dz, c))

    def w_x(n, r, recv=False):
        src = w_rows(n, shard(r))
        dst = w_rows(n, ((y + 4 - r) % 4) * 2 + 1 - xl) if recv else src
        return remote(src, dst, wx_s.at[n, r], wx_r.at[n, r], x_to)

    def w_ystart(n):
        for r in (1, 3, 2):
            for p in range(PARTS[n]):
                w_y(n, p, r).start()

    def w_own(n):
        for load in (loads[:3], loads[4:6], loads[6:7], loads[3:4])[n]:
            load.wait()
        w_x(n, 0).start()

    def w_zstart(n):
        for r in (1, 3, 2):
            for p in range(PARTS[n]):
                w_y(n, p, r, True).wait_recv()
            for dz in (1, 3, 2):
                w_z(n, r, dz).start()

    def w_xstart(n):
        for r in (1, 3, 2):
            for dz in (1, 3, 2):
                w_z(n, r, dz, True).wait_recv()
            w_x(n, r).start()
            if n == 3:
                wo_pass(2 * ((4 - r) % 4)).start()

    def w_finish(n):
        for r in range(4):
            w_x(n, r, True).wait_recv()

    def wo_pass(n, recv=False):
        f_ = ((y + n // 2) % 4) * 2 + (xl + n % 2) % 2
        ref = wo_all.at[rows(f_ * 128 + ((1 - c) if recv else c) * 64, 64)]
        return remote(ref, ref, wp_s.at[n], wp_r.at[n], sibling)

    def wo_pass_x():
        for r in range(4):
            w_x(3, r, True).wait_recv()
            wo_pass(2 * ((4 - r) % 4) + 1).start()

    def wo_pass_finish():
        for n in range(1, 8):
            wo_pass(n, True).wait_recv()

    for n in (0, 3, 1, 2):
        w_ystart(n)
    w_own(0)

    def piece(buf, y_, c_):
        return buf.at[rows((((y_ + 4) % 4) * 2 + c_) * PIECE, PIECE)]

    def half(buf, y_, c_, h):
        return buf.at[rows((((y_ + 4) % 4) * 2 + c_) * PIECE + h * 64, 64)]

    def ag(buf, k, n, recv=False):
        if n == 0:
            ref, to = (piece(buf, y - 1, c) if recv else piece(buf, y, c)), y_up
        elif n == 1:
            ref, to = (piece(buf, y + 1, c) if recv else piece(buf, y, c)), y_dn
        elif n == 2:
            ref, to = (piece(buf, y, 1 - c) if recv else piece(buf, y, c)), sibling
        elif n == 3:
            ref, to = (half(buf, y - 2, c, 0) if recv else half(buf, y - 1, c, 0)), y_up
        elif n == 4:
            ref, to = (piece(buf, y - 1, 1 - c) if recv else piece(buf, y - 1, c)), sibling
        elif n == 5:
            ref, to = (half(buf, y + 2, c, 1) if recv else half(buf, y + 1, c, 1)), y_dn
        elif n == 6:
            ref, to = (piece(buf, y + 1, 1 - c) if recv else piece(buf, y + 1, c)), sibling
        else:
            ref, to = (piece(buf, y + 2, 1 - c) if recv else piece(buf, y + 2, c)), sibling
        return remote(ref, ref, ag_s.at[k, n], ag_r.at[k, n], to)

    def ag_start(buf, k):
        for n in range(3):
            ag(buf, k, n).start()

    def ag_near(buf, k):
        ag(buf, k, 0, True).wait_recv()
        ag(buf, k, 3).start()
        ag(buf, k, 4).start()
        ag(buf, k, 1, True).wait_recv()
        ag(buf, k, 5).start()
        ag(buf, k, 6).start()

    def ag_far(buf, k):
        ag(buf, k, 3, True).wait_recv()
        ag(buf, k, 5, True).wait_recv()
        ag(buf, k, 7).start()

    def ag_run(buf, k, consume, after_far=None):
        def step(i, carry):
            @pl.when(i == 0)
            def _():
                ag(buf, k, 2, True).wait_recv()

            @pl.when(i == 1)
            def _():
                ag_near(buf, k)
                ag(buf, k, 4, True).wait_recv()

            @pl.when(i == 2)
            def _():
                ag(buf, k, 6, True).wait_recv()

            @pl.when(i == 3)
            def _():
                ag_far(buf, k)
                if after_far is not None:
                    after_far()
                ag(buf, k, 7, True).wait_recv()

            consume((y + (3 * ((i * (i + 1)) // 2)) % 4) % 4)
            return carry

        lax.fori_loop(0, 4, step, 0)

    def other(i):
        return part.at[i, rows((1 - c) * PIECE, PIECE)]

    def own_part(i):
        return part[i, rows(c * PIECE, PIECE), :].astype(F32)

    def c_sib(k, i):
        return remote(other(i), sib.at[k, i], sib_ss.at[k, i], sib_rs.at[k, i], sibling)

    def c_far(k, n):
        return remote(far_s.at[k, pl.ds(64 * n, 64)], far_r.at[k, n], far_ss.at[k, n], far_rs.at[k, n], y_up if n == 0 else y_dn)

    def c_fin(k, n, h):
        cut = pl.ds(64 * h, 64)
        return remote(fin_s.at[k, n, cut], fin_r.at[k, n, cut], fin_ss.at[k, n, h], fin_rs.at[k, n, h], y_up if n == 0 else y_dn)

    def rs_far(k):
        c_sib(k, 0).wait_recv()
        far_s[k] = (own_part(0) + sib[k, 0].astype(F32)).astype(BF16)
        c_far(k, 0).start()
        c_far(k, 1).start()

    def rs_near(k, n):
        c_sib(k, 1 + n).wait_recv()
        fin_s[k, n] = (own_part(1 + n) + sib[k, 1 + n].astype(F32)).astype(BF16)
        c_fin(k, n, 1 - n).start()

    def rs_start(k, produce, eager=True):
        def step(i, carry):
            if k > 1:
                c_sib(k - 1, i).wait_send()
            part[i] = produce((y + (2 - (i * (i + 1)) // 2 + 8) % 4) % 4).astype(BF16)
            c_sib(k, i).start()
            if eager:
                @pl.when(i == 1)
                def _():
                    rs_far(k)

                @pl.when(i == 2)
                def _():
                    rs_near(k, 0)

                @pl.when(i == 3)
                def _():
                    rs_near(k, 1)

            return carry

        lax.fori_loop(0, 4, step, 0)

    def rs_mid(k):
        for n in (0, 1):
            c_far(k, n).wait_recv()
            cut = pl.ds(64 * n, 64)
            fin_s[k, n, cut] = (fin_s[k, n, cut].astype(F32) + far_r[k, n].astype(F32)).astype(BF16)
            c_fin(k, n, n).start()

    def rs_finish(k):
        c_sib(k, 3).wait_recv()
        total = own_part(3) + sib[k, 3].astype(F32)
        for n in (0, 1):
            for h in (0, 1):
                c_fin(k, n, h).wait_recv()
        return total + fin_r[k, 0].astype(F32) + fin_r[k, 1].astype(F32)

    w_zstart(0)
    lax.fori_loop(1, 8, vec_wait, 0)

    def gathered(row):
        return jnp.concatenate([vall[i, row : row + 1, :] for i in range(8)], axis=1)

    swap_wait(x_in, x_own, 0)
    x32 = x_own[...].astype(F32)
    normed_all[rows(j * PIECE, PIECE), :] = (x32 * rms_scale(x32) * gathered(0)).astype(BF16)
    ag_start(normed_all, 0)
    w_xstart(0)
    swap_start(cot_in, cot_own, 1)
    w_zstart(3)
    w_own(3)
    w_zstart(1)
    w_own(1)
    w_zstart(2)
    w_own(2)
    for load in loads[7:]:
        load.wait()
    w_finish(0)

    def project(yy):
        cut = rows(yy * BLOCK, BLOCK)
        lin = nn(normed_all[cut, :], wqkv[...])
        cos = cos_ref[cut, :]
        sin = sin_ref[cut, :]
        bias = vall[pl.ds(j, 1)][0]
        q_lin = lin[:, :128] + bias[2:3, :]
        k_lin = lin[:, 128:256] + bias[3:4, :]
        v_lin = lin[:, 256:] + bias[4:5, :]
        q = (q_lin * cos + half_turn(q_lin) * sin).astype(BF16) * 0.125
        k32 = k_lin * cos + half_turn(k_lin) * sin
        k = k32.astype(BF16)
        v = v_lin.astype(BF16)
        for h in range(2):
            lanes = slice(64 * h, 64 * h + 64)
            q_h[h, cut, :] = q[:, lanes]
            k_h[h, cut, :] = k[:, lanes]
            v_h[h, cut, :] = v[:, lanes]
        k_t[:, cut] = k32.T.astype(BF16)
        v_t[:, cut] = v_lin.T.astype(BF16)

    def cot_start():
        swap_wait(cot_in, cot_own, 1)
        cot_all[rows(j * PIECE, PIECE), :] = cot_own[...]
        ag_start(cot_all, 1)

    ag_run(normed_all, 0, project, cot_start)

    def attend(i):
        width = (i + 1) * BLOCK
        cut = slice(i * BLOCK, (i + 1) * BLOCK)
        key_at = lax.broadcasted_iota(jnp.int32, (width, BLOCK), 0)
        query_at = lax.broadcasted_iota(jnp.int32, (width, BLOCK), 1) + i * BLOCK
        allowed = (key_at >= start_ref[0:1, cut]) & (key_at <= query_at)
        for h in range(2):
            scores = nt(k_h[h, :width, :], q_h[h, cut, :])
            scores = jnp.where(allowed, scores, NEG)
            weights = jnp.exp(scores - jnp.max(scores, axis=0, keepdims=True))
            inverse = 1.0 / jnp.sum(weights, axis=0, keepdims=True)
            probs = (weights * inverse).astype(BF16)
            p_t[h, i, :width, :] = probs
            mixed_t[64 * h : 64 * h + 64, cut] = nn(v_t[64 * h : 64 * h + 64, :width], probs)
        mixed[cut, :] = mixed_t[:, cut].T.astype(BF16)
        for m in (2 * i, 2 * i + 1):
            mix_start(m)

    def mix(m, sender):
        return remote(
            mixed.at[rows(m * PIECE, PIECE), :], mixed_own.at[:, rows(sender * 128, 128)],
            mx_s.at[m], mx_r.at[sender], dev(x, m // 2, z, m % 2),
        )

    def mix_start(m):
        @pl.when(j != m)
        def _():
            mix(m, j).start()

        @pl.when(j == m)
        def _():
            mixed_own[:, rows(j * 128, 128)] = mixed[m * PIECE : (m + 1) * PIECE, :]

    def mix_wait(r, carry):
        m = (j + r) % 8
        mix(m, m).wait_recv()
        mix(m, j).wait_send()
        return carry

    w_xstart(3)
    attend(0)
    w_xstart(2)
    attend(1)
    w_xstart(1)
    attend(2)
    wo_pass_x()
    attend(3)
    ag_near(cot_all, 1)
    wo_pass_finish()
    lax.fori_loop(1, 8, mix_wait, 0)

    hidden[...] = x_own[...].astype(F32) + nn(mixed_own[...], wo_all[...])
    hid = hidden[...]
    mlp_all[rows(j * PIECE, PIECE), :] = (hid * rms_scale(hid) * gathered(1)).astype(BF16)
    ag_start(mlp_all, 2)
    ag_far(cot_all, 1)
    w_finish(2)
    for n in (2, 4, 6, 7):
        ag(cot_all, 1, n, True).wait_recv()

    def active_back(i, carry):
        cut = rows(i * BLOCK, BLOCK)
        g_act[cut, :] = nt(cot_all[cut, :], wdn[...])
        return carry

    lax.fori_loop(0, 4, active_back, 0)
    w_finish(1)

    unit = lax.broadcasted_iota(jnp.int32, (1, FB), 1)
    low_edge = 128 * (j // 7)
    high_edge = FB - 128 * ((j // 6) * (1 - j // 7))
    live = (unit >= low_edge) & (unit < high_edge)

    def feed(yy):
        cut = rows(yy * BLOCK, BLOCK)
        both = nn(mlp_all[cut, :], wgu[...])
        gate = both[:, :FB]
        up = both[:, FB:]
        sig = 1.0 / (1.0 + jnp.exp(-gate))
        silu = gate * sig
        back = jnp.where(live, g_act[cut, :], 0.0)
        act = jnp.where(live, silu * up, 0.0)
        active[cut, :] = act.astype(BF16)
        active_t[:, cut] = act.T.astype(BF16)
        g_gu[cut, :FB] = (back * up * sig * (1.0 + gate * (1.0 - sig))).astype(BF16)
        g_gu[cut, FB:] = (back * silu).astype(BF16)

    ag_run(mlp_all, 2, feed)
    rs_start(1, lambda yy: nt(g_gu[rows(yy * BLOCK, BLOCK), :], wgu[...]))

    def plane(n, r):
        x_, z_ = (x + r // 4) % 4, (z + r % 4) % 4
        src = (dwo, dqkv)[n].at[x_ * 4 + z_]
        dst = (rwo, rqkv)[n].at[r - 1]
        return remote(src, dst, pl_s.at[n, r - 1], pl_r.at[n, r - 1], dev(x_, y, z_, c))

    def plane_start(n):
        def go(r, carry):
            plane(n, r).start()
            return carry

        lax.fori_loop(1, 16, go, 0)

    def plane_sum(n):
        own, recv = ((dwo, rwo), (dqkv, rqkv))[n]

        def go(r, total):
            plane(n, r).wait()
            return total + recv[r - 1].astype(F32)

        return lax.fori_loop(1, 16, go, own[x * 4 + z].astype(F32))

    def first(n, r):
        if n == 0:
            src, to = dga.at[(x + r) % 4], dev(x + r, y, z, c)
        else:
            src, to = (dgb, ddn)[n - 1].at[:, (z + r) % 4], dev(x, y, z + r, c)
        return remote(src, (ra, rb, rd)[n].at[r - 1], f1_s.at[n, r], f1_r.at[n, r], to)

    def second(n, r):
        src = (ha, hb, hd)[n].at[((z if n == 0 else x) + r) % 4]
        to = dev(x, y, z + r, c) if n == 0 else dev(x + r, y, z, c)
        return remote(src, (sa, sb, sd)[n].at[r - 1], f2_s.at[n, r], f2_r.at[n, r], to)

    def first_start(n):
        for r in (1, 3, 2):
            first(n, r).start()

    def first_sum(n):
        total = (dga[x] if n == 0 else (dgb, ddn)[n - 1][:, z]).astype(F32)
        for r in (1, 3, 2):
            first(n, r).wait()
            total = total + (ra, rb, rd)[n][r - 1].astype(F32)
        (ha, hb, hd)[n][...] = total.astype(BF16)
        for r in (1, 3, 2):
            second(n, r).start()

    def second_sum(n):
        total = (ha, hb, hd)[n][z if n == 0 else x].astype(F32)
        for r in (1, 3, 2):
            second(n, r).wait()
            total = total + (sa, sb, sd)[n][r - 1].astype(F32)
        return total.astype(BF16)

    def chunk(t, xl_):
        return (t % 2) * 2 + xl_, t // 2

    def grad_gu(i, carry):
        got = tn(mlp_all[:, rows(i * BLOCK, BLOCK)], g_gu[...]).astype(BF16)
        for xl_ in range(2):
            for t in range(8):
                x_, z_ = chunk(t, xl_)
                share = got[xl_ * 128 + t * 16 : xl_ * 128 + t * 16 + 16]
                dga[x_, z_, i] = share[:, :512]
                dgb[x_, z_, i] = share[:, 512:]
        return carry

    def grad_dn(i, carry):
        got = nn(active_t[...], cot_all[:, rows(i * BLOCK, BLOCK)]).astype(BF16)
        for xl_ in range(2):
            for t in range(8):
                x_, z_ = chunk(t, xl_)
                ddn[x_, z_, i] = got[t * 48 : t * 48 + 48, xl_ * 128 : xl_ * 128 + 128]
        return carry

    def grad_qkv(i, carry):
        got = tn(normed_all[:, rows(i * BLOCK, BLOCK)], g_qkv[...]).astype(BF16)
        for xl_ in range(2):
            for t in range(8):
                x_, z_ = chunk(t, xl_)
                dqkv[x_ * 4 + z_, i] = got[xl_ * 128 + t * 16 : xl_ * 128 + t * 16 + 16]
        return carry

    def grad_wo():
        got = tn(mixed[...], branch_all[...]).astype(BF16)
        for h in range(2):
            for t in range(8):
                to = ((t % 2) * 2 + (h + c) % 2) * 4 + t // 2
                dwo[pl.ds(to, 1)] = got[h * 64 : h * 64 + 64, t * 128 : t * 128 + 128][None]

    lax.fori_loop(0, 2, grad_gu, 0)
    rs_mid(1)
    lax.fori_loop(2, 4, grad_gu, 0)
    first_start(1)
    first_start(0)
    lax.fori_loop(0, 4, grad_dn, 0)
    first_start(2)

    grad = rs_finish(1)
    hid = hidden[...]
    scale = rms_scale(hid)
    scaled = grad * gathered(1)
    back = scale * scaled - hid * (scale * scale * scale) * jnp.mean(scaled * hid, axis=-1, keepdims=True)
    gain_two = jnp.sum(grad * hid * scale, axis=0, keepdims=True)
    g_hidden[...] = cot_own[...].astype(F32) + back
    branch_all[rows(j * PIECE, PIECE), :] = g_hidden[...].astype(BF16)
    ag_start(branch_all, 3)

    def mixed_back(yy):
        cut = rows(yy * BLOCK, BLOCK)
        g_mixed[cut, :] = nt(branch_all[cut, :], wo_all[rows(j * 128, 128), :])

    gk_acc[...] = jnp.zeros_like(gk_acc)
    gv_acc[...] = jnp.zeros_like(gv_acc)
    ag_run(branch_all, 3, mixed_back)
    for n in (1, 0, 2):
        first_sum(n)
    rs_start(2, lambda yy: nn(active[rows(yy * BLOCK, BLOCK), :], wdn[...]), eager=False)

    def along_y(n, r, recv=False):
        src = (sum_gu, sum_dn, sum_qkv)[n].at[(y + r) % 4]
        dst = (all_gu, all_dn, all_qkv)[n].at[place, c, (y + 4 - r) % 4 if recv else y]
        return remote(src, dst, ya_s.at[n, r], ya_r.at[n, r], dev(x, y + r, z, c))

    def share(n):
        total, every = ((sum_gu, all_gu), (sum_dn, all_dn), (sum_qkv, all_qkv))[n]
        if n == 0:
            total[:, :, :512] = second_sum(0)
            total[:, :, 512:] = second_sum(1)
        elif n == 1:
            total[...] = second_sum(2)
        else:
            total[...] = plane_sum(1).astype(BF16)
        for r in (1, 3, 2):
            along_y(n, r).start()
        every[place, c, y] = total[y]

    arrays = (all_gu, all_dn, all_wo, all_qkv)

    def spot(n, r, c_):
        return arrays[n].at[((z + 4 - r % 4) % 4) * 2 + (xh + r // 4) % 2, c_]

    def gd(n, r, recv=False):
        ref = spot(n, r if recv else 0, c)
        return remote(ref, ref, gd_s.at[n, r], gd_r.at[n, r], dev(x + 2 * (r // 4), y, z + r % 4, c))

    def gp(n, r, recv=False):
        ref = spot(n, r, (1 - c) if recv else c)
        return remote(ref, ref, gp_s.at[n, r], gp_r.at[n, r], sibling)

    def pair(n, z_, c_):
        return arrays[n].at[pl.ds(((z_ + 4) % 4) * 2, 2), c_]

    def single(n, z_, h):
        return arrays[n].at[pl.ds(((z_ + 4) % 4) * 2 + h, 1), c]

    def ring(n, k, recv=False):
        if k == 0:
            ref, to = single(n, z, (1 - xh) if recv else xh), dev(x + 2, y, z, c)
        elif k == 1:
            ref, to = pair(n, z - 1 if recv else z, c), dev(x, y, z + 1, c)
        elif k == 2:
            ref, to = pair(n, z + 1 if recv else z, c), dev(x, y, z + 3, c)
        elif k == 3:
            ref, to = single(n, z - 2 if recv else z - 1, 0), dev(x, y, z + 1, c)
        elif k == 4:
            ref, to = single(n, z + 2 if recv else z + 1, 1), dev(x, y, z + 3, c)
        else:
            ref, to = pair(n, z + (k - 5), (1 - c) if recv else c), sibling
        return remote(ref, ref, rg_s.at[n, k], rg_r.at[n, k], to)

    def ring_one(n):
        for r in (1, 3, 2):
            along_y(n, r, True).wait_recv()
        ring(n, 0).start()

    def ring_two(n):
        ring(n, 0, True).wait_recv()
        for k in (1, 2, 5):
            ring(n, k).start()

    def ring_three(n):
        ring(n, 1, True).wait_recv()
        ring(n, 3).start()
        ring(n, 8).start()
        ring(n, 2, True).wait_recv()
        ring(n, 4).start()
        ring(n, 6).start()

    def ring_four(n):
        ring(n, 3, True).wait_recv()
        ring(n, 4, True).wait_recv()
        ring(n, 7).start()

    def ring_five(n):
        for k in (5, 6, 7, 8):
            ring(n, k, True).wait_recv()

    def spread_start(n):
        if n != 2:
            for r in (1, 3, 2):
                along_y(min(n, 2), r, True).wait_recv()
        for r in (2, 1, 3, 6, 5, 7, 4):
            gd(n, r).start()
        gp(n, 0).start()

    def spread_pass(n):
        for r in (1, 3, 2, 4, 5, 7, 6):
            gd(n, r, True).wait_recv()
            gp(n, r).start()

    def spread_finish(n):
        for r in range(8):
            gp(n, r, True).wait_recv()

    def unturn(value, cut):
        value = value.astype(BF16).astype(F32)
        return (value * cos_ref[cut, :] - half_turn(value) * sin_ref[cut, :]).astype(BF16)

    def attend_back(i):
        width = (i + 1) * BLOCK
        cut = slice(i * BLOCK, (i + 1) * BLOCK)
        grad_t = g_mixed[cut, :].T
        grad_bf = g_mixed[cut, :].astype(BF16)
        products = grad_t * mixed_t[:, cut]
        queries_t = []
        for h in range(2):
            lanes = slice(64 * h, 64 * h + 64)
            grad_h = grad_bf[:, lanes]
            delta = jnp.sum(products[lanes, :], axis=0, keepdims=True)
            probs = p_t[h, i, :width, :]
            gv_acc[h, :width, :] += nn(probs, grad_h)
            g_probs = nt(v_h[h, :width, :], grad_h)
            g_scores = (probs.astype(F32) * (g_probs - delta)).astype(BF16)
            gk_acc[h, :width, :] += nn(g_scores, q_h[h, cut, :])
            queries_t.append(nn(k_t[lanes, :width], g_scores))
        g_query = (jnp.concatenate(queries_t, axis=0) * 0.125).T
        g_qkv[cut, :128] = unturn(g_query, cut)

    attend_back(0)
    rs_far(2)
    attend_back(1)
    rs_near(2, 0)
    rs_near(2, 1)
    attend_back(2)
    rs_mid(2)
    share(0)
    share(1)
    attend_back(3)
    for i in range(4):
        cut = slice(i * BLOCK, (i + 1) * BLOCK)
        g_qkv[cut, 128:256] = unturn(jnp.concatenate([gk_acc[0, cut, :], gk_acc[1, cut, :]], axis=1), cut)
        g_qkv[cut, 256:] = jnp.concatenate([gv_acc[0, cut, :], gv_acc[1, cut, :]], axis=1).astype(BF16)
    lo_last = own_part(3)
    rs_start(3, lambda yy: nt(g_qkv[rows(yy * BLOCK, BLOCK), :], wqkv[...]))
    lax.fori_loop(0, 4, grad_qkv, 0)
    plane_start(1)
    ring_one(0)
    ring_one(1)
    rs_mid(3)
    grad_wo()
    plane_start(0)
    ring_two(0)
    ring_two(1)

    c_sib(2, 3).wait_recv()
    for n in (0, 1):
        for h in (0, 1):
            c_fin(2, n, h).wait_recv()
    lo_send[...] = (
        hidden[...] + lo_last + sib[2, 3].astype(F32) + fin_r[2, 0].astype(F32) + fin_r[2, 1].astype(F32)
    ).astype(BF16)
    swap_start(lo_send, layer_out, 2)

    ring_three(0)
    ring_three(1)

    grad = rs_finish(3)
    scale = rms_scale(x32)
    scaled = grad * gathered(0)
    back = scale * scaled - x32 * (scale * scale * scale) * jnp.mean(scaled * x32, axis=-1, keepdims=True)
    gain_one = jnp.sum(grad * x32 * scale, axis=0, keepdims=True)
    ig_send[...] = (g_hidden[...] + back).astype(BF16)
    swap_start(ig_send, in_grad, 3)

    vs[...] = jnp.zeros_like(vs)
    for i in range(8):
        vs[i, 0:1, :] = gain_one[:, 128 * i : 128 * i + 128]
        vs[i, 1:2, :] = gain_two[:, 128 * i : 128 * i + 128]
    bias_sum = jnp.sum(g_qkv[...].astype(F32), axis=0, keepdims=True)
    for i in range(3):
        vs[pl.ds(j, 1), 2 + i : 3 + i, :] = bias_sum[:, 128 * i : 128 * i + 128][None]

    def v1_copy(r):
        return remote(vs.at[(f + r) % 8], vr.at[r - 1], v1_ss.at[r - 1], v1_rs.at[r - 1], (s, (f + r) % 8))

    def v1_start(r, carry):
        v1_copy(r).start()
        return carry

    def v1_wait(r, carry):
        v1_copy(r).wait()
        return carry

    lax.fori_loop(1, 8, v1_start, 0)
    share(2)
    wo_send[...] = plane_sum(0).astype(BF16)
    swap_start(wo_send, all_wo.at[place, (c + moves) % 2], 4)
    lax.fori_loop(1, 8, v1_wait, 0)
    v2s[...] = jnp.sum(vr[...], axis=0) + vs[pl.ds(f, 1)][0]

    def v2_copy(r):
        to = dev(x + 2 * (r // 4), y, z + r % 4, c)
        return remote(v2s, v2r.at[r - 1], v2_ss.at[r - 1], v2_rs.at[r - 1], to)

    def v2_start(r, carry):
        v2_copy(r).start()
        return carry

    def v2_wait(r, carry):
        v2_copy(r).wait()
        return carry

    lax.fori_loop(1, 8, v2_start, 0)
    spread_start(3)
    swap_wait(wo_send, all_wo.at[place, c], 4)
    spread_start(2)
    lax.fori_loop(1, 8, v2_wait, 0)
    v3s[...] = jnp.sum(v2r[...], axis=0) + v2s[...]
    v3_copy = remote(v3s, v3r, v3_ss.at[0], v3_rs.at[0], sibling)
    v3_copy.start()
    ring_four(0)
    ring_four(1)
    for n in (3, 2):
        spread_pass(n)
    v3_copy.wait()
    vec_out[...] = v3s[...] + v3r[...]
    swap_wait(lo_send, layer_out, 2)
    swap_wait(ig_send, in_grad, 3)
    for n in (0, 1):
        ring_five(n)
    for n in (3, 2):
        spread_finish(n)

    for n in range(4):
        for r in (1, 2, 3):
            for p in range(PARTS[n]):
                w_y(n, p, r).wait_send()
            for dz in (1, 2, 3):
                w_z(n, r, dz).wait_send()
        for r in range(4):
            w_x(n, r).wait_send()
    for n in range(1, 8):
        wo_pass(n).wait_send()
    for k, buf in enumerate((normed_all, cot_all, mlp_all, branch_all)):
        for n in range(8):
            ag(buf, k, n).wait_send()
    for k in range(1, 4):
        if k == 3:
            for i in range(4):
                c_sib(k, i).wait_send()
        for n in (0, 1):
            c_far(k, n).wait_send()
            for h in (0, 1):
                c_fin(k, n, h).wait_send()
    for n in range(3):
        for r in (1, 2, 3):
            along_y(n, r).wait_send()
    for n in (0, 1):
        for k in range(9):
            ring(n, k).wait_send()
    for n in (2, 3):
        for r in range(8):
            if r > 0:
                gd(n, r).wait_send()
            gp(n, r).wait_send()


def fused_layer(*args):
    def vmem(*shape, dtype=BF16):
        return pltpu.VMEM(shape, dtype)

    def dma(*shape):
        return pltpu.SemaphoreType.DMA(shape)

    full = vmem(D, D)
    scratch = [
        vmem(D, 128, dtype=F32), vmem(D, 128, dtype=F32), vmem(1, D, dtype=jnp.int32), vmem(8, 128, dtype=F32),
        vmem(PIECE, D), vmem(PIECE, D), vmem(PIECE, D, dtype=F32), vmem(PIECE, D, dtype=F32),
        full, vmem(D, FB), vmem(D, 2 * FB), vmem(FB, D), vmem(8, 8, 128, dtype=F32),
        full, full, full, full,
        vmem(2, D, 64), vmem(2, D, 64), vmem(2, D, 64), vmem(128, D), vmem(128, D),
        vmem(2, 4, D, BLOCK), vmem(128, D, dtype=F32), vmem(D, 128), vmem(PIECE, D),
        vmem(D, FB, dtype=F32), vmem(D, FB), vmem(FB, D), vmem(D, 2 * FB), vmem(D, 128, dtype=F32),
        vmem(2, D, 64, dtype=F32), vmem(2, D, 64, dtype=F32), vmem(D, FB),
        vmem(4, BLOCK, D), vmem(4, 4, PIECE, D), vmem(4, PIECE, D), vmem(4, 2, 64, D), vmem(4, 2, PIECE, D), vmem(4, 2, PIECE, D),
        vmem(4, 4, 4, 16, 512), vmem(4, 4, 4, 16, 256), vmem(4, 4, 4, 48, 128), vmem(16, 64, 128), vmem(16, 4, 16, FB),
        vmem(3, 4, 4, 16, 512), vmem(3, 4, 4, 16, 256), vmem(3, 4, 4, 48, 128),
        vmem(4, 4, 16, 512), vmem(4, 4, 16, 256), vmem(4, 4, 48, 128),
        vmem(3, 4, 16, 512), vmem(3, 4, 16, 256), vmem(3, 4, 48, 128),
        vmem(15, 64, 128), vmem(15, 4, 16, FB),
        vmem(64, 128), vmem(4, 16, 2 * FB), vmem(4, 48, 128), vmem(4, 16, FB),
        vmem(PIECE, D), vmem(PIECE, D),
        vmem(8, 8, 128, dtype=F32), vmem(7, 8, 128, dtype=F32), vmem(8, 128, dtype=F32), vmem(7, 8, 128, dtype=F32),
        vmem(8, 128, dtype=F32), vmem(8, 128, dtype=F32),
        dma(9), dma(5), dma(5), dma(8), dma(8), dma(4, 3, 4), dma(4, 3, 4), dma(4, 4, 4), dma(4, 4, 4), dma(4, 4), dma(4, 4),
        dma(8), dma(8), dma(8), dma(8), dma(4, 8), dma(4, 8),
        dma(4, 4), dma(4, 4), dma(4, 2), dma(4, 2), dma(4, 2, 2), dma(4, 2, 2),
        dma(2, 15), dma(2, 15), dma(3, 4), dma(3, 4), dma(3, 4), dma(3, 4), dma(3, 4), dma(3, 4), dma(2, 9), dma(2, 9), dma(4, 8), dma(4, 8), dma(4, 8), dma(4, 8),
        dma(7), dma(7), dma(7), dma(7), dma(1), dma(1),
    ]
    anywhere = pl.BlockSpec(memory_space=pl.ANY)
    inside = pl.BlockSpec(memory_space=pltpu.VMEM)

    def out(*shape, dtype=BF16):
        return jax.ShapeDtypeStruct(shape, dtype)

    return pl.pallas_call(
        layer_kernel,
        out_shape=(
            out(PIECE, D), out(PIECE, D), out(8, 2, 4, 16, 2 * FB), out(8, 2, 4, 48, 128), out(8, 2, 64, 128),
            out(8, 2, 4, 16, FB), out(8, 128, dtype=F32),
        ),
        in_specs=[anywhere] * 11 + [inside] * 6,
        out_specs=[inside] * 7,
        scratch_shapes=scratch,
        compiler_params=pltpu.CompilerParams(
            collective_id=0, has_side_effects=True, vmem_limit_bytes=63 * 1024 * 1024
        ),
        name="layer",
    )(*args)


def spread_kernel(
    lo_in, ig_in, gu_in, dn_in, wo_in, qkv_in, vec_in,
    lo, ig, d_gain_a, d_q, d_k, d_v, d_bq, d_bk, d_bv, d_o, d_gain_m, d_gate, d_up, d_down,
    lo_v, ig_v, gu, dn, wo, qkv, vec, sems,
):
    loads = [
        pltpu.make_async_copy(src, dst, sems.at[i])
        for i, (src, dst) in enumerate(
            ((vec_in, vec), (qkv_in, qkv), (wo_in, wo), (gu_in, gu), (dn_in, dn), (ig_in, ig_v), (lo_in, lo_v))
        )
    ]
    for load in loads:
        load.start()
    loads[0].wait()
    for ref, row in ((d_gain_a, 0), (d_gain_m, 1), (d_bq, 2), (d_bk, 3), (d_bv, 4)):
        ref[...] = vec[row : row + 1, :]
    loads[1].wait()
    for t in range(8):
        cut = slice(16 * t, 16 * t + 16)
        for m in range(8):
            for i, ref in enumerate((d_q, d_k, d_v)):
                ref[cut, 128 * m : 128 * m + 128] = qkv[t, m % 2, m // 2, :, 128 * i : 128 * i + 128].astype(F32)
    loads[2].wait()
    flip = lax.axis_index("fsdp") % 2
    for t in range(8):
        for core in range(2):
            to = pl.ds(pl.multiple_of(64 * ((core + flip) % 2), 64), 64)
            d_o[to, 128 * t : 128 * t + 128] = wo[t, core].astype(F32)
    loads[3].wait()
    loads[4].wait()
    for m in range(8):
        first = 128 if m == 7 else 0
        count = 256 if m >= 6 else FB
        start = min(m, 6) * FB + (256 if m == 7 else 0)
        for t in range(8):
            cut = slice(16 * t, 16 * t + 16)
            d_gate[cut, start : start + count] = gu[t, m % 2, m // 2, :, first : first + count].astype(F32)
            d_up[cut, start : start + count] = gu[t, m % 2, m // 2, :, FB + first : FB + first + count].astype(F32)
            low, high = max(48 * t, first), min(48 * t + 48, first + count)
            if low < high:
                d_down[start + low - first : start + high - first, :] = dn[
                    t, m % 2, m // 2, low - 48 * t : high - 48 * t, :
                ].astype(F32)
    loads[5].wait()
    ig[...] = ig_v[...].astype(F32)
    loads[6].wait()
    lo[...] = lo_v[...]


def spread(*args):
    def out(*shape, dtype=F32):
        return jax.ShapeDtypeStruct(shape, dtype)

    inside = pl.BlockSpec(memory_space=pltpu.VMEM)
    vec, square, wide = out(1, 128), out(128, D), out(128, 2816)
    return pl.pallas_call(
        spread_kernel,
        out_shape=(
            out(PIECE, D, dtype=BF16), out(PIECE, D), vec, square, square, square, vec, vec, vec,
            square, vec, wide, wide, out(2816, 128),
        ),
        in_specs=[pl.BlockSpec(memory_space=pl.ANY)] * 7,
        out_specs=[inside] * 14,
        scratch_shapes=[pltpu.VMEM(a.shape, a.dtype) for a in args] + [pltpu.SemaphoreType.DMA((7,))],
        compiler_params=pltpu.CompilerParams(vmem_limit_bytes=60 * 1024 * 1024),
        name="spread",
    )(*args)


def rotary_tables():
    exponent = np.arange(HEAD_DIM // 2, dtype=np.float32) * np.float32(2.0 / HEAD_DIM)
    inverse = np.exp(np.float32(-math.log(THETA)) * exponent)
    angles = np.arange(D, dtype=np.float32)[:, None] * inverse
    cos, sin = np.cos(angles), np.sin(angles)
    return np.concatenate([cos] * 4, axis=1), np.concatenate([-sin, sin] * 2, axis=1)


def per_device(
    inputs, doc_ids, positions, attn_gain, query_weight, key_weight, value_weight,
    query_bias, key_bias, value_bias, out_weight, mlp_gain, gate_weight, up_weight,
    down_weight, cotangent,
):
    del positions
    cos, sin = rotary_tables()
    vectors = [v.reshape(1, 128) for v in (attn_gain, mlp_gain, query_bias, key_bias, value_bias)]
    blocks = fused_layer(
        inputs.reshape(PIECE, D), cotangent.reshape(PIECE, D),
        query_weight, key_weight, value_weight, out_weight, gate_weight, up_weight, down_weight,
        jnp.asarray(cos), jnp.asarray(sin), *vectors, doc_ids,
    )
    outs = list(spread(*blocks))
    outs[0] = outs[0].reshape(inputs.shape)
    outs[1] = outs[1].reshape(inputs.shape)
    return tuple(o.reshape(128) if o.shape == (1, 128) else o for o in outs)


def solution(mesh):
    rows_spec = P("fsdp", None)
    act = P("seq", "fsdp", None)
    vec = P("fsdp")
    return jax.shard_map(
        per_device,
        mesh=mesh,
        in_specs=(
            act, P(), P("seq", "fsdp"), vec, rows_spec, rows_spec, rows_spec, vec, vec, vec,
            rows_spec, vec, rows_spec, rows_spec, P(None, "fsdp"), act,
        ),
        out_specs=(
            act, act, vec, rows_spec, rows_spec, rows_spec, vec, vec, vec, rows_spec, vec,
            rows_spec, rows_spec, P(None, "fsdp"),
        ),
        check_vma=False,
    )
```

```python
import math

import jax
import jax.numpy as jnp
import numpy as np
from jax import lax
from jax.experimental import pallas as pl
from jax.experimental.pallas import tpu as pltpu
from jax.sharding import PartitionSpec as P

MESH = pl.DeviceIdType.MESH
HEAD_DIM = 64
EPS = 1e-06
THETA = 1000000.0
NEG = -1000000000.0
D = 1024
PIECE = 128
BLOCK = 256
FB = 384
F32 = jnp.float32
BF16 = jnp.bfloat16


def nn(a, b):
    return lax.dot_general(a, b, (((1,), (0,)), ((), ())), preferred_element_type=F32)


def nt(a, b):
    return lax.dot_general(a, b, (((1,), (1,)), ((), ())), preferred_element_type=F32)


def tn(a, b):
    return lax.dot_general(a, b, (((0,), (0,)), ((), ())), preferred_element_type=F32)


def rms_scale(value):
    return lax.rsqrt(jnp.mean(value * value, axis=-1, keepdims=True) + EPS)


def rows(start, size):
    return pl.ds(pl.multiple_of(start, size), size)


def half_turn(value):
    lane = lax.broadcasted_iota(jnp.int32, value.shape, 1)
    ahead = pltpu.roll(value, 96, 1)
    behind = pltpu.roll(value, 32, 1)
    return jnp.where(lane % 64 < 32, ahead, behind)


def layer_kernel(
    x_in, cot_in, wq_in, wk_in, wv_in, wo_in, wg_in, wu_in, wd_in, cos_in, sin_in,
    gain_a, gain_m, bias_q, bias_k, bias_v, docs,
    layer_out, in_grad, all_gu, all_dn, all_wo, all_qkv, vec_out,
    cos_ref, sin_ref, start_ref, vec_in,
    x_own, cot_own, hidden, g_hidden, wo_all, wqkv, wgu, wdn, vall,
    normed_all, cot_all, mlp_all, branch_all,
    q_h, k_h, v_h, k_t, v_t, p_t, mixed_t, mixed, mixed_own, mixed_grad,
    g_act, active, active_t, g_gu, g_mixed, gk_acc, gv_acc, g_qkv,
    part, sib, far_s, far_r, fin_s, fin_r,
    dga, dgb, ddn, dqa, dqb, dwo, ra, rb, rd, rqa, rqb, rw, ha, hb, hd, hqa, hqb, hw, sa, sb, sd, sqa, sqb, sw, wo_send, sum_gu, sum_dn, sum_qkv,
    lo_send, ig_send,
    vs, vr, v2s, v2r, v3s, v3r,
    sem_load, swap_s, swap_r, vec_s, vec_r, wy_s, wy_r, wz_s, wz_r, wx_s, wx_r, wp_s, wp_r, mx_s, mx_r, um_s, um_r, ag_s, ag_r,
    sib_ss, sib_rs, far_ss, far_rs, fin_ss, fin_rs,
    f1_s, f1_r, f2_s, f2_r, ya_s, ya_r, rg_s, rg_r, gd_s, gd_r, gp_s, gp_r, v1_ss, v1_rs, v2_ss, v2_rs, v3_ss, v3_rs,
):
    s = lax.axis_index("seq")
    f = lax.axis_index("fsdp")
    xh = s // 8
    z = (s % 8) // 2
    c = s % 2
    y = f // 2
    xl = f % 2
    x = xh * 2 + xl
    j = y * 2 + c
    place = z * 2 + xh

    def dev(x_, y_, z_, c_):
        x_, y_, z_ = (x_ + 4) % 4, (y_ + 4) % 4, (z_ + 4) % 4
        return ((x_ // 2) * 8 + z_ * 2 + c_, y_ * 2 + x_ % 2)

    sibling = dev(x, y, z, 1 - c)
    y_up = dev(x, y + 1, z, c)
    y_dn = dev(x, y + 3, z, c)
    moves = (c + xl) % 2
    partner = dev(xh * 2 + 1 - xl, y, z, 1 - c)
    x_to = dev(x + 1 + 2 * c, y, z, c)

    def window(m):
        return (3 * m - 2 * (m // 7)) * 128

    def remote(src, dst, ss, rs, to):
        return pltpu.make_async_remote_copy(
            src_ref=src, dst_ref=dst, send_sem=ss, recv_sem=rs, device_id=to, device_id_type=MESH
        )

    def at(start, size, unit):
        return pl.ds(pl.multiple_of(start, unit), size)

    own_rows = rows(f * 128, 128)
    own_win = at(window(j), FB, 128)
    loads = [
        pltpu.make_async_copy(wq_in.at[:, rows(j * 128, 128)], wqkv.at[own_rows, pl.ds(0, 128)], sem_load.at[0]),
        pltpu.make_async_copy(wk_in.at[:, rows(j * 128, 128)], wqkv.at[own_rows, pl.ds(128, 128)], sem_load.at[1]),
        pltpu.make_async_copy(wv_in.at[:, rows(j * 128, 128)], wqkv.at[own_rows, pl.ds(256, 128)], sem_load.at[2]),
        pltpu.make_async_copy(wo_in, wo_all.at[own_rows], sem_load.at[3]),
        pltpu.make_async_copy(wg_in.at[:, own_win], wgu.at[own_rows, pl.ds(0, FB)], sem_load.at[4]),
        pltpu.make_async_copy(wu_in.at[:, own_win], wgu.at[own_rows, pl.ds(FB, FB)], sem_load.at[5]),
        pltpu.make_async_copy(wd_in.at[own_win, :], wdn.at[:, own_rows], sem_load.at[6]),
        pltpu.make_async_copy(cos_in, cos_ref, sem_load.at[7]),
        pltpu.make_async_copy(sin_in, sin_ref, sem_load.at[8]),
    ]
    for load in loads:
        load.start()

    barrier = pltpu.get_barrier_semaphore()

    def greet(to):
        pl.semaphore_signal(barrier, inc=1, device_id=to, device_id_type=MESH)

    def greet_near(r, carry):
        greet(dev(x + r, y, z, c))
        greet(dev(x, y, z + r, c))
        greet(dev(x + 2, y, z + r, c))
        return carry

    def greet_fsdp(r, carry):
        greet((s, (f + r) % 8))
        return carry

    def greet_cross(r, carry):
        greet(dev(x, y + r, z, 1 - c))
        return carry

    lax.fori_loop(1, 4, greet_near, 0)
    lax.fori_loop(1, 8, greet_fsdp, 0)
    lax.fori_loop(0, 4, greet_cross, 0)

    @pl.when(moves == 1)
    def _():
        greet(partner)
        pl.semaphore_wait(barrier, 21)

    @pl.when(moves == 0)
    def _():
        pl.semaphore_wait(barrier, 20)

    def swap_start(src, dst, n):
        @pl.when(moves == 1)
        def _():
            remote(src, dst, swap_s.at[n], swap_r.at[n], partner).start()

        @pl.when(moves == 0)
        def _():
            pltpu.make_async_copy(src, dst, swap_r.at[n]).start()

    def swap_wait(src, dst, n):
        @pl.when(moves == 1)
        def _():
            remote(src, dst, swap_s.at[n], swap_r.at[n], partner).wait()

        @pl.when(moves == 0)
        def _():
            pltpu.make_async_copy(src, dst, swap_r.at[n]).wait()

    def vec_copy(r):
        return remote(vec_in, vall.at[f], vec_s.at[r], vec_r.at[r], (s, (f + r) % 8))

    def vec_start(r, carry):
        vec_copy(r).start()
        return carry

    def vec_wait(r, carry):
        vec_copy(r).wait()
        return carry

    vec_in[...] = jnp.zeros_like(vec_in)
    for i, ref in enumerate((gain_a, gain_m, bias_q, bias_k, bias_v)):
        vec_in[i : i + 1, :] = ref[...].astype(F32)
    lax.fori_loop(1, 8, vec_start, 0)
    swap_start(x_in, x_own, 0)
    vall[pl.ds(f, 1)] = vec_in[...][None]
    doc_row = docs[pl.ds(xh * 8 + z * 2 + xl, 1), :]
    start_ref[...] = jnp.where(doc_row == 1, jnp.sum(1 - doc_row, axis=1, keepdims=True), 0)

    PARTS = (3, 2, 1, 1)

    def shard(r):
        return ((y + 4 - r) % 4) * 2 + xl

    def w_quarter(n, f_, q, p=None):
        if n == 0:
            return wqkv.at[at(f_ * 128 + q * 32, 32, 32), slice(None) if p is None else pl.ds(p * 128, 128)]
        if n == 1:
            return wgu.at[at(f_ * 128 + q * 32, 32, 32), slice(None) if p is None else pl.ds(p * FB, FB)]
        if n == 2:
            return wdn.at[at(q * 96, 96, 32), rows(f_ * 128, 128)]
        return wo_all.at[at(f_ * 128 + c * 64 + q * 16, 16, 16)]

    def w_rows(n, f_):
        if n == 0:
            return wqkv.at[rows(f_ * 128, 128)]
        if n == 1:
            return wgu.at[rows(f_ * 128, 128)]
        if n == 2:
            return wdn.at[:, rows(f_ * 128, 128)]
        return wo_all.at[rows(f_ * 128 + c * 64, 64)]

    def w_y(n, p, r, recv=False):
        m = ((y + r) % 4) * 2 + c
        if n == 0:
            src = (wq_in, wk_in, wv_in)[p].at[at(z * 32, 32, 32), rows(m * 128, 128)]
        elif n == 1:
            src = (wg_in, wu_in)[p].at[at(z * 32, 32, 32), at(window(m), FB, 128)]
        elif n == 2:
            src = wd_in.at[at(window(m) + z * 96, 96, 32), :]
        else:
            src = wo_in.at[at(c * 64 + z * 16, 16, 16)]
        dst = w_quarter(n, shard(r) if recv else f, z, p)
        return remote(src, dst, wy_s.at[n, p, r], wy_r.at[n, p, r], dev(x, y + r, z, c))

    def w_z(n, r, dz, recv=False):
        src = w_quarter(n, shard(r), z)
        dst = w_quarter(n, shard(r), (z + 4 - dz) % 4) if recv else src
        return remote(src, dst, wz_s.at[n, r, dz], wz_r.at[n, r, dz], dev(x, y, z + dz, c))

    def w_x(n, r, recv=False):
        src = w_rows(n, shard(r))
        dst = w_rows(n, ((y + 4 - r) % 4) * 2 + 1 - xl) if recv else src
        return remote(src, dst, wx_s.at[n, r], wx_r.at[n, r], x_to)

    def w_ystart(n):
        for r in (1, 3, 2):
            for p in range(PARTS[n]):
                w_y(n, p, r).start()

    def w_own(n):
        for load in (loads[:3], loads[4:6], loads[6:7], loads[3:4])[n]:
            load.wait()
        w_x(n, 0).start()

    def w_zstart(n):
        for r in (1, 3, 2):
            for p in range(PARTS[n]):
                w_y(n, p, r, True).wait_recv()
            for dz in (1, 3, 2):
                w_z(n, r, dz).start()

    def w_xstart(n):
        for r in (1, 3, 2):
            for dz in (1, 3, 2):
                w_z(n, r, dz, True).wait_recv()
            w_x(n, r).start()
            if n == 3:
                wo_pass(2 * ((4 - r) % 4)).start()

    def w_finish(n):
        for r in range(4):
            w_x(n, r, True).wait_recv()

    def wo_pass(n, recv=False):
        f_ = ((y + n // 2) % 4) * 2 + (xl + n % 2) % 2
        ref = wo_all.at[rows(f_ * 128 + ((1 - c) if recv else c) * 64, 64)]
        return remote(ref, ref, wp_s.at[n], wp_r.at[n], sibling)

    def wo_pass_x():
        for r in range(4):
            w_x(3, r, True).wait_recv()
            wo_pass(2 * ((4 - r) % 4) + 1).start()

    def wo_pass_finish():
        for n in range(1, 8):
            wo_pass(n, True).wait_recv()

    for n in (0, 3, 2, 1):
        w_ystart(n)
    w_own(0)

    def piece(buf, y_, c_):
        return buf.at[rows((((y_ + 4) % 4) * 2 + c_) * PIECE, PIECE)]

    def half(buf, y_, c_, h):
        return buf.at[rows((((y_ + 4) % 4) * 2 + c_) * PIECE + h * 64, 64)]

    def ag(buf, k, n, recv=False):
        if n in (0, 8):
            h = 0 if n == 0 else 1
            ref, to = (half(buf, y - 1, c, h) if recv else half(buf, y, c, h)), y_up
        elif n in (1, 9):
            h = 1 if n == 1 else 0
            ref, to = (half(buf, y + 1, c, h) if recv else half(buf, y, c, h)), y_dn
        elif n == 2:
            ref, to = (piece(buf, y, 1 - c) if recv else piece(buf, y, c)), sibling
        elif n == 3:
            ref, to = (half(buf, y - 2, c, 0) if recv else half(buf, y - 1, c, 0)), y_up
        elif n == 4:
            ref, to = (piece(buf, y - 1, 1 - c) if recv else piece(buf, y - 1, c)), sibling
        elif n == 5:
            ref, to = (half(buf, y + 2, c, 1) if recv else half(buf, y + 1, c, 1)), y_dn
        elif n == 6:
            ref, to = (piece(buf, y + 1, 1 - c) if recv else piece(buf, y + 1, c)), sibling
        else:
            ref, to = (piece(buf, y + 2, 1 - c) if recv else piece(buf, y + 2, c)), sibling
        return remote(ref, ref, ag_s.at[k, n], ag_r.at[k, n], to)

    def ag_start(buf, k):
        for n in (0, 1, 2, 8, 9):
            ag(buf, k, n).start()

    def ag_near(buf, k):
        ag(buf, k, 0, True).wait_recv()
        ag(buf, k, 3).start()
        ag(buf, k, 1, True).wait_recv()
        ag(buf, k, 5).start()

    def ag_pass(buf, k):
        ag(buf, k, 8, True).wait_recv()
        ag(buf, k, 4).start()
        ag(buf, k, 9, True).wait_recv()
        ag(buf, k, 6).start()

    def ag_far(buf, k):
        ag(buf, k, 3, True).wait_recv()
        ag(buf, k, 5, True).wait_recv()
        ag(buf, k, 7).start()

    def ag_finish(buf, k):
        for n in (2, 4, 6, 7):
            ag(buf, k, n, True).wait_recv()

    def ag_run(buf, k, consume, after_pass=None, after_far=None):
        def step(i, carry):
            @pl.when(i == 0)
            def _():
                ag(buf, k, 2, True).wait_recv()

            @pl.when(i == 1)
            def _():
                ag_pass(buf, k)
                if after_pass is not None:
                    after_pass()
                ag(buf, k, 4, True).wait_recv()

            @pl.when(i == 2)
            def _():
                ag(buf, k, 6, True).wait_recv()
                ag_far(buf, k)

            @pl.when(i == 3)
            def _():
                if after_far is not None:
                    after_far()
                ag(buf, k, 7, True).wait_recv()

            consume((y + (3 * ((i * (i + 1)) // 2)) % 4) % 4)

            @pl.when(i == 0)
            def _():
                if k > 0:
                    ag_near(buf, k)

            return carry

        lax.fori_loop(0, 4, step, 0)

    def held(k):
        return part.at[1 if k == 2 else 0]

    def own_part(k, a):
        return held(k)[a, rows(c * PIECE, PIECE), :].astype(F32)

    def c_sib(k, a):
        src = held(k).at[a, rows((1 - c) * PIECE, PIECE)]
        return remote(src, sib.at[k, a], sib_ss.at[k, a], sib_rs.at[k, a], sibling)

    def c_far(k, n):
        return remote(far_s.at[k, pl.ds(64 * n, 64)], far_r.at[k, n], far_ss.at[k, n], far_rs.at[k, n], y_up if n == 0 else y_dn)

    def c_fin(k, n, h):
        cut = pl.ds(64 * h, 64)
        return remote(fin_s.at[k, n, cut], fin_r.at[k, n, cut], fin_ss.at[k, n, h], fin_rs.at[k, n, h], y_up if n == 0 else y_dn)

    def rs_put(k, a, value):
        if k == 3:
            c_sib(1, a).wait_send()
        held(k)[a] = value.astype(BF16)
        c_sib(k, a).start()

    def rs_pair(k, a):
        c_sib(k, a).wait_recv()
        return own_part(k, a) + sib[k, a].astype(F32)

    def rs_far(k):
        far_s[k] = rs_pair(k, (y + 2) % 4).astype(BF16)
        c_far(k, 0).start()
        c_far(k, 1).start()

    def rs_near(k, n):
        fin_s[k, n] = rs_pair(k, (y + 1 + 2 * n) % 4).astype(BF16)
        c_fin(k, n, 1 - n).start()

    def rs_mid(k):
        for n in (0, 1):
            c_far(k, n).wait_recv()
            cut = pl.ds(64 * n, 64)
            fin_s[k, n, cut] = (fin_s[k, n, cut].astype(F32) + far_r[k, n].astype(F32)).astype(BF16)
            c_fin(k, n, n).start()

    def rs_finish(k):
        total = rs_pair(k, y)
        for n in (0, 1):
            for h in (0, 1):
                c_fin(k, n, h).wait_recv()
        return total + fin_r[k, 0].astype(F32) + fin_r[k, 1].astype(F32)

    w_zstart(0)
    lax.fori_loop(1, 8, vec_wait, 0)

    def gathered(row):
        return jnp.concatenate([vall[i, row : row + 1, :] for i in range(8)], axis=1)

    swap_wait(x_in, x_own, 0)
    x32 = x_own[...].astype(F32)
    normed_all[rows(j * PIECE, PIECE), :] = (x32 * rms_scale(x32) * gathered(0)).astype(BF16)
    ag_start(normed_all, 0)
    w_xstart(0)
    swap_start(cot_in, cot_own, 1)
    w_zstart(3)
    w_own(3)
    w_zstart(2)
    w_own(2)
    w_zstart(1)
    w_own(1)
    ag_near(normed_all, 0)
    for load in loads[7:]:
        load.wait()
    w_finish(0)

    def project(yy):
        cut = rows(yy * BLOCK, BLOCK)
        lin = nn(normed_all[cut, :], wqkv[...])
        cos = cos_ref[cut, :]
        sin = sin_ref[cut, :]
        bias = vall[pl.ds(j, 1)][0]
        q_lin = lin[:, :128] + bias[2:3, :]
        k_lin = lin[:, 128:256] + bias[3:4, :]
        v_lin = lin[:, 256:] + bias[4:5, :]
        q = (q_lin * cos + half_turn(q_lin) * sin).astype(BF16) * 0.125
        k32 = k_lin * cos + half_turn(k_lin) * sin
        k = k32.astype(BF16)
        v = v_lin.astype(BF16)
        for h in range(2):
            lanes = slice(64 * h, 64 * h + 64)
            q_h[h, cut, :] = q[:, lanes]
            k_h[h, cut, :] = k[:, lanes]
            v_h[h, cut, :] = v[:, lanes]
        k_t[:, cut] = k32.T.astype(BF16)
        v_t[:, cut] = v_lin.T.astype(BF16)

    def cot_start():
        swap_wait(cot_in, cot_own, 1)
        cot_all[rows(j * PIECE, PIECE), :] = cot_own[...]
        ag_start(cot_all, 1)

    ag_run(normed_all, 0, project, lambda: w_xstart(3), cot_start)

    def attend(i):
        width = (i + 1) * BLOCK
        cut = slice(i * BLOCK, (i + 1) * BLOCK)
        key_at = lax.broadcasted_iota(jnp.int32, (width, BLOCK), 0)
        query_at = lax.broadcasted_iota(jnp.int32, (width, BLOCK), 1) + i * BLOCK
        allowed = (key_at >= start_ref[0:1, cut]) & (key_at <= query_at)
        for h in range(2):
            scores = nt(k_h[h, :width, :], q_h[h, cut, :])
            scores = jnp.where(allowed, scores, NEG)
            weights = jnp.exp(scores - jnp.max(scores, axis=0, keepdims=True))
            inverse = 1.0 / jnp.sum(weights, axis=0, keepdims=True)
            probs = (weights * inverse).astype(BF16)
            p_t[h, i, :width, :] = probs
            mixed_t[64 * h : 64 * h + 64, cut] = nn(v_t[64 * h : 64 * h + 64, :width], probs)
        mixed[cut, :] = mixed_t[:, cut].T.astype(BF16)
        for m in (2 * i, 2 * i + 1):
            mix_start(m)

    def mix(m, sender):
        return remote(
            mixed.at[rows(m * PIECE, PIECE), :], mixed_own.at[:, rows(sender * 128, 128)],
            mx_s.at[m], mx_r.at[sender], dev(x, m // 2, z, m % 2),
        )

    def mix_start(m):
        @pl.when(j != m)
        def _():
            mix(m, j).start()

        @pl.when(j == m)
        def _():
            mixed_own[:, rows(j * 128, 128)] = mixed[m * PIECE : (m + 1) * PIECE, :]

    def mix_wait(r, carry):
        m = (j + r) % 8
        mix(m, m).wait_recv()
        mix(m, j).wait_send()
        return carry

    w_xstart(2)
    attend(0)
    w_xstart(1)
    ag_near(cot_all, 1)
    attend(1)
    attend(2)
    wo_pass_x()
    attend(3)
    ag_pass(cot_all, 1)
    wo_pass_finish()
    lax.fori_loop(1, 8, mix_wait, 0)

    hidden[...] = x_own[...].astype(F32) + nn(mixed_own[...], wo_all[...])
    hid = hidden[...]
    mlp_all[rows(j * PIECE, PIECE), :] = (hid * rms_scale(hid) * gathered(1)).astype(BF16)
    ag_start(mlp_all, 2)
    ag_far(cot_all, 1)
    w_finish(2)
    ag_finish(cot_all, 1)

    def active_back(i, carry):
        cut = rows(i * BLOCK, BLOCK)
        g_act[cut, :] = nt(cot_all[cut, :], wdn[...])
        return carry

    lax.fori_loop(0, 4, active_back, 0)
    w_finish(1)

    unit = lax.broadcasted_iota(jnp.int32, (1, FB), 1)
    low_edge = 128 * (j // 7)
    high_edge = FB - 128 * ((j // 6) * (1 - j // 7))
    live = (unit >= low_edge) & (unit < high_edge)

    def feed(yy):
        cut = rows(yy * BLOCK, BLOCK)
        both = nn(mlp_all[cut, :], wgu[...])
        gate = both[:, :FB]
        up = both[:, FB:]
        sig = 1.0 / (1.0 + jnp.exp(-gate))
        silu = gate * sig
        back = jnp.where(live, g_act[cut, :], 0.0)
        act = jnp.where(live, silu * up, 0.0)
        active[cut, :] = act.astype(BF16)
        g_gu[cut, :FB] = (back * up * sig * (1.0 + gate * (1.0 - sig))).astype(BF16)
        g_gu[cut, FB:] = (back * silu).astype(BF16)
        rs_put(1, yy, nt(g_gu[cut, :], wgu[...]))

    ag_run(mlp_all, 2, feed)
    rs_far(1)

    terms = (dga, dgb, ddn, dqa, dqb, dwo)
    term_in = (ra, rb, rd, rqa, rqb, rw)
    halfway = (ha, hb, hd, hqa, hqb, hw)
    half_in = (sa, sb, sd, sqa, sqb, sw)

    def first(n, r):
        if n in (0, 3, 5):
            src, to = terms[n].at[(x + r) % 4], dev(x + r, y, z, c)
        else:
            src, to = terms[n].at[:, (z + r) % 4], dev(x, y, z + r, c)
        return remote(src, term_in[n].at[r - 1], f1_s.at[n, r], f1_r.at[n, r], to)

    def second(n, r):
        if n in (0, 3, 5):
            src, to = halfway[n].at[(z + r) % 4], dev(x, y, z + r, c)
        else:
            src, to = halfway[n].at[(x + r) % 4], dev(x + r, y, z, c)
        return remote(src, half_in[n].at[r - 1], f2_s.at[n, r], f2_r.at[n, r], to)

    def first_start(n):
        for r in (1, 3, 2):
            first(n, r).start()

    def first_sum(n):
        total = (terms[n][x] if n in (0, 3, 5) else terms[n][:, z]).astype(F32)
        for r in (1, 3, 2):
            first(n, r).wait()
            total = total + term_in[n][r - 1].astype(F32)
        halfway[n][...] = total.astype(BF16)
        for r in (1, 3, 2):
            second(n, r).start()

    def second_sum(n):
        total = halfway[n][z if n in (0, 3, 5) else x].astype(F32)
        for r in (1, 3, 2):
            second(n, r).wait()
            total = total + half_in[n][r - 1].astype(F32)
        return total.astype(BF16)

    def chunk(t, xl_):
        return (t % 2) * 2 + xl_, t // 2

    def grad_gu(i, carry):
        got = tn(mlp_all[:, rows(i * BLOCK, BLOCK)], g_gu[...]).astype(BF16)
        for xl_ in range(2):
            for t in range(8):
                x_, z_ = chunk(t, xl_)
                share = got[xl_ * 128 + t * 16 : xl_ * 128 + t * 16 + 16]
                dga[x_, z_, i] = share[:, :512]
                dgb[x_, z_, i] = share[:, 512:]
        return carry

    def grad_dn(i, carry):
        got = nn(active_t[...], cot_all[:, rows(i * BLOCK, BLOCK)]).astype(BF16)
        for xl_ in range(2):
            for t in range(8):
                x_, z_ = chunk(t, xl_)
                ddn[x_, z_, i] = got[t * 48 : t * 48 + 48, xl_ * 128 : xl_ * 128 + 128]
        return carry

    def grad_qkv(i, carry):
        got = tn(normed_all[:, rows(i * BLOCK, BLOCK)], g_qkv[...]).astype(BF16)
        for xl_ in range(2):
            for t in range(8):
                x_, z_ = chunk(t, xl_)
                share = got[xl_ * 128 + t * 16 : xl_ * 128 + t * 16 + 16]
                dqa[x_, z_, i] = share[:, :256]
                dqb[x_, z_, i] = share[:, 256:]
        return carry

    def grad_wo():
        got = tn(mixed[...], branch_all[...]).astype(BF16)
        for h in range(2):
            for t in range(8):
                x_, z_ = chunk(t, (h + c) % 2)
                dwo[pl.ds(x_, 1), z_] = got[h * 64 : h * 64 + 64, t * 128 : t * 128 + 128][None]

    lax.fori_loop(0, 4, grad_gu, 0)
    rs_near(1, 0)
    rs_near(1, 1)
    first_start(1)
    first_start(0)
    rs_mid(1)
    active_t[...] = active[...].T
    lax.fori_loop(0, 4, grad_dn, 0)
    first_start(2)

    grad = rs_finish(1)
    hid = hidden[...]
    scale = rms_scale(hid)
    scaled = grad * gathered(1)
    back = scale * scaled - hid * (scale * scale * scale) * jnp.mean(scaled * hid, axis=-1, keepdims=True)
    gain_two = jnp.sum(grad * hid * scale, axis=0, keepdims=True)
    g_hidden[...] = cot_own[...].astype(F32) + back
    branch_all[rows(j * PIECE, PIECE), :] = g_hidden[...].astype(BF16)

    def unmix_term(i, carry):
        cut = rows(i * BLOCK, BLOCK)
        mixed_grad[:, cut] = nt(branch_all[rows(j * PIECE, PIECE), :], wo_all[cut, :]).astype(BF16)
        return carry

    lax.fori_loop(0, 4, unmix_term, 0)
    g_mixed[rows(j * PIECE, PIECE), :] = mixed_grad[:, rows(j * 128, 128)]

    def unmix(m, sender):
        return remote(
            mixed_grad.at[:, rows(m * 128, 128)], g_mixed.at[rows(sender * PIECE, PIECE), :],
            um_s.at[m], um_r.at[sender], dev(x, m // 2, z, m % 2),
        )

    def unmix_start(r, carry):
        unmix((j + r) % 8, j).start()
        return carry

    def unmix_wait(r, carry):
        m = (j + r) % 8
        unmix(m, m).wait_recv()
        unmix(m, j).wait_send()
        return carry

    lax.fori_loop(1, 8, unmix_start, 0)
    ag_start(branch_all, 3)
    gk_acc[...] = jnp.zeros_like(gk_acc)
    gv_acc[...] = jnp.zeros_like(gv_acc)

    def output_term(i, carry):
        rs_put(2, i, nn(active[rows(i * BLOCK, BLOCK), :], wdn[...]))
        return carry

    lax.fori_loop(0, 4, output_term, 0)
    first_sum(0)
    lax.fori_loop(1, 8, unmix_wait, 0)

    def along_y(n, r, recv=False):
        src = (sum_gu, sum_dn, sum_qkv)[n].at[(y + r) % 4]
        dst = (all_gu, all_dn, all_qkv)[n].at[place, c, (y + 4 - r) % 4 if recv else y]
        return remote(src, dst, ya_s.at[n, r], ya_r.at[n, r], dev(x, y + r, z, c))

    def share(n):
        total, every = ((sum_gu, all_gu), (sum_dn, all_dn), (sum_qkv, all_qkv))[n]
        if n == 0:
            total[:, :, :512] = second_sum(0)
            total[:, :, 512:] = second_sum(1)
        elif n == 1:
            total[...] = second_sum(2)
        else:
            total[:, :, :256] = second_sum(3)
            total[:, :, 256:] = second_sum(4)
        for r in (1, 3, 2):
            along_y(n, r).start()
        every[place, c, y] = total[y]

    arrays = (all_gu, all_dn, all_wo, all_qkv)

    def spot(n, r, c_):
        return arrays[n].at[((z + 4 - r % 4) % 4) * 2 + (xh + r // 4) % 2, c_]

    def gd(n, r, recv=False):
        ref = spot(n, r if recv else 0, c)
        return remote(ref, ref, gd_s.at[n, r], gd_r.at[n, r], dev(x + 2 * (r // 4), y, z + r % 4, c))

    def gp(n, r, recv=False):
        ref = spot(n, r, (1 - c) if recv else c)
        return remote(ref, ref, gp_s.at[n, r], gp_r.at[n, r], sibling)

    def pair(n, z_, c_):
        return arrays[n].at[pl.ds(((z_ + 4) % 4) * 2, 2), c_]

    def single(n, z_, h):
        return arrays[n].at[pl.ds(((z_ + 4) % 4) * 2 + h, 1), c]

    def ring(n, k, recv=False):
        if k == 0:
            ref, to = single(n, z, (1 - xh) if recv else xh), dev(x + 2, y, z, c)
        elif k == 1:
            ref, to = pair(n, z - 1 if recv else z, c), dev(x, y, z + 1, c)
        elif k == 2:
            ref, to = pair(n, z + 1 if recv else z, c), dev(x, y, z + 3, c)
        elif k == 3:
            ref, to = single(n, z - 2 if recv else z - 1, 0), dev(x, y, z + 1, c)
        elif k == 4:
            ref, to = single(n, z + 2 if recv else z + 1, 1), dev(x, y, z + 3, c)
        else:
            ref, to = pair(n, z + (k - 5), (1 - c) if recv else c), sibling
        return remote(ref, ref, rg_s.at[n, k], rg_r.at[n, k], to)

    def ring_one(n):
        for r in (1, 3, 2):
            along_y(n, r, True).wait_recv()
        ring(n, 0).start()

    def ring_two(n):
        ring(n, 0, True).wait_recv()
        for k in (1, 2, 5):
            ring(n, k).start()

    def ring_three(n):
        ring(n, 1, True).wait_recv()
        ring(n, 3).start()
        ring(n, 8).start()
        ring(n, 2, True).wait_recv()
        ring(n, 4).start()
        ring(n, 6).start()

    def ring_four(n):
        ring(n, 3, True).wait_recv()
        ring(n, 4, True).wait_recv()
        ring(n, 7).start()

    def ring_five(n):
        for k in (5, 6, 7, 8):
            ring(n, k, True).wait_recv()

    def spread_start(n):
        if n != 2:
            for r in (1, 3, 2):
                along_y(min(n, 2), r, True).wait_recv()
        for r in (2, 1, 3, 6, 5, 7, 4):
            gd(n, r).start()
        gp(n, 0).start()

    def spread_pass(n):
        for r in (1, 3, 2, 4, 5, 7, 6):
            gd(n, r, True).wait_recv()
            gp(n, r).start()

    def spread_finish(n):
        for r in range(8):
            gp(n, r, True).wait_recv()

    def unturn(value, cut):
        value = value.astype(BF16).astype(F32)
        return (value * cos_ref[cut, :] - half_turn(value) * sin_ref[cut, :]).astype(BF16)

    def attend_back(i):
        width = (i + 1) * BLOCK
        cut = slice(i * BLOCK, (i + 1) * BLOCK)
        grad_bf = g_mixed[cut, :]
        grad_t = grad_bf.astype(F32).T
        products = grad_t * mixed_t[:, cut]
        queries_t = []
        for h in range(2):
            lanes = slice(64 * h, 64 * h + 64)
            grad_h = grad_bf[:, lanes]
            delta = jnp.sum(products[lanes, :], axis=0, keepdims=True)
            probs = p_t[h, i, :width, :]
            gv_acc[h, :width, :] += nn(probs, grad_h)
            g_probs = nt(v_h[h, :width, :], grad_h)
            g_scores = (probs.astype(F32) * (g_probs - delta)).astype(BF16)
            gk_acc[h, :width, :] += nn(g_scores, q_h[h, cut, :])
            queries_t.append(nn(k_t[lanes, :width], g_scores))
        g_query = (jnp.concatenate(queries_t, axis=0) * 0.125).T
        g_qkv[cut, :128] = unturn(g_query, cut)

    def block_back(i):
        cut = slice(i * BLOCK, (i + 1) * BLOCK)
        attend_back(i)
        g_qkv[cut, 128:256] = unturn(jnp.concatenate([gk_acc[0, cut, :], gk_acc[1, cut, :]], axis=1), cut)
        g_qkv[cut, 256:] = jnp.concatenate([gv_acc[0, cut, :], gv_acc[1, cut, :]], axis=1).astype(BF16)
        rs_put(3, i, nt(g_qkv[cut, :], wqkv[...]))

    block_back(3)
    ag_near(branch_all, 3)
    first_sum(1)
    first_sum(2)
    block_back(2)
    ag_pass(branch_all, 3)
    block_back(1)
    share(0)
    share(1)
    block_back(0)
    rs_far(3)
    lax.fori_loop(0, 4, grad_qkv, 0)
    rs_near(3, 0)
    rs_near(3, 1)
    first_start(3)
    first_start(4)
    ag_far(branch_all, 3)
    ring_one(0)
    ring_one(1)
    rs_mid(3)
    rs_far(2)
    ag_finish(branch_all, 3)
    grad_wo()
    first_start(5)
    first_sum(3)
    first_sum(4)
    ring_two(0)
    ring_two(1)

    grad = rs_finish(3)
    scale = rms_scale(x32)
    scaled = grad * gathered(0)
    back = scale * scaled - x32 * (scale * scale * scale) * jnp.mean(scaled * x32, axis=-1, keepdims=True)
    gain_one = jnp.sum(grad * x32 * scale, axis=0, keepdims=True)
    ig_send[...] = (g_hidden[...] + back).astype(BF16)
    swap_start(ig_send, in_grad, 3)

    vs[...] = jnp.zeros_like(vs)
    for i in range(8):
        vs[i, 0:1, :] = gain_one[:, 128 * i : 128 * i + 128]
        vs[i, 1:2, :] = gain_two[:, 128 * i : 128 * i + 128]
    bias_sum = jnp.sum(g_qkv[...].astype(F32), axis=0, keepdims=True)
    for i in range(3):
        vs[pl.ds(j, 1), 2 + i : 3 + i, :] = bias_sum[:, 128 * i : 128 * i + 128][None]

    def v1_copy(r):
        return remote(vs.at[(f + r) % 8], vr.at[r - 1], v1_ss.at[r - 1], v1_rs.at[r - 1], (s, (f + r) % 8))

    def v1_start(r, carry):
        v1_copy(r).start()
        return carry

    def v1_wait(r, carry):
        v1_copy(r).wait()
        return carry

    lax.fori_loop(1, 8, v1_start, 0)
    rs_near(2, 0)
    rs_near(2, 1)
    first_sum(5)
    share(2)
    lax.fori_loop(1, 8, v1_wait, 0)
    v2s[...] = jnp.sum(vr[...], axis=0) + vs[pl.ds(f, 1)][0]

    def v2_copy(r):
        to = dev(x + 2 * (r // 4), y, z + r % 4, c)
        return remote(v2s, v2r.at[r - 1], v2_ss.at[r - 1], v2_rs.at[r - 1], to)

    def v2_start(r, carry):
        v2_copy(r).start()
        return carry

    def v2_wait(r, carry):
        v2_copy(r).wait()
        return carry

    lax.fori_loop(1, 8, v2_start, 0)
    spread_start(3)
    wo_send[...] = second_sum(5)
    swap_start(wo_send, all_wo.at[place, (c + moves) % 2], 4)
    rs_mid(2)
    ring_three(0)
    ring_three(1)
    swap_wait(wo_send, all_wo.at[place, c], 4)
    spread_start(2)
    lax.fori_loop(1, 8, v2_wait, 0)
    v3s[...] = jnp.sum(v2r[...], axis=0) + v2s[...]
    v3_copy = remote(v3s, v3r, v3_ss.at[0], v3_rs.at[0], sibling)
    v3_copy.start()
    lo_send[...] = (hidden[...] + rs_finish(2)).astype(BF16)
    swap_start(lo_send, layer_out, 2)
    spread_pass(3)
    ring_four(0)
    ring_four(1)
    spread_pass(2)
    v3_copy.wait()
    vec_out[...] = v3s[...] + v3r[...]
    swap_wait(lo_send, layer_out, 2)
    swap_wait(ig_send, in_grad, 3)
    for n in (0, 1):
        ring_five(n)
    for n in (3, 2):
        spread_finish(n)

    for n in range(4):
        for r in (1, 2, 3):
            for p in range(PARTS[n]):
                w_y(n, p, r).wait_send()
            for dz in (1, 2, 3):
                w_z(n, r, dz).wait_send()
        for r in range(4):
            w_x(n, r).wait_send()
    for n in range(1, 8):
        wo_pass(n).wait_send()
    for k, buf in enumerate((normed_all, cot_all, mlp_all, branch_all)):
        for n in range(10):
            ag(buf, k, n).wait_send()
    for k in range(1, 4):
        if k > 1:
            for i in range(4):
                c_sib(k, i).wait_send()
        for n in (0, 1):
            c_far(k, n).wait_send()
            for h in (0, 1):
                c_fin(k, n, h).wait_send()
    for n in range(3):
        for r in (1, 2, 3):
            along_y(n, r).wait_send()
    for n in (0, 1):
        for k in range(9):
            ring(n, k).wait_send()
    for n in (2, 3):
        for r in range(8):
            if r > 0:
                gd(n, r).wait_send()
            gp(n, r).wait_send()


def fused_layer(*args):
    def vmem(*shape, dtype=BF16):
        return pltpu.VMEM(shape, dtype)

    def dma(*shape):
        return pltpu.SemaphoreType.DMA(shape)

    full = vmem(D, D)
    shares = ((4, 16, 512), (4, 16, 256), (4, 48, 128), (4, 16, 256), (4, 16, 128), (64, 128))
    scratch = [
        vmem(D, 128, dtype=F32), vmem(D, 128, dtype=F32), vmem(1, D, dtype=jnp.int32), vmem(8, 128, dtype=F32),
        vmem(PIECE, D), vmem(PIECE, D), vmem(PIECE, D, dtype=F32), vmem(PIECE, D, dtype=F32),
        full, vmem(D, FB), vmem(D, 2 * FB), vmem(FB, D), vmem(8, 8, 128, dtype=F32),
        full, full, full, full,
        vmem(2, D, 64), vmem(2, D, 64), vmem(2, D, 64), vmem(128, D), vmem(128, D),
        vmem(2, 4, D, BLOCK), vmem(128, D, dtype=F32), vmem(D, 128), vmem(PIECE, D), vmem(PIECE, D),
        vmem(D, FB, dtype=F32), vmem(D, FB), vmem(FB, D), vmem(D, 2 * FB), vmem(D, 128),
        vmem(2, D, 64, dtype=F32), vmem(2, D, 64, dtype=F32), vmem(D, FB),
        vmem(2, 4, BLOCK, D), vmem(4, 4, PIECE, D), vmem(4, PIECE, D), vmem(4, 2, 64, D), vmem(4, 2, PIECE, D), vmem(4, 2, PIECE, D),
        *(vmem(4, 4, *dims) for dims in shares),
        *(vmem(3, 4, *dims) for dims in shares),
        *(vmem(4, *dims) for dims in shares),
        *(vmem(3, *dims) for dims in shares),
        vmem(64, 128), vmem(4, 16, 2 * FB), vmem(4, 48, 128), vmem(4, 16, FB),
        vmem(PIECE, D), vmem(PIECE, D),
        vmem(8, 8, 128, dtype=F32), vmem(7, 8, 128, dtype=F32), vmem(8, 128, dtype=F32), vmem(7, 8, 128, dtype=F32),
        vmem(8, 128, dtype=F32), vmem(8, 128, dtype=F32),
        dma(9), dma(5), dma(5), dma(8), dma(8), dma(4, 3, 4), dma(4, 3, 4), dma(4, 4, 4), dma(4, 4, 4), dma(4, 4), dma(4, 4),
        dma(8), dma(8), dma(8), dma(8), dma(8), dma(8), dma(4, 10), dma(4, 10),
        dma(4, 4), dma(4, 4), dma(4, 2), dma(4, 2), dma(4, 2, 2), dma(4, 2, 2),
        dma(6, 4), dma(6, 4), dma(6, 4), dma(6, 4), dma(3, 4), dma(3, 4), dma(2, 9), dma(2, 9), dma(4, 8), dma(4, 8), dma(4, 8), dma(4, 8),
        dma(7), dma(7), dma(7), dma(7), dma(1), dma(1),
    ]
    anywhere = pl.BlockSpec(memory_space=pl.ANY)
    inside = pl.BlockSpec(memory_space=pltpu.VMEM)

    def out(*shape, dtype=BF16):
        return jax.ShapeDtypeStruct(shape, dtype)

    return pl.pallas_call(
        layer_kernel,
        out_shape=(
            out(PIECE, D), out(PIECE, D), out(8, 2, 4, 16, 2 * FB), out(8, 2, 4, 48, 128), out(8, 2, 64, 128),
            out(8, 2, 4, 16, FB), out(8, 128, dtype=F32),
        ),
        in_specs=[anywhere] * 11 + [inside] * 6,
        out_specs=[inside] * 7,
        scratch_shapes=scratch,
        compiler_params=pltpu.CompilerParams(
            collective_id=0, has_side_effects=True, vmem_limit_bytes=63 * 1024 * 1024
        ),
        name="layer",
    )(*args)


def spread_kernel(
    lo_in, ig_in, gu_in, dn_in, wo_in, qkv_in, vec_in,
    lo, ig, d_gain_a, d_q, d_k, d_v, d_bq, d_bk, d_bv, d_o, d_gain_m, d_gate, d_up, d_down,
    lo_v, ig_v, gu, dn, wo, qkv, vec, sems,
):
    loads = [
        pltpu.make_async_copy(src, dst, sems.at[i])
        for i, (src, dst) in enumerate(
            ((vec_in, vec), (qkv_in, qkv), (wo_in, wo), (gu_in, gu), (dn_in, dn), (ig_in, ig_v), (lo_in, lo_v))
        )
    ]
    for load in loads:
        load.start()
    loads[0].wait()
    for ref, row in ((d_gain_a, 0), (d_gain_m, 1), (d_bq, 2), (d_bk, 3), (d_bv, 4)):
        ref[...] = vec[row : row + 1, :]
    loads[1].wait()
    for t in range(8):
        cut = slice(16 * t, 16 * t + 16)
        for m in range(8):
            for i, ref in enumerate((d_q, d_k, d_v)):
                ref[cut, 128 * m : 128 * m + 128] = qkv[t, m % 2, m // 2, :, 128 * i : 128 * i + 128].astype(F32)
    loads[2].wait()
    flip = lax.axis_index("fsdp") % 2
    for t in range(8):
        for core in range(2):
            to = pl.ds(pl.multiple_of(64 * ((core + flip) % 2), 64), 64)
            d_o[to, 128 * t : 128 * t + 128] = wo[t, core].astype(F32)
    loads[3].wait()
    loads[4].wait()
    for m in range(8):
        first = 128 if m == 7 else 0
        count = 256 if m >= 6 else FB
        start = min(m, 6) * FB + (256 if m == 7 else 0)
        for t in range(8):
            cut = slice(16 * t, 16 * t + 16)
            d_gate[cut, start : start + count] = gu[t, m % 2, m // 2, :, first : first + count].astype(F32)
            d_up[cut, start : start + count] = gu[t, m % 2, m // 2, :, FB + first : FB + first + count].astype(F32)
            low, high = max(48 * t, first), min(48 * t + 48, first + count)
            if low < high:
                d_down[start + low - first : start + high - first, :] = dn[
                    t, m % 2, m // 2, low - 48 * t : high - 48 * t, :
                ].astype(F32)
    loads[5].wait()
    ig[...] = ig_v[...].astype(F32)
    loads[6].wait()
    lo[...] = lo_v[...]


def spread(*args):
    def out(*shape, dtype=F32):
        return jax.ShapeDtypeStruct(shape, dtype)

    inside = pl.BlockSpec(memory_space=pltpu.VMEM)
    vec, square, wide = out(1, 128), out(128, D), out(128, 2816)
    return pl.pallas_call(
        spread_kernel,
        out_shape=(
            out(PIECE, D, dtype=BF16), out(PIECE, D), vec, square, square, square, vec, vec, vec,
            square, vec, wide, wide, out(2816, 128),
        ),
        in_specs=[pl.BlockSpec(memory_space=pl.ANY)] * 7,
        out_specs=[inside] * 14,
        scratch_shapes=[pltpu.VMEM(a.shape, a.dtype) for a in args] + [pltpu.SemaphoreType.DMA((7,))],
        compiler_params=pltpu.CompilerParams(vmem_limit_bytes=60 * 1024 * 1024),
        name="spread",
    )(*args)


def rotary_tables():
    exponent = np.arange(HEAD_DIM // 2, dtype=np.float32) * np.float32(2.0 / HEAD_DIM)
    inverse = np.exp(np.float32(-math.log(THETA)) * exponent)
    angles = np.arange(D, dtype=np.float32)[:, None] * inverse
    cos, sin = np.cos(angles), np.sin(angles)
    return np.concatenate([cos] * 4, axis=1), np.concatenate([-sin, sin] * 2, axis=1)


def per_device(
    inputs, doc_ids, positions, attn_gain, query_weight, key_weight, value_weight,
    query_bias, key_bias, value_bias, out_weight, mlp_gain, gate_weight, up_weight,
    down_weight, cotangent,
):
    del positions
    cos, sin = rotary_tables()
    vectors = [v.reshape(1, 128) for v in (attn_gain, mlp_gain, query_bias, key_bias, value_bias)]
    blocks = fused_layer(
        inputs.reshape(PIECE, D), cotangent.reshape(PIECE, D),
        query_weight, key_weight, value_weight, out_weight, gate_weight, up_weight, down_weight,
        jnp.asarray(cos), jnp.asarray(sin), *vectors, doc_ids,
    )
    outs = list(spread(*blocks))
    outs[0] = outs[0].reshape(inputs.shape)
    outs[1] = outs[1].reshape(inputs.shape)
    return tuple(o.reshape(128) if o.shape == (1, 128) else o for o in outs)


def solution(mesh):
    rows_spec = P("fsdp", None)
    act = P("seq", "fsdp", None)
    vec = P("fsdp")
    return jax.shard_map(
        per_device,
        mesh=mesh,
        in_specs=(
            act, P(), P("seq", "fsdp"), vec, rows_spec, rows_spec, rows_spec, vec, vec, vec,
            rows_spec, vec, rows_spec, rows_spec, P(None, "fsdp"), act,
        ),
        out_specs=(
            act, act, vec, rows_spec, rows_spec, rows_spec, vec, vec, vec, rows_spec, vec,
            rows_spec, rows_spec, P(None, "fsdp"),
        ),
        check_vma=False,
    )
```

```python
import math

import jax
import jax.numpy as jnp
import numpy as np
from jax import lax
from jax.experimental import pallas as pl
from jax.experimental.pallas import tpu as pltpu
from jax.sharding import PartitionSpec as P

MESH = pl.DeviceIdType.MESH
HEAD_DIM = 64
EPS = 1e-06
THETA = 1000000.0
NEG = -1000000000.0
D = 1024
PIECE = 128
BLOCK = 256
FB = 384
F32 = jnp.float32
BF16 = jnp.bfloat16


def nn(a, b):
    return lax.dot_general(a, b, (((1,), (0,)), ((), ())), preferred_element_type=F32)


def nt(a, b):
    return lax.dot_general(a, b, (((1,), (1,)), ((), ())), preferred_element_type=F32)


def tn(a, b):
    return lax.dot_general(a, b, (((0,), (0,)), ((), ())), preferred_element_type=F32)


def rms_scale(value):
    return lax.rsqrt(jnp.mean(value * value, axis=-1, keepdims=True) + EPS)


def rows(start, size):
    return pl.ds(pl.multiple_of(start, size), size)


def half_turn(value):
    lane = lax.broadcasted_iota(jnp.int32, value.shape, 1)
    ahead = pltpu.roll(value, 96, 1)
    behind = pltpu.roll(value, 32, 1)
    return jnp.where(lane % 64 < 32, ahead, behind)


def layer_kernel(
    x_in, cot_in, wq_in, wk_in, wv_in, wo_in, wg_in, wu_in, wd_in, cos_in, sin_in,
    gain_a, gain_m, bias_q, bias_k, bias_v, docs,
    layer_out, in_grad, all_gu, all_dn, all_wo, all_qkv, vec_out,
    cos_ref, sin_ref, start_ref, vec_in,
    x_own, cot_own, hidden, g_hidden, wo_all, wqkv, wgu, wdn, vall,
    normed_all, cot_all, mlp_all, branch_all,
    q_h, k_h, v_h, k_t, v_t, p_t, mixed_t, mixed, mixed_own, mixed_grad,
    g_act, active, active_t, g_gu, g_mixed, gk_acc, gv_acc, g_qkv,
    part, sib, far_s, far_r, fin_s, fin_r,
    dga, dgb, ddn, dqa, dqb, dwo, ra, rb, rd, rqa, rqb, rw, ha, hb, hd, hqa, hqb, hw, sa, sb, sd, sqa, sqb, sw, wo_send, sum_gu, sum_dn, sum_qkv,
    lo_send, ig_send,
    vs, vr, v2s, v2r, v3s, v3r,
    sem_load, swap_s, swap_r, vec_s, vec_r, wy_s, wy_r, wz_s, wz_r, wx_s, wx_r, wp_s, wp_r, mx_s, mx_r, um_s, um_r, ag_s, ag_r,
    sib_ss, sib_rs, far_ss, far_rs, fin_ss, fin_rs,
    f1_s, f1_r, f2_s, f2_r, ya_s, ya_r, rg_s, rg_r, gd_s, gd_r, gp_s, gp_r, v1_ss, v1_rs, v2_ss, v2_rs, v3_ss, v3_rs,
):
    s = lax.axis_index("seq")
    f = lax.axis_index("fsdp")
    xh = s // 8
    z = (s % 8) // 2
    c = s % 2
    y = f // 2
    xl = f % 2
    x = xh * 2 + xl
    j = y * 2 + c
    place = z * 2 + xh

    def dev(x_, y_, z_, c_):
        x_, y_, z_ = (x_ + 4) % 4, (y_ + 4) % 4, (z_ + 4) % 4
        return ((x_ // 2) * 8 + z_ * 2 + c_, y_ * 2 + x_ % 2)

    sibling = dev(x, y, z, 1 - c)
    y_up = dev(x, y + 1, z, c)
    y_dn = dev(x, y + 3, z, c)
    moves = (c + xl) % 2
    partner = dev(xh * 2 + 1 - xl, y, z, 1 - c)
    x_to = dev(x + 1 + 2 * c, y, z, c)

    def window(m):
        return (3 * m - 2 * (m // 7)) * 128

    def remote(src, dst, ss, rs, to):
        return pltpu.make_async_remote_copy(
            src_ref=src, dst_ref=dst, send_sem=ss, recv_sem=rs, device_id=to, device_id_type=MESH
        )

    def at(start, size, unit):
        return pl.ds(pl.multiple_of(start, unit), size)

    own_rows = rows(f * 128, 128)
    own_win = at(window(j), FB, 128)
    loads = [
        pltpu.make_async_copy(wq_in.at[:, rows(j * 128, 128)], wqkv.at[own_rows, pl.ds(0, 128)], sem_load.at[0]),
        pltpu.make_async_copy(wk_in.at[:, rows(j * 128, 128)], wqkv.at[own_rows, pl.ds(128, 128)], sem_load.at[1]),
        pltpu.make_async_copy(wv_in.at[:, rows(j * 128, 128)], wqkv.at[own_rows, pl.ds(256, 128)], sem_load.at[2]),
        pltpu.make_async_copy(wo_in, wo_all.at[own_rows], sem_load.at[3]),
        pltpu.make_async_copy(wg_in.at[:, own_win], wgu.at[own_rows, pl.ds(0, FB)], sem_load.at[4]),
        pltpu.make_async_copy(wu_in.at[:, own_win], wgu.at[own_rows, pl.ds(FB, FB)], sem_load.at[5]),
        pltpu.make_async_copy(wd_in.at[own_win, :], wdn.at[:, own_rows], sem_load.at[6]),
        pltpu.make_async_copy(cos_in, cos_ref, sem_load.at[7]),
        pltpu.make_async_copy(sin_in, sin_ref, sem_load.at[8]),
    ]
    for load in loads:
        load.start()

    barrier = pltpu.get_barrier_semaphore()

    def greet(to):
        pl.semaphore_signal(barrier, inc=1, device_id=to, device_id_type=MESH)

    def greet_near(r, carry):
        greet(dev(x + r, y, z, c))
        greet(dev(x, y, z + r, c))
        greet(dev(x + 2, y, z + r, c))
        return carry

    def greet_fsdp(r, carry):
        greet((s, (f + r) % 8))
        return carry

    def greet_cross(r, carry):
        greet(dev(x, y + r, z, 1 - c))
        return carry

    lax.fori_loop(1, 4, greet_near, 0)
    lax.fori_loop(1, 8, greet_fsdp, 0)
    lax.fori_loop(0, 4, greet_cross, 0)

    @pl.when(moves == 1)
    def _():
        greet(partner)
        pl.semaphore_wait(barrier, 21)

    @pl.when(moves == 0)
    def _():
        pl.semaphore_wait(barrier, 20)

    def swap_start(src, dst, n):
        @pl.when(moves == 1)
        def _():
            remote(src, dst, swap_s.at[n], swap_r.at[n], partner).start()

        @pl.when(moves == 0)
        def _():
            pltpu.make_async_copy(src, dst, swap_r.at[n]).start()

    def swap_wait(src, dst, n):
        @pl.when(moves == 1)
        def _():
            remote(src, dst, swap_s.at[n], swap_r.at[n], partner).wait()

        @pl.when(moves == 0)
        def _():
            pltpu.make_async_copy(src, dst, swap_r.at[n]).wait()

    def vec_copy(r):
        return remote(vec_in, vall.at[f], vec_s.at[r], vec_r.at[r], (s, (f + r) % 8))

    def vec_start(r, carry):
        vec_copy(r).start()
        return carry

    def vec_wait(r, carry):
        vec_copy(r).wait()
        return carry

    vec_in[...] = jnp.zeros_like(vec_in)
    for i, ref in enumerate((gain_a, gain_m, bias_q, bias_k, bias_v)):
        vec_in[i : i + 1, :] = ref[...].astype(F32)
    lax.fori_loop(1, 8, vec_start, 0)
    swap_start(x_in, x_own, 0)
    vall[pl.ds(f, 1)] = vec_in[...][None]
    doc_row = docs[pl.ds(xh * 8 + z * 2 + xl, 1), :]
    start_ref[...] = jnp.where(doc_row == 1, jnp.sum(1 - doc_row, axis=1, keepdims=True), 0)

    PARTS = (3, 2, 1, 1)

    def shard(r):
        return ((y + 4 - r) % 4) * 2 + xl

    def w_quarter(n, f_, q, p=None):
        if n == 0:
            return wqkv.at[at(f_ * 128 + q * 32, 32, 32), slice(None) if p is None else pl.ds(p * 128, 128)]
        if n == 1:
            return wgu.at[at(f_ * 128 + q * 32, 32, 32), slice(None) if p is None else pl.ds(p * FB, FB)]
        if n == 2:
            return wdn.at[at(q * 96, 96, 32), rows(f_ * 128, 128)]
        return wo_all.at[at(f_ * 128 + c * 64 + q * 16, 16, 16)]

    def w_rows(n, f_):
        if n == 0:
            return wqkv.at[rows(f_ * 128, 128)]
        if n == 1:
            return wgu.at[rows(f_ * 128, 128)]
        if n == 2:
            return wdn.at[:, rows(f_ * 128, 128)]
        return wo_all.at[rows(f_ * 128 + c * 64, 64)]

    def w_y(n, p, r, recv=False):
        m = ((y + r) % 4) * 2 + c
        if n == 0:
            src = (wq_in, wk_in, wv_in)[p].at[at(z * 32, 32, 32), rows(m * 128, 128)]
        elif n == 1:
            src = (wg_in, wu_in)[p].at[at(z * 32, 32, 32), at(window(m), FB, 128)]
        elif n == 2:
            src = wd_in.at[at(window(m) + z * 96, 96, 32), :]
        else:
            src = wo_in.at[at(c * 64 + z * 16, 16, 16)]
        dst = w_quarter(n, shard(r) if recv else f, z, p)
        return remote(src, dst, wy_s.at[n, p, r], wy_r.at[n, p, r], dev(x, y + r, z, c))

    def w_z(n, r, dz, recv=False):
        src = w_quarter(n, shard(r), z)
        dst = w_quarter(n, shard(r), (z + 4 - dz) % 4) if recv else src
        return remote(src, dst, wz_s.at[n, r, dz], wz_r.at[n, r, dz], dev(x, y, z + dz, c))

    def w_x(n, r, recv=False):
        src = w_rows(n, shard(r))
        dst = w_rows(n, ((y + 4 - r) % 4) * 2 + 1 - xl) if recv else src
        return remote(src, dst, wx_s.at[n, r], wx_r.at[n, r], x_to)

    def w_ystart(n):
        for r in (1, 3, 2):
            for p in range(PARTS[n]):
                w_y(n, p, r).start()

    def w_own(n):
        for load in (loads[:3], loads[4:6], loads[6:7], loads[3:4])[n]:
            load.wait()
        w_x(n, 0).start()

    def w_zstart(n):
        for r in (1, 3, 2):
            for p in range(PARTS[n]):
                w_y(n, p, r, True).wait_recv()
            for dz in (1, 3, 2):
                w_z(n, r, dz).start()

    def w_xstart(n):
        for r in (1, 3, 2):
            for dz in (1, 3, 2):
                w_z(n, r, dz, True).wait_recv()
            w_x(n, r).start()
            if n == 3:
                wo_pass(2 * ((4 - r) % 4)).start()

    def w_finish(n):
        for r in range(4):
            w_x(n, r, True).wait_recv()

    def wo_pass(n, recv=False):
        f_ = ((y + n // 2) % 4) * 2 + (xl + n % 2) % 2
        ref = wo_all.at[rows(f_ * 128 + ((1 - c) if recv else c) * 64, 64)]
        return remote(ref, ref, wp_s.at[n], wp_r.at[n], sibling)

    def wo_pass_x():
        for r in range(4):
            w_x(3, r, True).wait_recv()
            wo_pass(2 * ((4 - r) % 4) + 1).start()

    def wo_pass_finish():
        for n in range(1, 8):
            wo_pass(n, True).wait_recv()

    for n in (0, 3, 2, 1):
        w_ystart(n)
    w_own(0)

    def piece(buf, y_, c_):
        return buf.at[rows((((y_ + 4) % 4) * 2 + c_) * PIECE, PIECE)]

    def half(buf, y_, c_, h):
        return buf.at[rows((((y_ + 4) % 4) * 2 + c_) * PIECE + h * 64, 64)]

    def ag(buf, k, n, recv=False):
        if n in (0, 8):
            h = 0 if n == 0 else 1
            ref, to = (half(buf, y - 1, c, h) if recv else half(buf, y, c, h)), y_up
        elif n in (1, 9):
            h = 1 if n == 1 else 0
            ref, to = (half(buf, y + 1, c, h) if recv else half(buf, y, c, h)), y_dn
        elif n == 2:
            ref, to = (piece(buf, y, 1 - c) if recv else piece(buf, y, c)), sibling
        elif n == 3:
            ref, to = (half(buf, y - 2, c, 0) if recv else half(buf, y - 1, c, 0)), y_up
        elif n == 4:
            ref, to = (piece(buf, y - 1, 1 - c) if recv else piece(buf, y - 1, c)), sibling
        elif n == 5:
            ref, to = (half(buf, y + 2, c, 1) if recv else half(buf, y + 1, c, 1)), y_dn
        elif n == 6:
            ref, to = (piece(buf, y + 1, 1 - c) if recv else piece(buf, y + 1, c)), sibling
        else:
            ref, to = (piece(buf, y + 2, 1 - c) if recv else piece(buf, y + 2, c)), sibling
        return remote(ref, ref, ag_s.at[k, n], ag_r.at[k, n], to)

    def ag_start(buf, k):
        for n in (0, 1, 2, 8, 9):
            ag(buf, k, n).start()

    def ag_near(buf, k):
        ag(buf, k, 0, True).wait_recv()
        ag(buf, k, 3).start()
        ag(buf, k, 1, True).wait_recv()
        ag(buf, k, 5).start()

    def ag_pass(buf, k):
        ag(buf, k, 8, True).wait_recv()
        ag(buf, k, 4).start()
        ag(buf, k, 9, True).wait_recv()
        ag(buf, k, 6).start()

    def ag_far(buf, k):
        ag(buf, k, 3, True).wait_recv()
        ag(buf, k, 5, True).wait_recv()
        ag(buf, k, 7).start()

    def ag_finish(buf, k):
        for n in (2, 4, 6, 7):
            ag(buf, k, n, True).wait_recv()

    def ag_run(buf, k, consume, after_pass=None, after_far=None):
        def step(i, carry):
            @pl.when(i == 0)
            def _():
                ag(buf, k, 2, True).wait_recv()

            @pl.when(i == 1)
            def _():
                ag_pass(buf, k)
                if after_pass is not None:
                    after_pass()
                ag(buf, k, 4, True).wait_recv()

            @pl.when(i == 2)
            def _():
                ag(buf, k, 6, True).wait_recv()
                ag_far(buf, k)

            @pl.when(i == 3)
            def _():
                if after_far is not None:
                    after_far()
                ag(buf, k, 7, True).wait_recv()

            consume((y + (3 * ((i * (i + 1)) // 2)) % 4) % 4)

            @pl.when(i == 0)
            def _():
                if k > 0:
                    ag_near(buf, k)

            return carry

        lax.fori_loop(0, 4, step, 0)

    def held(k):
        return part.at[1 if k == 2 else 0]

    def own_part(k, a):
        return held(k)[a, rows(c * PIECE, PIECE), :].astype(F32)

    def c_sib(k, a):
        src = held(k).at[a, rows((1 - c) * PIECE, PIECE)]
        return remote(src, sib.at[k, a], sib_ss.at[k, a], sib_rs.at[k, a], sibling)

    def c_far(k, n):
        return remote(far_s.at[k, pl.ds(64 * n, 64)], far_r.at[k, n], far_ss.at[k, n], far_rs.at[k, n], y_up if n == 0 else y_dn)

    def c_fin(k, n, h):
        cut = pl.ds(64 * h, 64)
        return remote(fin_s.at[k, n, cut], fin_r.at[k, n, cut], fin_ss.at[k, n, h], fin_rs.at[k, n, h], y_up if n == 0 else y_dn)

    def rs_put(k, a, value):
        if k == 3:
            c_sib(1, a).wait_send()
        held(k)[a] = value.astype(BF16)
        c_sib(k, a).start()

    def rs_pair(k, a):
        c_sib(k, a).wait_recv()
        return own_part(k, a) + sib[k, a].astype(F32)

    def rs_far(k):
        far_s[k] = rs_pair(k, (y + 2) % 4).astype(BF16)
        c_far(k, 0).start()
        c_far(k, 1).start()

    def rs_near(k, n):
        fin_s[k, n] = rs_pair(k, (y + 1 + 2 * n) % 4).astype(BF16)
        c_fin(k, n, 1 - n).start()

    def rs_mid(k):
        for n in (0, 1):
            c_far(k, n).wait_recv()
            cut = pl.ds(64 * n, 64)
            fin_s[k, n, cut] = (fin_s[k, n, cut].astype(F32) + far_r[k, n].astype(F32)).astype(BF16)
            c_fin(k, n, n).start()

    def rs_finish(k):
        total = rs_pair(k, y)
        for n in (0, 1):
            for h in (0, 1):
                c_fin(k, n, h).wait_recv()
        return total + fin_r[k, 0].astype(F32) + fin_r[k, 1].astype(F32)

    w_zstart(0)
    lax.fori_loop(1, 8, vec_wait, 0)

    def gathered(row):
        return jnp.concatenate([vall[i, row : row + 1, :] for i in range(8)], axis=1)

    swap_wait(x_in, x_own, 0)
    x32 = x_own[...].astype(F32)
    normed_all[rows(j * PIECE, PIECE), :] = (x32 * rms_scale(x32) * gathered(0)).astype(BF16)
    ag_start(normed_all, 0)
    w_xstart(0)
    swap_start(cot_in, cot_own, 1)
    w_zstart(3)
    w_own(3)
    w_zstart(2)
    w_own(2)
    w_zstart(1)
    w_own(1)
    ag_near(normed_all, 0)
    for load in loads[7:]:
        load.wait()
    w_finish(0)

    def project(yy):
        cut = rows(yy * BLOCK, BLOCK)
        lin = nn(normed_all[cut, :], wqkv[...])
        cos = cos_ref[cut, :]
        sin = sin_ref[cut, :]
        bias = vall[pl.ds(j, 1)][0]
        q_lin = lin[:, :128] + bias[2:3, :]
        k_lin = lin[:, 128:256] + bias[3:4, :]
        v_lin = lin[:, 256:] + bias[4:5, :]
        q = (q_lin * cos + half_turn(q_lin) * sin).astype(BF16) * 0.125
        k32 = k_lin * cos + half_turn(k_lin) * sin
        k = k32.astype(BF16)
        v = v_lin.astype(BF16)
        for h in range(2):
            lanes = slice(64 * h, 64 * h + 64)
            q_h[h, cut, :] = q[:, lanes]
            k_h[h, cut, :] = k[:, lanes]
            v_h[h, cut, :] = v[:, lanes]
        k_t[:, cut] = k32.T.astype(BF16)
        v_t[:, cut] = v_lin.T.astype(BF16)

    def cot_start():
        swap_wait(cot_in, cot_own, 1)
        cot_all[rows(j * PIECE, PIECE), :] = cot_own[...]
        ag_start(cot_all, 1)

    ag_run(normed_all, 0, project, lambda: w_xstart(3), cot_start)

    def attend(i):
        width = (i + 1) * BLOCK
        cut = slice(i * BLOCK, (i + 1) * BLOCK)
        key_at = lax.broadcasted_iota(jnp.int32, (width, BLOCK), 0)
        query_at = lax.broadcasted_iota(jnp.int32, (width, BLOCK), 1) + i * BLOCK
        allowed = (key_at >= start_ref[0:1, cut]) & (key_at <= query_at)
        for h in range(2):
            scores = nt(k_h[h, :width, :], q_h[h, cut, :])
            scores = jnp.where(allowed, scores, NEG)
            weights = jnp.exp(scores - jnp.max(scores, axis=0, keepdims=True))
            inverse = 1.0 / jnp.sum(weights, axis=0, keepdims=True)
            probs = (weights * inverse).astype(BF16)
            p_t[h, i, :width, :] = probs
            mixed_t[64 * h : 64 * h + 64, cut] = nn(v_t[64 * h : 64 * h + 64, :width], probs)
        mixed[cut, :] = mixed_t[:, cut].T.astype(BF16)
        for m in (2 * i, 2 * i + 1):
            mix_start(m)

    def mix(m, sender):
        return remote(
            mixed.at[rows(m * PIECE, PIECE), :], mixed_own.at[:, rows(sender * 128, 128)],
            mx_s.at[m], mx_r.at[sender], dev(x, m // 2, z, m % 2),
        )

    def mix_start(m):
        @pl.when(j != m)
        def _():
            mix(m, j).start()

        @pl.when(j == m)
        def _():
            mixed_own[:, rows(j * 128, 128)] = mixed[m * PIECE : (m + 1) * PIECE, :]

    def mix_wait(r, carry):
        m = (j + r) % 8
        mix(m, m).wait_recv()
        mix(m, j).wait_send()
        return carry

    w_xstart(2)
    attend(0)
    attend(1)
    w_xstart(1)
    ag_near(cot_all, 1)
    attend(2)
    wo_pass_x()
    attend(3)
    ag_pass(cot_all, 1)
    wo_pass_finish()
    lax.fori_loop(1, 8, mix_wait, 0)

    hidden[...] = x_own[...].astype(F32) + nn(mixed_own[...], wo_all[...])
    hid = hidden[...]
    mlp_all[rows(j * PIECE, PIECE), :] = (hid * rms_scale(hid) * gathered(1)).astype(BF16)
    ag_start(mlp_all, 2)
    ag_far(cot_all, 1)
    w_finish(2)
    ag_finish(cot_all, 1)

    def active_back(i, carry):
        cut = rows(i * BLOCK, BLOCK)
        g_act[cut, :] = nt(cot_all[cut, :], wdn[...])
        return carry

    lax.fori_loop(0, 4, active_back, 0)
    w_finish(1)

    unit = lax.broadcasted_iota(jnp.int32, (1, FB), 1)
    low_edge = 128 * (j // 7)
    high_edge = FB - 128 * ((j // 6) * (1 - j // 7))
    live = (unit >= low_edge) & (unit < high_edge)

    def feed(yy):
        cut = rows(yy * BLOCK, BLOCK)
        both = nn(mlp_all[cut, :], wgu[...])
        gate = both[:, :FB]
        up = both[:, FB:]
        sig = 1.0 / (1.0 + jnp.exp(-gate))
        silu = gate * sig
        back = jnp.where(live, g_act[cut, :], 0.0)
        act = jnp.where(live, silu * up, 0.0)
        active[cut, :] = act.astype(BF16)
        g_gu[cut, :FB] = (back * up * sig * (1.0 + gate * (1.0 - sig))).astype(BF16)
        g_gu[cut, FB:] = (back * silu).astype(BF16)
        rs_put(1, yy, nt(g_gu[cut, :], wgu[...]))

    ag_run(mlp_all, 2, feed)
    rs_far(1)

    terms = (dga, dgb, ddn, dqa, dqb, dwo)
    term_in = (ra, rb, rd, rqa, rqb, rw)
    halfway = (ha, hb, hd, hqa, hqb, hw)
    half_in = (sa, sb, sd, sqa, sqb, sw)

    def first(n, r):
        if n in (0, 3, 5):
            src, to = terms[n].at[(x + r) % 4], dev(x + r, y, z, c)
        else:
            src, to = terms[n].at[:, (z + r) % 4], dev(x, y, z + r, c)
        return remote(src, term_in[n].at[r - 1], f1_s.at[n, r], f1_r.at[n, r], to)

    def second(n, r):
        if n in (0, 3, 5):
            src, to = halfway[n].at[(z + r) % 4], dev(x, y, z + r, c)
        else:
            src, to = halfway[n].at[(x + r) % 4], dev(x + r, y, z, c)
        return remote(src, half_in[n].at[r - 1], f2_s.at[n, r], f2_r.at[n, r], to)

    def first_start(n):
        for r in (1, 3, 2):
            first(n, r).start()

    def first_sum(n):
        total = (terms[n][x] if n in (0, 3, 5) else terms[n][:, z]).astype(F32)
        for r in (1, 3, 2):
            first(n, r).wait()
            total = total + term_in[n][r - 1].astype(F32)
        halfway[n][...] = total.astype(BF16)
        for r in (1, 3, 2):
            second(n, r).start()

    def second_sum(n):
        total = halfway[n][z if n in (0, 3, 5) else x].astype(F32)
        for r in (1, 3, 2):
            second(n, r).wait()
            total = total + half_in[n][r - 1].astype(F32)
        return total.astype(BF16)

    def chunk(t, xl_):
        return (t % 2) * 2 + xl_, t // 2

    def grad_gu(i, carry):
        got = tn(mlp_all[:, rows(i * BLOCK, BLOCK)], g_gu[...]).astype(BF16)
        for xl_ in range(2):
            for t in range(8):
                x_, z_ = chunk(t, xl_)
                share = got[xl_ * 128 + t * 16 : xl_ * 128 + t * 16 + 16]
                dga[x_, z_, i] = share[:, :512]
                dgb[x_, z_, i] = share[:, 512:]
        return carry

    def grad_dn(i, carry):
        got = nn(active_t[...], cot_all[:, rows(i * BLOCK, BLOCK)]).astype(BF16)
        for xl_ in range(2):
            for t in range(8):
                x_, z_ = chunk(t, xl_)
                ddn[x_, z_, i] = got[t * 48 : t * 48 + 48, xl_ * 128 : xl_ * 128 + 128]
        return carry

    def grad_qkv(i, carry):
        got = tn(normed_all[:, rows(i * BLOCK, BLOCK)], g_qkv[...]).astype(BF16)
        for xl_ in range(2):
            for t in range(8):
                x_, z_ = chunk(t, xl_)
                share = got[xl_ * 128 + t * 16 : xl_ * 128 + t * 16 + 16]
                dqa[x_, z_, i] = share[:, :256]
                dqb[x_, z_, i] = share[:, 256:]
        return carry

    def grad_wo():
        got = tn(mixed[...], branch_all[...]).astype(BF16)
        for h in range(2):
            for t in range(8):
                x_, z_ = chunk(t, (h + c) % 2)
                dwo[pl.ds(x_, 1), z_] = got[h * 64 : h * 64 + 64, t * 128 : t * 128 + 128][None]

    lax.fori_loop(0, 4, grad_gu, 0)
    rs_near(1, 0)
    rs_near(1, 1)
    first_start(1)
    first_start(0)
    rs_mid(1)
    active_t[...] = active[...].T
    lax.fori_loop(0, 4, grad_dn, 0)
    first_start(2)

    grad = rs_finish(1)
    hid = hidden[...]
    scale = rms_scale(hid)
    scaled = grad * gathered(1)
    back = scale * scaled - hid * (scale * scale * scale) * jnp.mean(scaled * hid, axis=-1, keepdims=True)
    g_hidden[...] = cot_own[...].astype(F32) + back
    branch_all[rows(j * PIECE, PIECE), :] = g_hidden[...].astype(BF16)

    def unmix_term(i, carry):
        cut = rows(i * BLOCK, BLOCK)
        mixed_grad[:, cut] = nt(branch_all[rows(j * PIECE, PIECE), :], wo_all[cut, :]).astype(BF16)
        return carry

    lax.fori_loop(0, 4, unmix_term, 0)
    g_mixed[rows(j * PIECE, PIECE), :] = mixed_grad[:, rows(j * 128, 128)]

    def unmix(m, sender):
        return remote(
            mixed_grad.at[:, rows(m * 128, 128)], g_mixed.at[rows(sender * PIECE, PIECE), :],
            um_s.at[m], um_r.at[sender], dev(x, m // 2, z, m % 2),
        )

    def unmix_start(r, carry):
        unmix((j + r) % 8, j).start()
        return carry

    def unmix_wait(r, carry):
        m = (j + r) % 8
        unmix(m, m).wait_recv()
        unmix(m, j).wait_send()
        return carry

    lax.fori_loop(1, 8, unmix_start, 0)
    gain_two = jnp.sum(grad * hid * scale, axis=0, keepdims=True)
    gk_acc[...] = jnp.zeros_like(gk_acc)
    gv_acc[...] = jnp.zeros_like(gv_acc)

    def output_term(i, carry):
        rs_put(2, i, nn(active[rows(i * BLOCK, BLOCK), :], wdn[...]))
        return carry

    lax.fori_loop(0, 4, output_term, 0)
    first_sum(1)
    first_sum(0)
    lax.fori_loop(1, 8, unmix_wait, 0)
    ag_start(branch_all, 3)

    def along_y(n, r, recv=False):
        src = (sum_gu, sum_dn, sum_qkv)[n].at[(y + r) % 4]
        dst = (all_gu, all_dn, all_qkv)[n].at[place, c, (y + 4 - r) % 4 if recv else y]
        return remote(src, dst, ya_s.at[n, r], ya_r.at[n, r], dev(x, y + r, z, c))

    def share(n):
        total, every = ((sum_gu, all_gu), (sum_dn, all_dn), (sum_qkv, all_qkv))[n]
        if n == 0:
            total[:, :, :512] = second_sum(0)
            total[:, :, 512:] = second_sum(1)
        elif n == 1:
            total[...] = second_sum(2)
        else:
            total[:, :, :256] = second_sum(3)
            total[:, :, 256:] = second_sum(4)
        for r in (1, 3, 2):
            along_y(n, r).start()
        every[place, c, y] = total[y]

    arrays = (all_gu, all_dn, all_wo, all_qkv)

    def spot(n, r, c_):
        return arrays[n].at[((z + 4 - r % 4) % 4) * 2 + (xh + r // 4) % 2, c_]

    def gd(n, r, recv=False):
        ref = spot(n, r if recv else 4 * (r // 5), c)
        return remote(ref, ref, gd_s.at[n, r], gd_r.at[n, r], dev(x + 2 * (r == 4), y, z + r % 4, c))

    def gp(n, r, recv=False):
        ref = spot(n, r, (1 - c) if recv else c)
        return remote(ref, ref, gp_s.at[n, r], gp_r.at[n, r], sibling)

    def pair(n, z_, c_):
        return arrays[n].at[pl.ds(((z_ + 4) % 4) * 2, 2), c_]

    def single(n, z_, h):
        return arrays[n].at[pl.ds(((z_ + 4) % 4) * 2 + h, 1), c]

    def ring(n, k, recv=False):
        if k == 0:
            ref, to = single(n, z, (1 - xh) if recv else xh), dev(x + 2, y, z, c)
        elif k == 1:
            ref, to = pair(n, z - 1 if recv else z, c), dev(x, y, z + 1, c)
        elif k == 2:
            ref, to = pair(n, z + 1 if recv else z, c), dev(x, y, z + 3, c)
        elif k == 3:
            ref, to = single(n, z - 2 if recv else z - 1, 0), dev(x, y, z + 1, c)
        elif k == 4:
            ref, to = single(n, z + 2 if recv else z + 1, 1), dev(x, y, z + 3, c)
        else:
            ref, to = pair(n, z + (k - 5), (1 - c) if recv else c), sibling
        return remote(ref, ref, rg_s.at[n, k], rg_r.at[n, k], to)

    def ring_one(n):
        for r in (1, 3, 2):
            along_y(n, r, True).wait_recv()
        ring(n, 0).start()

    def ring_two(n):
        ring(n, 0, True).wait_recv()
        for k in (1, 2, 5):
            ring(n, k).start()

    def ring_three(n):
        ring(n, 1, True).wait_recv()
        ring(n, 3).start()
        ring(n, 8).start()
        ring(n, 2, True).wait_recv()
        ring(n, 4).start()
        ring(n, 6).start()

    def ring_four(n):
        ring(n, 3, True).wait_recv()
        ring(n, 4, True).wait_recv()
        ring(n, 7).start()

    def ring_five(n):
        for k in (5, 6, 7, 8):
            ring(n, k, True).wait_recv()

    def spread_start(n):
        if n != 2:
            for r in (1, 3, 2):
                along_y(min(n, 2), r, True).wait_recv()
        for r in (4, 2, 1, 3):
            gd(n, r).start()
        gp(n, 0).start()

    def spread_next(n):
        gd(n, 4, True).wait_recv()
        for r in (6, 5, 7):
            gd(n, r).start()
        gp(n, 4).start()

    def spread_pass(n):
        for r in (1, 3, 2, 5, 7, 6):
            gd(n, r, True).wait_recv()
            gp(n, r).start()

    def spread_finish(n):
        for r in range(8):
            gp(n, r, True).wait_recv()

    def unturn(value, cut):
        value = value.astype(BF16).astype(F32)
        return (value * cos_ref[cut, :] - half_turn(value) * sin_ref[cut, :]).astype(BF16)

    def attend_back(i):
        width = (i + 1) * BLOCK
        cut = slice(i * BLOCK, (i + 1) * BLOCK)
        grad_bf = g_mixed[cut, :]
        grad_t = grad_bf.astype(F32).T
        products = grad_t * mixed_t[:, cut]
        queries_t = []
        for h in range(2):
            lanes = slice(64 * h, 64 * h + 64)
            grad_h = grad_bf[:, lanes]
            delta = jnp.sum(products[lanes, :], axis=0, keepdims=True)
            probs = p_t[h, i, :width, :]
            gv_acc[h, :width, :] += nn(probs, grad_h)
            g_probs = nt(v_h[h, :width, :], grad_h)
            g_scores = (probs.astype(F32) * (g_probs - delta)).astype(BF16)
            gk_acc[h, :width, :] += nn(g_scores, q_h[h, cut, :])
            queries_t.append(nn(k_t[lanes, :width], g_scores))
        g_query = (jnp.concatenate(queries_t, axis=0) * 0.125).T
        g_qkv[cut, :128] = unturn(g_query, cut)

    def block_back(i):
        cut = slice(i * BLOCK, (i + 1) * BLOCK)
        attend_back(i)
        g_qkv[cut, 128:256] = unturn(jnp.concatenate([gk_acc[0, cut, :], gk_acc[1, cut, :]], axis=1), cut)
        g_qkv[cut, 256:] = jnp.concatenate([gv_acc[0, cut, :], gv_acc[1, cut, :]], axis=1).astype(BF16)
        rs_put(3, i, nt(g_qkv[cut, :], wqkv[...]))

    block_back(3)
    block_back(2)
    share(0)
    first_sum(2)
    ag_near(branch_all, 3)
    block_back(1)
    block_back(0)
    rs_far(3)
    ag_pass(branch_all, 3)
    ring_one(0)
    share(1)
    lax.fori_loop(0, 4, grad_qkv, 0)
    first_start(4)
    first_start(3)
    rs_near(3, 0)
    rs_near(3, 1)
    ring_two(0)
    ring_one(1)
    ag_far(branch_all, 3)
    rs_mid(3)
    rs_far(2)
    ag_finish(branch_all, 3)
    grad_wo()
    first_start(5)
    rs_near(2, 0)
    rs_near(2, 1)
    first_sum(3)
    first_sum(4)
    ring_two(1)

    grad = rs_finish(3)
    scale = rms_scale(x32)
    scaled = grad * gathered(0)
    back = scale * scaled - x32 * (scale * scale * scale) * jnp.mean(scaled * x32, axis=-1, keepdims=True)
    ig_send[...] = (g_hidden[...] + back).astype(BF16)
    swap_start(ig_send, in_grad, 3)
    share(2)
    first_sum(5)

    gain_one = jnp.sum(grad * x32 * scale, axis=0, keepdims=True)
    vs[...] = jnp.zeros_like(vs)
    for i in range(8):
        vs[i, 0:1, :] = gain_one[:, 128 * i : 128 * i + 128]
        vs[i, 1:2, :] = gain_two[:, 128 * i : 128 * i + 128]
    bias_sum = jnp.sum(g_qkv[...].astype(F32), axis=0, keepdims=True)
    for i in range(3):
        vs[pl.ds(j, 1), 2 + i : 3 + i, :] = bias_sum[:, 128 * i : 128 * i + 128][None]

    def v1_copy(r):
        return remote(vs.at[(f + r) % 8], vr.at[r - 1], v1_ss.at[r - 1], v1_rs.at[r - 1], (s, (f + r) % 8))

    def v1_start(r, carry):
        v1_copy(r).start()
        return carry

    def v1_wait(r, carry):
        v1_copy(r).wait()
        return carry

    lax.fori_loop(1, 8, v1_start, 0)
    ring_three(0)
    spread_start(3)
    rs_mid(2)
    wo_send[...] = second_sum(5)
    swap_start(wo_send, all_wo.at[place, (c + moves) % 2], 4)
    lax.fori_loop(1, 8, v1_wait, 0)
    v2s[...] = jnp.sum(vr[...], axis=0) + vs[pl.ds(f, 1)][0]

    def v2_copy(r):
        to = dev(x + 2 * (r // 4), y, z + r % 4, c)
        return remote(v2s, v2r.at[r - 1], v2_ss.at[r - 1], v2_rs.at[r - 1], to)

    def v2_start(r, carry):
        v2_copy(r).start()
        return carry

    def v2_wait(r, carry):
        v2_copy(r).wait()
        return carry

    lax.fori_loop(1, 8, v2_start, 0)
    spread_next(3)
    swap_wait(wo_send, all_wo.at[place, c], 4)
    spread_start(2)
    ring_three(1)
    lo_send[...] = (hidden[...] + rs_finish(2)).astype(BF16)
    swap_start(lo_send, layer_out, 2)
    spread_next(2)
    lax.fori_loop(1, 8, v2_wait, 0)
    v3s[...] = jnp.sum(v2r[...], axis=0) + v2s[...]
    v3_copy = remote(v3s, v3r, v3_ss.at[0], v3_rs.at[0], sibling)
    v3_copy.start()
    spread_pass(3)
    ring_four(0)
    ring_four(1)
    spread_pass(2)
    v3_copy.wait()
    vec_out[...] = v3s[...] + v3r[...]
    swap_wait(lo_send, layer_out, 2)
    swap_wait(ig_send, in_grad, 3)
    for n in (0, 1):
        ring_five(n)
    for n in (3, 2):
        spread_finish(n)

    for n in range(4):
        for r in (1, 2, 3):
            for p in range(PARTS[n]):
                w_y(n, p, r).wait_send()
            for dz in (1, 2, 3):
                w_z(n, r, dz).wait_send()
        for r in range(4):
            w_x(n, r).wait_send()
    for n in range(1, 8):
        wo_pass(n).wait_send()
    for k, buf in enumerate((normed_all, cot_all, mlp_all, branch_all)):
        for n in range(10):
            ag(buf, k, n).wait_send()
    for k in range(1, 4):
        if k > 1:
            for i in range(4):
                c_sib(k, i).wait_send()
        for n in (0, 1):
            c_far(k, n).wait_send()
            for h in (0, 1):
                c_fin(k, n, h).wait_send()
    for n in range(3):
        for r in (1, 2, 3):
            along_y(n, r).wait_send()
    for n in (0, 1):
        for k in range(9):
            ring(n, k).wait_send()
    for n in (2, 3):
        for r in range(8):
            if r > 0:
                gd(n, r).wait_send()
            gp(n, r).wait_send()


def fused_layer(*args):
    def vmem(*shape, dtype=BF16):
        return pltpu.VMEM(shape, dtype)

    def dma(*shape):
        return pltpu.SemaphoreType.DMA(shape)

    full = vmem(D, D)
    shares = ((4, 16, 512), (4, 16, 256), (4, 48, 128), (4, 16, 256), (4, 16, 128), (64, 128))
    scratch = [
        vmem(D, 128, dtype=F32), vmem(D, 128, dtype=F32), vmem(1, D, dtype=jnp.int32), vmem(8, 128, dtype=F32),
        vmem(PIECE, D), vmem(PIECE, D), vmem(PIECE, D, dtype=F32), vmem(PIECE, D, dtype=F32),
        full, vmem(D, FB), vmem(D, 2 * FB), vmem(FB, D), vmem(8, 8, 128, dtype=F32),
        full, full, full, full,
        vmem(2, D, 64), vmem(2, D, 64), vmem(2, D, 64), vmem(128, D), vmem(128, D),
        vmem(2, 4, D, BLOCK), vmem(128, D, dtype=F32), vmem(D, 128), vmem(PIECE, D), vmem(PIECE, D),
        vmem(D, FB, dtype=F32), vmem(D, FB), vmem(FB, D), vmem(D, 2 * FB), vmem(D, 128),
        vmem(2, D, 64, dtype=F32), vmem(2, D, 64, dtype=F32), vmem(D, FB),
        vmem(2, 4, BLOCK, D), vmem(4, 4, PIECE, D), vmem(4, PIECE, D), vmem(4, 2, 64, D), vmem(4, 2, PIECE, D), vmem(4, 2, PIECE, D),
        *(vmem(4, 4, *dims) for dims in shares),
        *(vmem(3, 4, *dims) for dims in shares),
        *(vmem(4, *dims) for dims in shares),
        *(vmem(3, *dims) for dims in shares),
        vmem(64, 128), vmem(4, 16, 2 * FB), vmem(4, 48, 128), vmem(4, 16, FB),
        vmem(PIECE, D), vmem(PIECE, D),
        vmem(8, 8, 128, dtype=F32), vmem(7, 8, 128, dtype=F32), vmem(8, 128, dtype=F32), vmem(7, 8, 128, dtype=F32),
        vmem(8, 128, dtype=F32), vmem(8, 128, dtype=F32),
        dma(9), dma(5), dma(5), dma(8), dma(8), dma(4, 3, 4), dma(4, 3, 4), dma(4, 4, 4), dma(4, 4, 4), dma(4, 4), dma(4, 4),
        dma(8), dma(8), dma(8), dma(8), dma(8), dma(8), dma(4, 10), dma(4, 10),
        dma(4, 4), dma(4, 4), dma(4, 2), dma(4, 2), dma(4, 2, 2), dma(4, 2, 2),
        dma(6, 4), dma(6, 4), dma(6, 4), dma(6, 4), dma(3, 4), dma(3, 4), dma(2, 9), dma(2, 9), dma(4, 8), dma(4, 8), dma(4, 8), dma(4, 8),
        dma(7), dma(7), dma(7), dma(7), dma(1), dma(1),
    ]
    anywhere = pl.BlockSpec(memory_space=pl.ANY)
    inside = pl.BlockSpec(memory_space=pltpu.VMEM)

    def out(*shape, dtype=BF16):
        return pltpu.VMEM(shape, dtype)

    return pl.pallas_call(
        layer_kernel,
        out_shape=(
            out(PIECE, D), out(PIECE, D), out(8, 2, 4, 16, 2 * FB), out(8, 2, 4, 48, 128), out(8, 2, 64, 128),
            out(8, 2, 4, 16, FB), out(8, 128, dtype=F32),
        ),
        in_specs=[anywhere] * 11 + [inside] * 6,
        out_specs=[inside] * 7,
        scratch_shapes=scratch,
        compiler_params=pltpu.CompilerParams(
            collective_id=0, has_side_effects=True, vmem_limit_bytes=57 * 1024 * 1024
        ),
        name="layer",
    )(*args)


def spread_kernel(
    lo_in, ig_in, gu, dn, wo, qkv, vec,
    lo, ig, d_gain_a, d_q, d_k, d_v, d_bq, d_bk, d_bv, d_o, d_gain_m, d_gate, d_up, d_down,
    ig_v, q_v, k_v, v_v, o_v, gate_v, up_v, down_v, sems,
):
    stores = []

    def store(src, dst):
        copy = pltpu.make_async_copy(src, dst, sems.at[len(stores)])
        copy.start()
        stores.append(copy)

    for ref, row in ((d_gain_a, 0), (d_gain_m, 1), (d_bq, 2), (d_bk, 3), (d_bv, 4)):
        ref[...] = vec[row : row + 1, :]
    store(lo_in, lo)
    for m in range(8):
        first = 128 if m == 7 else 0
        count = 256 if m >= 6 else FB
        start = min(m, 6) * FB + (256 if m == 7 else 0)
        for t in range(8):
            low, high = max(48 * t, first), min(48 * t + 48, first + count)
            if low < high:
                down_v[start + low - first : start + high - first, :] = dn[
                    t, m % 2, m // 2, low - 48 * t : high - 48 * t, :
                ].astype(F32)
    store(down_v, d_down)
    for ref, off, dst in ((gate_v, 0, d_gate), (up_v, FB, d_up)):
        for m in range(8):
            first = 128 if m == 7 else 0
            count = 256 if m >= 6 else FB
            start = min(m, 6) * FB + (256 if m == 7 else 0)
            for t in range(8):
                cut = slice(16 * t, 16 * t + 16)
                ref[cut, start : start + count] = gu[t, m % 2, m // 2, :, off + first : off + first + count].astype(F32)
        store(ref, dst)
    for i, (ref, dst) in enumerate(((q_v, d_q), (k_v, d_k), (v_v, d_v))):
        for t in range(8):
            for m in range(8):
                ref[16 * t : 16 * t + 16, 128 * m : 128 * m + 128] = qkv[
                    t, m % 2, m // 2, :, 128 * i : 128 * i + 128
                ].astype(F32)
        store(ref, dst)
    flip = lax.axis_index("fsdp") % 2
    for t in range(8):
        for core in range(2):
            to = pl.ds(pl.multiple_of(64 * ((core + flip) % 2), 64), 64)
            o_v[to, 128 * t : 128 * t + 128] = wo[t, core].astype(F32)
    store(o_v, d_o)
    ig_v[...] = ig_in[...].astype(F32)
    store(ig_v, ig)
    for copy in stores:
        copy.wait()


def spread(*args):
    def out(*shape, dtype=F32):
        return jax.ShapeDtypeStruct(shape, dtype)

    inside = pl.BlockSpec(memory_space=pltpu.VMEM)
    anywhere = pl.BlockSpec(memory_space=pl.ANY)
    vec, square, wide, tall = out(1, 128), out(128, D), out(128, 2816), out(2816, 128)
    return pl.pallas_call(
        spread_kernel,
        out_shape=(
            out(PIECE, D, dtype=BF16), out(PIECE, D), vec, square, square, square, vec, vec, vec,
            square, vec, wide, wide, tall,
        ),
        in_specs=[inside] * 7,
        out_specs=[anywhere, anywhere, inside, anywhere, anywhere, anywhere, inside, inside, inside]
        + [anywhere, inside, anywhere, anywhere, anywhere],
        scratch_shapes=[pltpu.VMEM(o.shape, o.dtype) for o in (square,) * 5 + (wide, wide, tall)]
        + [pltpu.SemaphoreType.DMA((9,))],
        compiler_params=pltpu.CompilerParams(vmem_limit_bytes=24 * 1024 * 1024),
        name="spread",
    )(*args)


def rotary_tables():
    exponent = np.arange(HEAD_DIM // 2, dtype=np.float32) * np.float32(2.0 / HEAD_DIM)
    inverse = np.exp(np.float32(-math.log(THETA)) * exponent)
    angles = np.arange(D, dtype=np.float32)[:, None] * inverse
    cos, sin = np.cos(angles), np.sin(angles)
    return np.concatenate([cos] * 4, axis=1), np.concatenate([-sin, sin] * 2, axis=1)


def per_device(
    inputs, doc_ids, positions, attn_gain, query_weight, key_weight, value_weight,
    query_bias, key_bias, value_bias, out_weight, mlp_gain, gate_weight, up_weight,
    down_weight, cotangent,
):
    del positions
    cos, sin = rotary_tables()
    vectors = [v.reshape(1, 128) for v in (attn_gain, mlp_gain, query_bias, key_bias, value_bias)]
    blocks = fused_layer(
        inputs.reshape(PIECE, D), cotangent.reshape(PIECE, D),
        query_weight, key_weight, value_weight, out_weight, gate_weight, up_weight, down_weight,
        jnp.asarray(cos), jnp.asarray(sin), *vectors, doc_ids,
    )
    outs = list(spread(*blocks))
    outs[0] = outs[0].reshape(inputs.shape)
    outs[1] = outs[1].reshape(inputs.shape)
    return tuple(o.reshape(128) if o.shape == (1, 128) else o for o in outs)


def solution(mesh):
    rows_spec = P("fsdp", None)
    act = P("seq", "fsdp", None)
    vec = P("fsdp")
    return jax.shard_map(
        per_device,
        mesh=mesh,
        in_specs=(
            act, P(), P("seq", "fsdp"), vec, rows_spec, rows_spec, rows_spec, vec, vec, vec,
            rows_spec, vec, rows_spec, rows_spec, P(None, "fsdp"), act,
        ),
        out_specs=(
            act, act, vec, rows_spec, rows_spec, rows_spec, vec, vec, vec, rows_spec, vec,
            rows_spec, rows_spec, P(None, "fsdp"),
        ),
        check_vma=False,
    )
```

```python
import math

import jax
import jax.numpy as jnp
import numpy as np
from jax import lax
from jax.experimental import pallas as pl
from jax.experimental.pallas import tpu as pltpu
from jax.sharding import PartitionSpec as P

MESH = pl.DeviceIdType.MESH
HEAD_DIM = 64
EPS = 1e-06
THETA = 1000000.0
NEG = -1000000000.0
OTHER_DOC = -(2.0**30)
LOG2_E = math.log2(math.e)
D = 1024
PIECE = 128
BLOCK = 256
FB = 384
F32 = jnp.float32
BF16 = jnp.bfloat16


def nn(a, b):
    return lax.dot_general(a, b, (((1,), (0,)), ((), ())), preferred_element_type=F32)


def nt(a, b):
    return lax.dot_general(a, b, (((1,), (1,)), ((), ())), preferred_element_type=F32)


def tn(a, b):
    return lax.dot_general(a, b, (((0,), (0,)), ((), ())), preferred_element_type=F32)


def rms_scale(value):
    return lax.rsqrt(jnp.mean(value * value, axis=-1, keepdims=True) + EPS)


def rows(start, size):
    return pl.ds(pl.multiple_of(start, size), size)


def half_turn(value):
    lane = lax.broadcasted_iota(jnp.int32, value.shape, 1)
    ahead = pltpu.roll(value, 96, 1)
    behind = pltpu.roll(value, 32, 1)
    return jnp.where(lane % 64 < 32, ahead, behind)


def layer_kernel(
    x_in, cot_in, wq_in, wk_in, wv_in, wo_in, wg_in, wu_in, wd_in, cos_in, sin_in,
    gain_a, gain_m, bias_q, bias_k, bias_v, docs,
    layer_out, in_grad, all_gu, all_dn, all_wo, all_qkv, vec_out,
    cos_ref, sin_ref, vec_in,
    x_own, cot_own, hidden, g_hidden, wo_all, wqkv, wgu, wdn, vall,
    normed_all, cot_all, mlp_all, branch_all,
    q_two, k_all, v_all, k_t, v_t, p_t, inv, mixed_t, mixed, mixed_own, mixed_grad,
    g_act, active, active_t, g_gu, g_mixed, gk_acc, gv_acc, g_qkv,
    part, sib, far_s, far_r, fin_s, fin_r,
    dga, dgb, ddn, dqa, dqb, dwo, ra, rb, rd, rqa, rqb, rw, ha, hb, hd, hqa, hqb, hw, sa, sb, sd, sqa, sqb, sw, wo_send, sum_gu, sum_dn, sum_qkv,
    lo_send, ig_send,
    vs, vr, v2s, v2r, v3s, v3r,
    sem_load, swap_s, swap_r, vec_s, vec_r, wy_s, wy_r, wz_s, wz_r, wx_s, wx_r, wp_s, wp_r, mx_s, mx_r, um_s, um_r, ag_s, ag_r,
    sib_ss, sib_rs, far_ss, far_rs, fin_ss, fin_rs,
    f1_s, f1_r, f2_s, f2_r, ya_s, ya_r, rg_s, rg_r, gd_s, gd_r, gp_s, gp_r, v1_ss, v1_rs, v2_ss, v2_rs, v3_ss, v3_rs,
):
    s = lax.axis_index("seq")
    f = lax.axis_index("fsdp")
    xh = s // 8
    z = (s % 8) // 2
    c = s % 2
    y = f // 2
    xl = f % 2
    x = xh * 2 + xl
    j = y * 2 + c
    place = z * 2 + xh

    def dev(x_, y_, z_, c_):
        x_, y_, z_ = (x_ + 4) % 4, (y_ + 4) % 4, (z_ + 4) % 4
        return ((x_ // 2) * 8 + z_ * 2 + c_, y_ * 2 + x_ % 2)

    sibling = dev(x, y, z, 1 - c)
    y_up = dev(x, y + 1, z, c)
    y_dn = dev(x, y + 3, z, c)
    moves = (c + xl) % 2
    partner = dev(xh * 2 + 1 - xl, y, z, 1 - c)
    x_to = dev(x + 1 + 2 * c, y, z, c)

    def window(m):
        return (3 * m - 2 * (m // 7)) * 128

    def remote(src, dst, ss, rs, to):
        return pltpu.make_async_remote_copy(
            src_ref=src, dst_ref=dst, send_sem=ss, recv_sem=rs, device_id=to, device_id_type=MESH
        )

    def at(start, size, unit):
        return pl.ds(pl.multiple_of(start, unit), size)

    own_rows = rows(f * 128, 128)
    own_win = at(window(j), FB, 128)
    loads = [
        pltpu.make_async_copy(wq_in.at[:, rows(j * 128, 128)], wqkv.at[own_rows, pl.ds(0, 128)], sem_load.at[0]),
        pltpu.make_async_copy(wk_in.at[:, rows(j * 128, 128)], wqkv.at[own_rows, pl.ds(128, 128)], sem_load.at[1]),
        pltpu.make_async_copy(wv_in.at[:, rows(j * 128, 128)], wqkv.at[own_rows, pl.ds(256, 128)], sem_load.at[2]),
        pltpu.make_async_copy(wo_in, wo_all.at[own_rows], sem_load.at[3]),
        pltpu.make_async_copy(wg_in.at[:, own_win], wgu.at[own_rows, pl.ds(0, FB)], sem_load.at[4]),
        pltpu.make_async_copy(wu_in.at[:, own_win], wgu.at[own_rows, pl.ds(FB, FB)], sem_load.at[5]),
        pltpu.make_async_copy(wd_in.at[own_win, :], wdn.at[:, own_rows], sem_load.at[6]),
        pltpu.make_async_copy(cos_in, cos_ref, sem_load.at[7]),
        pltpu.make_async_copy(sin_in, sin_ref, sem_load.at[8]),
    ]
    for load in loads:
        load.start()

    barrier = pltpu.get_barrier_semaphore()

    def greet(to):
        pl.semaphore_signal(barrier, inc=1, device_id=to, device_id_type=MESH)

    def greet_near(r, carry):
        greet(dev(x + r, y, z, c))
        greet(dev(x, y, z + r, c))
        greet(dev(x + 2, y, z + r, c))
        return carry

    def greet_fsdp(r, carry):
        greet((s, (f + r) % 8))
        return carry

    def greet_cross(r, carry):
        greet(dev(x, y + r, z, 1 - c))
        return carry

    lax.fori_loop(1, 4, greet_near, 0)
    lax.fori_loop(1, 8, greet_fsdp, 0)
    lax.fori_loop(0, 4, greet_cross, 0)

    @pl.when(moves == 1)
    def _():
        greet(partner)
        pl.semaphore_wait(barrier, 21)

    @pl.when(moves == 0)
    def _():
        pl.semaphore_wait(barrier, 20)

    def swap_start(src, dst, n):
        @pl.when(moves == 1)
        def _():
            remote(src, dst, swap_s.at[n], swap_r.at[n], partner).start()

        @pl.when(moves == 0)
        def _():
            pltpu.make_async_copy(src, dst, swap_r.at[n]).start()

    def swap_wait(src, dst, n):
        @pl.when(moves == 1)
        def _():
            remote(src, dst, swap_s.at[n], swap_r.at[n], partner).wait()

        @pl.when(moves == 0)
        def _():
            pltpu.make_async_copy(src, dst, swap_r.at[n]).wait()

    def vec_copy(r):
        return remote(vec_in, vall.at[f], vec_s.at[r], vec_r.at[r], (s, (f + r) % 8))

    def vec_start(r, carry):
        vec_copy(r).start()
        return carry

    def vec_wait(r, carry):
        vec_copy(r).wait()
        return carry

    vec_in[...] = jnp.zeros_like(vec_in)
    for i, ref in enumerate((gain_a, gain_m, bias_q, bias_k, bias_v)):
        vec_in[i : i + 1, :] = ref[...].astype(F32)
    lax.fori_loop(1, 8, vec_start, 0)
    swap_start(x_in, x_own, 0)
    vall[pl.ds(f, 1)] = vec_in[...][None]
    doc_row = docs[pl.ds(xh * 8 + z * 2 + xl, 1), :]

    PARTS = (3, 2, 1, 1)

    def shard(r):
        return ((y + 4 - r) % 4) * 2 + xl

    def w_quarter(n, f_, q, p=None):
        if n == 0:
            return wqkv.at[at(f_ * 128 + q * 32, 32, 32), slice(None) if p is None else pl.ds(p * 128, 128)]
        if n == 1:
            return wgu.at[at(f_ * 128 + q * 32, 32, 32), slice(None) if p is None else pl.ds(p * FB, FB)]
        if n == 2:
            return wdn.at[at(q * 96, 96, 32), rows(f_ * 128, 128)]
        return wo_all.at[at(f_ * 128 + c * 64 + q * 16, 16, 16)]

    def w_rows(n, f_):
        if n == 0:
            return wqkv.at[rows(f_ * 128, 128)]
        if n == 1:
            return wgu.at[rows(f_ * 128, 128)]
        if n == 2:
            return wdn.at[:, rows(f_ * 128, 128)]
        return wo_all.at[rows(f_ * 128 + c * 64, 64)]

    def w_y(n, p, r, recv=False):
        m = ((y + r) % 4) * 2 + c
        if n == 0:
            src = (wq_in, wk_in, wv_in)[p].at[at(z * 32, 32, 32), rows(m * 128, 128)]
        elif n == 1:
            src = (wg_in, wu_in)[p].at[at(z * 32, 32, 32), at(window(m), FB, 128)]
        elif n == 2:
            src = wd_in.at[at(window(m) + z * 96, 96, 32), :]
        else:
            src = wo_in.at[at(c * 64 + z * 16, 16, 16)]
        dst = w_quarter(n, shard(r) if recv else f, z, p)
        return remote(src, dst, wy_s.at[n, p, r], wy_r.at[n, p, r], dev(x, y + r, z, c))

    def w_z(n, r, dz, recv=False):
        src = w_quarter(n, shard(r), z)
        dst = w_quarter(n, shard(r), (z + 4 - dz) % 4) if recv else src
        return remote(src, dst, wz_s.at[n, r, dz], wz_r.at[n, r, dz], dev(x, y, z + dz, c))

    def w_x(n, r, recv=False):
        src = w_rows(n, shard(r))
        dst = w_rows(n, ((y + 4 - r) % 4) * 2 + 1 - xl) if recv else src
        return remote(src, dst, wx_s.at[n, r], wx_r.at[n, r], x_to)

    def w_ystart(n):
        for r in (1, 3, 2):
            for p in range(PARTS[n]):
                w_y(n, p, r).start()

    def w_own(n):
        for load in (loads[:3], loads[4:6], loads[6:7], loads[3:4])[n]:
            load.wait()
        w_x(n, 0).start()

    def w_zstart(n):
        for r in (1, 3, 2):
            for p in range(PARTS[n]):
                w_y(n, p, r, True).wait_recv()
            for dz in (1, 3, 2):
                w_z(n, r, dz).start()

    def w_xstart(n):
        for r in (1, 3, 2):
            for dz in (1, 3, 2):
                w_z(n, r, dz, True).wait_recv()
            w_x(n, r).start()
            if n == 3:
                wo_pass(2 * ((4 - r) % 4)).start()

    def w_finish(n):
        for r in range(4):
            w_x(n, r, True).wait_recv()

    def wo_pass(n, recv=False):
        f_ = ((y + n // 2) % 4) * 2 + (xl + n % 2) % 2
        ref = wo_all.at[rows(f_ * 128 + ((1 - c) if recv else c) * 64, 64)]
        return remote(ref, ref, wp_s.at[n], wp_r.at[n], sibling)

    def wo_pass_x():
        for r in range(4):
            w_x(3, r, True).wait_recv()
            wo_pass(2 * ((4 - r) % 4) + 1).start()

    def wo_pass_finish():
        for n in range(1, 8):
            wo_pass(n, True).wait_recv()

    for n in (0, 3, 2, 1):
        w_ystart(n)
    w_own(0)

    def piece(buf, y_, c_):
        return buf.at[rows((((y_ + 4) % 4) * 2 + c_) * PIECE, PIECE)]

    def half(buf, y_, c_, h):
        return buf.at[rows((((y_ + 4) % 4) * 2 + c_) * PIECE + h * 64, 64)]

    def ag(buf, k, n, recv=False):
        if n in (0, 8):
            h = 0 if n == 0 else 1
            ref, to = (half(buf, y - 1, c, h) if recv else half(buf, y, c, h)), y_up
        elif n in (1, 9):
            h = 1 if n == 1 else 0
            ref, to = (half(buf, y + 1, c, h) if recv else half(buf, y, c, h)), y_dn
        elif n == 2:
            ref, to = (piece(buf, y, 1 - c) if recv else piece(buf, y, c)), sibling
        elif n == 3:
            ref, to = (half(buf, y - 2, c, 0) if recv else half(buf, y - 1, c, 0)), y_up
        elif n == 4:
            ref, to = (piece(buf, y - 1, 1 - c) if recv else piece(buf, y - 1, c)), sibling
        elif n == 5:
            ref, to = (half(buf, y + 2, c, 1) if recv else half(buf, y + 1, c, 1)), y_dn
        elif n == 6:
            ref, to = (piece(buf, y + 1, 1 - c) if recv else piece(buf, y + 1, c)), sibling
        else:
            ref, to = (piece(buf, y + 2, 1 - c) if recv else piece(buf, y + 2, c)), sibling
        return remote(ref, ref, ag_s.at[k, n], ag_r.at[k, n], to)

    def ag_start(buf, k):
        for n in (0, 1, 2, 8, 9):
            ag(buf, k, n).start()

    def ag_near(buf, k):
        ag(buf, k, 0, True).wait_recv()
        ag(buf, k, 3).start()
        ag(buf, k, 1, True).wait_recv()
        ag(buf, k, 5).start()

    def ag_pass(buf, k):
        ag(buf, k, 8, True).wait_recv()
        ag(buf, k, 4).start()
        ag(buf, k, 9, True).wait_recv()
        ag(buf, k, 6).start()

    def ag_far(buf, k):
        ag(buf, k, 3, True).wait_recv()
        ag(buf, k, 5, True).wait_recv()
        ag(buf, k, 7).start()

    def ag_finish(buf, k):
        for n in (2, 4, 6, 7):
            ag(buf, k, n, True).wait_recv()

    def ag_run(buf, k, consume, after_pass=None, after_far=None):
        def step(i, carry):
            @pl.when(i == 0)
            def _():
                ag(buf, k, 2, True).wait_recv()

            @pl.when(i == 1)
            def _():
                ag_pass(buf, k)
                if after_pass is not None:
                    after_pass()
                ag(buf, k, 4, True).wait_recv()

            @pl.when(i == 2)
            def _():
                ag(buf, k, 6, True).wait_recv()
                ag_far(buf, k)

            @pl.when(i == 3)
            def _():
                if after_far is not None:
                    after_far()
                ag(buf, k, 7, True).wait_recv()

            consume((y + (3 * ((i * (i + 1)) // 2)) % 4) % 4)

            @pl.when(i == 0)
            def _():
                if k > 0:
                    ag_near(buf, k)

            return carry

        lax.fori_loop(0, 4, step, 0)

    def held(k):
        return part.at[1 if k == 2 else 0]

    def own_part(k, a):
        return held(k)[a, rows(c * PIECE, PIECE), :].astype(F32)

    def c_sib(k, a):
        src = held(k).at[a, rows((1 - c) * PIECE, PIECE)]
        return remote(src, sib.at[k, a], sib_ss.at[k, a], sib_rs.at[k, a], sibling)

    def c_far(k, n):
        return remote(far_s.at[k, pl.ds(64 * n, 64)], far_r.at[k, n], far_ss.at[k, n], far_rs.at[k, n], y_up if n == 0 else y_dn)

    def c_fin(k, n, h):
        cut = pl.ds(64 * h, 64)
        return remote(fin_s.at[k, n, cut], fin_r.at[k, n, cut], fin_ss.at[k, n, h], fin_rs.at[k, n, h], y_up if n == 0 else y_dn)

    def rs_put(k, a, value):
        if k == 3:
            c_sib(1, a).wait_send()
        held(k)[a] = value.astype(BF16)
        c_sib(k, a).start()

    def rs_pair(k, a):
        c_sib(k, a).wait_recv()
        return own_part(k, a) + sib[k, a].astype(F32)

    def rs_far(k):
        far_s[k] = rs_pair(k, (y + 2) % 4).astype(BF16)
        c_far(k, 0).start()
        c_far(k, 1).start()

    def rs_near(k, n):
        fin_s[k, n] = rs_pair(k, (y + 1 + 2 * n) % 4).astype(BF16)
        c_fin(k, n, 1 - n).start()

    def rs_mid(k):
        for n in (0, 1):
            c_far(k, n).wait_recv()
            cut = pl.ds(64 * n, 64)
            fin_s[k, n, cut] = (fin_s[k, n, cut].astype(F32) + far_r[k, n].astype(F32)).astype(BF16)
            c_fin(k, n, n).start()

    def rs_finish(k):
        total = rs_pair(k, y)
        for n in (0, 1):
            for h in (0, 1):
                c_fin(k, n, h).wait_recv()
        return total + fin_r[k, 0].astype(F32) + fin_r[k, 1].astype(F32)

    w_zstart(0)
    lax.fori_loop(1, 8, vec_wait, 0)

    def gathered(row):
        return jnp.concatenate([vall[i, row : row + 1, :] for i in range(8)], axis=1)

    swap_wait(x_in, x_own, 0)
    x32 = x_own[...].astype(F32)
    normed_all[rows(j * PIECE, PIECE), :] = (x32 * rms_scale(x32) * gathered(0)).astype(BF16)
    ag_start(normed_all, 0)
    w_xstart(0)
    swap_start(cot_in, cot_own, 1)
    w_zstart(3)
    w_own(3)
    w_zstart(2)
    w_own(2)
    w_zstart(1)
    w_own(1)
    ag_near(normed_all, 0)
    for load in loads[7:]:
        load.wait()
    w_finish(0)

    doc = jnp.broadcast_to(doc_row, (8, D)).astype(F32).T[:, :1]
    feature = lax.broadcasted_iota(jnp.int32, (D, 128), 1)
    k_all[:, 128:] = jnp.where(
        feature == 0, OTHER_DOC * (1.0 - doc), jnp.where(feature == 1, OTHER_DOC * doc, 0.0)
    ).astype(BF16)
    q_more = jnp.where(feature == 0, doc, jnp.where(feature == 1, 1.0 - doc, 0.0)).astype(BF16)
    for i in range(4):
        for h in range(2):
            q_two[i, BLOCK * h : BLOCK * h + BLOCK, 128:] = q_more[BLOCK * i : BLOCK * i + BLOCK]

    def two_heads(value):
        first_head = lax.broadcasted_iota(jnp.int32, value.shape, 1) < HEAD_DIM
        return jnp.concatenate([jnp.where(first_head, value, 0.0), jnp.where(first_head, 0.0, value)], axis=0)

    def own_quarters(value):
        return jnp.concatenate([value[:HEAD_DIM, :BLOCK], value[HEAD_DIM:, BLOCK:]], axis=0)

    def project(yy):
        cut = rows(yy * BLOCK, BLOCK)
        lin = nn(normed_all[cut, :], wqkv[...])
        cos = cos_ref[cut, :]
        sin = sin_ref[cut, :]
        bias = vall[pl.ds(j, 1)][0]
        q_lin = lin[:, :128] + bias[2:3, :]
        k_lin = lin[:, 128:256] + bias[3:4, :]
        v_lin = lin[:, 256:] + bias[4:5, :]
        q = (q_lin * cos + half_turn(q_lin) * sin) * (0.125 * LOG2_E)
        k32 = k_lin * cos + half_turn(k_lin) * sin
        q_two[pl.ds(yy, 1), :, :128] = two_heads(q).astype(BF16)[None]
        k_all[cut, :128] = k32.astype(BF16)
        v_all[cut, :] = v_lin.astype(BF16)
        k_t[:, cut] = k32.T.astype(BF16)
        v_t[:, cut] = v_lin.T.astype(BF16)

    def cot_start():
        swap_wait(cot_in, cot_own, 1)
        cot_all[rows(j * PIECE, PIECE), :] = cot_own[...]
        ag_start(cot_all, 1)

    ag_run(normed_all, 0, project, lambda: w_xstart(3), cot_start)

    def attend(i):
        width = (i + 1) * BLOCK
        before = i * BLOCK
        cut = slice(before, width)
        scores = nt(k_all[:width, :], q_two[i])
        key_at = lax.broadcasted_iota(jnp.int32, (BLOCK, 2 * BLOCK), 0)
        query_at = lax.broadcasted_iota(jnp.int32, (BLOCK, 2 * BLOCK), 1) % BLOCK
        last = jnp.where(key_at <= query_at, scores[before:], NEG)
        top = jnp.max(last, axis=0, keepdims=True)
        if i > 0:
            top = jnp.maximum(top, jnp.max(scores[:before], axis=0, keepdims=True))
        weights = jnp.exp2(last - top)
        total = jnp.sum(weights, axis=0, keepdims=True)
        p_t[i, before:width, :] = weights.astype(BF16)
        if i > 0:
            weights = jnp.exp2(scores[:before] - top)
            total = total + jnp.sum(weights, axis=0, keepdims=True)
            p_t[i, :before, :] = weights.astype(BF16)
        inverse = 1.0 / total
        inv[i : i + 1, :] = inverse
        both = nn(v_t[:, :width], p_t[i, :width, :]) * inverse
        mixed_t[:, cut] = own_quarters(both)
        mixed[cut, :] = mixed_t[:, cut].T.astype(BF16)
        for m in (2 * i, 2 * i + 1):
            mix_start(m)

    def mix(m, sender):
        return remote(
            mixed.at[rows(m * PIECE, PIECE), :], mixed_own.at[:, rows(sender * 128, 128)],
            mx_s.at[m], mx_r.at[sender], dev(x, m // 2, z, m % 2),
        )

    def mix_start(m):
        @pl.when(j != m)
        def _():
            mix(m, j).start()

        @pl.when(j == m)
        def _():
            mixed_own[:, rows(j * 128, 128)] = mixed[m * PIECE : (m + 1) * PIECE, :]

    def mix_wait(r, carry):
        m = (j + r) % 8
        mix(m, m).wait_recv()
        mix(m, j).wait_send()
        return carry

    w_xstart(2)
    attend(0)
    attend(1)
    w_xstart(1)
    ag_near(cot_all, 1)
    attend(2)
    wo_pass_x()
    attend(3)
    ag_pass(cot_all, 1)
    wo_pass_finish()
    lax.fori_loop(1, 8, mix_wait, 0)

    hidden[...] = x_own[...].astype(F32) + nn(mixed_own[...], wo_all[...])
    hid = hidden[...]
    mlp_all[rows(j * PIECE, PIECE), :] = (hid * rms_scale(hid) * gathered(1)).astype(BF16)
    ag_start(mlp_all, 2)
    ag_far(cot_all, 1)
    w_finish(2)
    ag_finish(cot_all, 1)

    def active_back(i, carry):
        cut = rows(i * BLOCK, BLOCK)
        g_act[cut, :] = nt(cot_all[cut, :], wdn[...])
        return carry

    lax.fori_loop(0, 4, active_back, 0)
    w_finish(1)

    unit = lax.broadcasted_iota(jnp.int32, (1, FB), 1)
    low_edge = 128 * (j // 7)
    high_edge = FB - 128 * ((j // 6) * (1 - j // 7))
    live = (unit >= low_edge) & (unit < high_edge)

    def feed(yy):
        cut = rows(yy * BLOCK, BLOCK)
        both = nn(mlp_all[cut, :], wgu[...])
        gate = both[:, :FB]
        up = both[:, FB:]
        sig = 1.0 / (1.0 + jnp.exp(-gate))
        silu = gate * sig
        back = jnp.where(live, g_act[cut, :], 0.0)
        act = jnp.where(live, silu * up, 0.0)
        active[cut, :] = act.astype(BF16)
        g_gu[cut, :FB] = (back * up * sig * (1.0 + gate * (1.0 - sig))).astype(BF16)
        g_gu[cut, FB:] = (back * silu).astype(BF16)
        rs_put(1, yy, nt(g_gu[cut, :], wgu[...]))

    ag_run(mlp_all, 2, feed)
    rs_far(1)

    terms = (dga, dgb, ddn, dqa, dqb, dwo)
    term_in = (ra, rb, rd, rqa, rqb, rw)
    halfway = (ha, hb, hd, hqa, hqb, hw)
    half_in = (sa, sb, sd, sqa, sqb, sw)

    def first(n, r):
        if n in (0, 3, 5):
            src, to = terms[n].at[(x + r) % 4], dev(x + r, y, z, c)
        else:
            src, to = terms[n].at[:, (z + r) % 4], dev(x, y, z + r, c)
        return remote(src, term_in[n].at[r - 1], f1_s.at[n, r], f1_r.at[n, r], to)

    def second(n, r):
        if n in (0, 3, 5):
            src, to = halfway[n].at[(z + r) % 4], dev(x, y, z + r, c)
        else:
            src, to = halfway[n].at[(x + r) % 4], dev(x + r, y, z, c)
        return remote(src, half_in[n].at[r - 1], f2_s.at[n, r], f2_r.at[n, r], to)

    def first_start(n):
        for r in (1, 3, 2):
            first(n, r).start()

    def first_sum(n):
        total = (terms[n][x] if n in (0, 3, 5) else terms[n][:, z]).astype(F32)
        for r in (1, 3, 2):
            first(n, r).wait()
            total = total + term_in[n][r - 1].astype(F32)
        halfway[n][...] = total.astype(BF16)
        for r in (1, 3, 2):
            second(n, r).start()

    def second_sum(n):
        total = halfway[n][z if n in (0, 3, 5) else x].astype(F32)
        for r in (1, 3, 2):
            second(n, r).wait()
            total = total + half_in[n][r - 1].astype(F32)
        return total.astype(BF16)

    def chunk(t, xl_):
        return (t % 2) * 2 + xl_, t // 2

    def grad_gu(i, carry):
        got = tn(mlp_all[:, rows(i * BLOCK, BLOCK)], g_gu[...]).astype(BF16)
        for xl_ in range(2):
            for t in range(8):
                x_, z_ = chunk(t, xl_)
                share = got[xl_ * 128 + t * 16 : xl_ * 128 + t * 16 + 16]
                dga[x_, z_, i] = share[:, :512]
                dgb[x_, z_, i] = share[:, 512:]
        return carry

    def grad_dn(i, carry):
        got = nn(active_t[...], cot_all[:, rows(i * BLOCK, BLOCK)]).astype(BF16)
        for xl_ in range(2):
            for t in range(8):
                x_, z_ = chunk(t, xl_)
                ddn[x_, z_, i] = got[t * 48 : t * 48 + 48, xl_ * 128 : xl_ * 128 + 128]
        return carry

    def grad_qkv(part_ref, base):
        def go(i, carry):
            got = tn(normed_all[:, rows((base + i) * BLOCK, BLOCK)], g_qkv[...]).astype(BF16)
            for xl_ in range(2):
                for t in range(8):
                    x_, z_ = chunk(t, xl_)
                    part_ref[x_, z_, i] = got[xl_ * 128 + t * 16 : xl_ * 128 + t * 16 + 16]
            return carry

        lax.fori_loop(0, 2, go, 0)

    def grad_wo():
        got = tn(mixed[...], branch_all[...]).astype(BF16)
        for h in range(2):
            for t in range(8):
                x_, z_ = chunk(t, (h + c) % 2)
                dwo[pl.ds(x_, 1), z_] = got[h * 64 : h * 64 + 64, t * 128 : t * 128 + 128][None]

    lax.fori_loop(0, 4, grad_gu, 0)
    rs_near(1, 0)
    rs_near(1, 1)
    first_start(1)
    first_start(0)
    rs_mid(1)
    active_t[...] = active[...].T
    lax.fori_loop(0, 4, grad_dn, 0)
    first_start(2)

    grad = rs_finish(1)
    hid = hidden[...]
    scale = rms_scale(hid)
    scaled = grad * gathered(1)
    back = scale * scaled - hid * (scale * scale * scale) * jnp.mean(scaled * hid, axis=-1, keepdims=True)
    g_hidden[...] = cot_own[...].astype(F32) + back
    branch_all[rows(j * PIECE, PIECE), :] = g_hidden[...].astype(BF16)

    def unmix_term(i, carry):
        cut = rows(i * BLOCK, BLOCK)
        mixed_grad[:, cut] = nt(branch_all[rows(j * PIECE, PIECE), :], wo_all[cut, :]).astype(BF16)
        return carry

    lax.fori_loop(0, 4, unmix_term, 0)
    g_mixed[rows(j * PIECE, PIECE), :] = mixed_grad[:, rows(j * 128, 128)]

    def unmix(m, sender):
        return remote(
            mixed_grad.at[:, rows(m * 128, 128)], g_mixed.at[rows(sender * PIECE, PIECE), :],
            um_s.at[m], um_r.at[sender], dev(x, m // 2, z, m % 2),
        )

    def unmix_start(r, carry):
        unmix((j + r) % 8, j).start()
        return carry

    def unmix_wait(r, carry):
        m = (j + r) % 8
        unmix(m, m).wait_recv()
        unmix(m, j).wait_send()
        return carry

    lax.fori_loop(1, 8, unmix_start, 0)
    gain_two = jnp.sum(grad * hid * scale, axis=0, keepdims=True)
    gk_acc[...] = jnp.zeros_like(gk_acc)
    gv_acc[...] = jnp.zeros_like(gv_acc)

    def output_term(i, carry):
        rs_put(2, i, nn(active[rows(i * BLOCK, BLOCK), :], wdn[...]))
        return carry

    lax.fori_loop(0, 4, output_term, 0)
    first_sum(1)
    first_sum(0)
    lax.fori_loop(1, 8, unmix_wait, 0)
    ag_start(branch_all, 3)

    def along_y(n, r, recv=False):
        src = (sum_gu, sum_dn, sum_qkv)[n].at[(y + r) % 4]
        dst = (all_gu, all_dn, all_qkv)[n].at[place, c, (y + 4 - r) % 4 if recv else y]
        return remote(src, dst, ya_s.at[n, r], ya_r.at[n, r], dev(x, y + r, z, c))

    def share(n):
        total, every = ((sum_gu, all_gu), (sum_dn, all_dn), (sum_qkv, all_qkv))[n]
        if n == 0:
            total[:, :, :512] = second_sum(0)
            total[:, :, 512:] = second_sum(1)
        elif n == 1:
            total[...] = second_sum(2)
        else:
            total[:2] = second_sum(3)
            total[2:] = second_sum(4)
        for r in (1, 3, 2):
            along_y(n, r).start()
        every[place, c, y] = total[y]

    arrays = (all_gu, all_dn, all_wo, all_qkv)

    def spot(n, r, c_):
        return arrays[n].at[((z + 4 - r % 4) % 4) * 2 + (xh + r // 4) % 2, c_]

    def gd(n, r, recv=False):
        if n == 2:
            ref = spot(n, r if recv else 0, c)
            return remote(ref, ref, gd_s.at[n, r], gd_r.at[n, r], dev(x + 2 * (r // 4), y, z + r % 4, c))
        ref = spot(n, r if recv else 4 * (r // 5), c)
        return remote(ref, ref, gd_s.at[n, r], gd_r.at[n, r], dev(x + 2 * (r == 4), y, z + r % 4, c))

    def gp(n, r, recv=False):
        ref = spot(n, r, (1 - c) if recv else c)
        return remote(ref, ref, gp_s.at[n, r], gp_r.at[n, r], sibling)

    def pair(n, z_, c_):
        return arrays[n].at[pl.ds(((z_ + 4) % 4) * 2, 2), c_]

    def single(n, z_, h):
        return arrays[n].at[pl.ds(((z_ + 4) % 4) * 2 + h, 1), c]

    def ring(n, k, recv=False):
        if k == 0:
            ref, to = single(n, z, (1 - xh) if recv else xh), dev(x + 2, y, z, c)
        elif k == 1:
            ref, to = pair(n, z - 1 if recv else z, c), dev(x, y, z + 1, c)
        elif k == 2:
            ref, to = pair(n, z + 1 if recv else z, c), dev(x, y, z + 3, c)
        elif k == 3:
            ref, to = single(n, z - 2 if recv else z - 1, 0), dev(x, y, z + 1, c)
        elif k == 4:
            ref, to = single(n, z + 2 if recv else z + 1, 1), dev(x, y, z + 3, c)
        else:
            ref, to = pair(n, z + (k - 5), (1 - c) if recv else c), sibling
        return remote(ref, ref, rg_s.at[n, k], rg_r.at[n, k], to)

    def ring_one(n):
        for r in (1, 3, 2):
            along_y(n, r, True).wait_recv()
        ring(n, 0).start()

    def ring_two(n):
        ring(n, 0, True).wait_recv()
        for k in (1, 2, 5):
            ring(n, k).start()

    def ring_three(n):
        ring(n, 1, True).wait_recv()
        ring(n, 3).start()
        ring(n, 8).start()
        ring(n, 2, True).wait_recv()
        ring(n, 4).start()
        ring(n, 6).start()

    def ring_four(n):
        ring(n, 3, True).wait_recv()
        ring(n, 4, True).wait_recv()
        ring(n, 7).start()

    def ring_five(n):
        for k in (5, 6, 7, 8):
            ring(n, k, True).wait_recv()

    def spread_start(n):
        if n != 2:
            for r in (1, 3, 2):
                along_y(min(n, 2), r, True).wait_recv()
        for r in (6, 4, 5, 7, 2, 1, 3) if n == 2 else (4, 2, 1, 3):
            gd(n, r).start()
        gp(n, 0).start()

    def spread_next(n):
        gd(n, 4, True).wait_recv()
        for r in () if n == 2 else (6, 5, 7):
            gd(n, r).start()
        gp(n, 4).start()

    def spread_pass(n):
        for r in (1, 3, 2, 5, 7, 6):
            gd(n, r, True).wait_recv()
            gp(n, r).start()

    def spread_finish(n):
        for r in range(8):
            gp(n, r, True).wait_recv()

    def unturn(value, cut):
        value = value.astype(BF16).astype(F32)
        return (value * cos_ref[cut, :] - half_turn(value) * sin_ref[cut, :]).astype(BF16)

    def attend_back(i):
        width = (i + 1) * BLOCK
        cut = slice(i * BLOCK, width)
        inverse = inv[i : i + 1, :]
        grad_t = g_mixed[cut, :].astype(F32).T
        products = grad_t * mixed_t[:, cut]
        scaled = jnp.concatenate([grad_t[:HEAD_DIM] * inverse[:, :BLOCK], grad_t[HEAD_DIM:] * inverse[:, BLOCK:]], axis=0)
        delta = inverse * jnp.concatenate(
            [jnp.sum(products[:HEAD_DIM], axis=0, keepdims=True), jnp.sum(products[HEAD_DIM:], axis=0, keepdims=True)], axis=1
        )
        grad_two = two_heads(scaled.T).astype(BF16)
        weights = p_t[i, :width, :]
        gv_acc[:width, :] += nn(weights, grad_two)
        g_probs = nt(v_all[:width, :], grad_two)
        g_scores = (weights.astype(F32) * (g_probs - delta)).astype(BF16)
        gk_acc[:width, :] += nn(g_scores, q_two[i, :, :128])
        g_query = own_quarters(nn(k_t[:, :width], g_scores)) * 0.125
        g_qkv[cut, :128] = unturn(g_query.T, cut)

    def block_back(i):
        cut = slice(i * BLOCK, (i + 1) * BLOCK)
        attend_back(i)
        g_qkv[cut, 128:256] = unturn(gk_acc[cut, :] * (1.0 / LOG2_E), cut)
        g_qkv[cut, 256:] = gv_acc[cut, :].astype(BF16)
        rs_put(3, i, nt(g_qkv[cut, :], wqkv[...]))

    block_back(3)
    block_back(2)
    share(0)
    first_sum(2)
    ag_near(branch_all, 3)
    block_back(1)
    block_back(0)
    rs_far(3)
    ag_pass(branch_all, 3)
    ring_one(0)
    share(1)
    grad_qkv(dqb, 2)
    first_start(4)
    grad_qkv(dqa, 0)
    first_start(3)
    rs_near(3, 0)
    rs_near(3, 1)
    ring_two(0)
    ag_far(branch_all, 3)
    rs_mid(3)
    ring_one(1)
    first_sum(4)
    first_sum(3)
    rs_far(2)
    ag_finish(branch_all, 3)
    grad_wo()
    first_start(5)
    ring_two(1)
    rs_near(2, 0)
    rs_near(2, 1)

    grad = rs_finish(3)
    scale = rms_scale(x32)
    scaled = grad * gathered(0)
    back = scale * scaled - x32 * (scale * scale * scale) * jnp.mean(scaled * x32, axis=-1, keepdims=True)
    ig_send[...] = (g_hidden[...] + back).astype(BF16)
    swap_start(ig_send, in_grad, 3)
    share(2)
    first_sum(5)

    gain_one = jnp.sum(grad * x32 * scale, axis=0, keepdims=True)
    vs[...] = jnp.zeros_like(vs)
    for i in range(8):
        vs[i, 0:1, :] = gain_one[:, 128 * i : 128 * i + 128]
        vs[i, 1:2, :] = gain_two[:, 128 * i : 128 * i + 128]
    bias_sum = jnp.sum(g_qkv[...].astype(F32), axis=0, keepdims=True)
    for i in range(3):
        vs[pl.ds(j, 1), 2 + i : 3 + i, :] = bias_sum[:, 128 * i : 128 * i + 128][None]

    def v1_copy(r):
        return remote(vs.at[(f + r) % 8], vr.at[r - 1], v1_ss.at[r - 1], v1_rs.at[r - 1], (s, (f + r) % 8))

    def v1_start(r, carry):
        v1_copy(r).start()
        return carry

    def v1_wait(r, carry):
        v1_copy(r).wait()
        return carry

    lax.fori_loop(1, 8, v1_start, 0)
    ring_three(0)
    spread_start(3)
    ring_three(1)
    rs_mid(2)
    wo_send[...] = second_sum(5)
    swap_start(wo_send, all_wo.at[place, (c + moves) % 2], 4)
    lax.fori_loop(1, 8, v1_wait, 0)
    v2s[...] = jnp.sum(vr[...], axis=0) + vs[pl.ds(f, 1)][0]

    def v2_copy(r):
        to = dev(x + 2 * (r // 4), y, z + r % 4, c)
        return remote(v2s, v2r.at[r - 1], v2_ss.at[r - 1], v2_rs.at[r - 1], to)

    def v2_start(r, carry):
        v2_copy(r).start()
        return carry

    def v2_wait(r, carry):
        v2_copy(r).wait()
        return carry

    lax.fori_loop(1, 8, v2_start, 0)
    spread_next(3)
    swap_wait(wo_send, all_wo.at[place, c], 4)
    spread_start(2)
    lo_send[...] = (hidden[...] + rs_finish(2)).astype(BF16)
    swap_start(lo_send, layer_out, 2)
    lax.fori_loop(1, 8, v2_wait, 0)
    v3s[...] = jnp.sum(v2r[...], axis=0) + v2s[...]
    v3_copy = remote(v3s, v3r, v3_ss.at[0], v3_rs.at[0], sibling)
    v3_copy.start()
    ring_four(0)
    spread_pass(3)
    ring_four(1)
    spread_next(2)
    spread_pass(2)
    v3_copy.wait()
    vec_out[...] = v3s[...] + v3r[...]
    swap_wait(lo_send, layer_out, 2)
    swap_wait(ig_send, in_grad, 3)
    for n in (0, 1):
        ring_five(n)
    for n in (3, 2):
        spread_finish(n)

    for n in range(4):
        for r in (1, 2, 3):
            for p in range(PARTS[n]):
                w_y(n, p, r).wait_send()
            for dz in (1, 2, 3):
                w_z(n, r, dz).wait_send()
        for r in range(4):
            w_x(n, r).wait_send()
    for n in range(1, 8):
        wo_pass(n).wait_send()
    for k, buf in enumerate((normed_all, cot_all, mlp_all, branch_all)):
        for n in range(10):
            ag(buf, k, n).wait_send()
    for k in range(1, 4):
        if k > 1:
            for i in range(4):
                c_sib(k, i).wait_send()
        for n in (0, 1):
            c_far(k, n).wait_send()
            for h in (0, 1):
                c_fin(k, n, h).wait_send()
    for n in range(3):
        for r in (1, 2, 3):
            along_y(n, r).wait_send()
    for n in (0, 1):
        for k in range(9):
            ring(n, k).wait_send()
    for n in (2, 3):
        for r in range(8):
            if r > 0:
                gd(n, r).wait_send()
            gp(n, r).wait_send()


def fused_layer(*args):
    def vmem(*shape, dtype=BF16):
        return pltpu.VMEM(shape, dtype)

    def dma(*shape):
        return pltpu.SemaphoreType.DMA(shape)

    full = vmem(D, D)
    shares = ((4, 16, 512), (4, 16, 256), (4, 48, 128), (2, 16, FB), (2, 16, FB), (64, 128))
    scratch = [
        vmem(D, 128, dtype=F32), vmem(D, 128, dtype=F32), vmem(8, 128, dtype=F32),
        vmem(PIECE, D), vmem(PIECE, D), vmem(PIECE, D, dtype=F32), vmem(PIECE, D, dtype=F32),
        full, vmem(D, FB), vmem(D, 2 * FB), vmem(FB, D), vmem(8, 8, 128, dtype=F32),
        full, full, full, full,
        vmem(4, 2 * BLOCK, 256), vmem(D, 256), vmem(D, 128), vmem(128, D), vmem(128, D),
        vmem(4, D, 2 * BLOCK), vmem(8, 2 * BLOCK, dtype=F32), vmem(128, D, dtype=F32), vmem(D, 128), vmem(PIECE, D), vmem(PIECE, D),
        vmem(D, FB, dtype=F32), vmem(D, FB), vmem(FB, D), vmem(D, 2 * FB), vmem(D, 128),
        vmem(D, 128, dtype=F32), vmem(D, 128, dtype=F32), vmem(D, FB),
        vmem(2, 4, BLOCK, D), vmem(4, 4, PIECE, D), vmem(4, PIECE, D), vmem(4, 2, 64, D), vmem(4, 2, PIECE, D), vmem(4, 2, PIECE, D),
        *(vmem(4, 4, *dims) for dims in shares),
        *(vmem(3, 4, *dims) for dims in shares),
        *(vmem(4, *dims) for dims in shares),
        *(vmem(3, *dims) for dims in shares),
        vmem(64, 128), vmem(4, 16, 2 * FB), vmem(4, 48, 128), vmem(4, 16, FB),
        vmem(PIECE, D), vmem(PIECE, D),
        vmem(8, 8, 128, dtype=F32), vmem(7, 8, 128, dtype=F32), vmem(8, 128, dtype=F32), vmem(7, 8, 128, dtype=F32),
        vmem(8, 128, dtype=F32), vmem(8, 128, dtype=F32),
        dma(9), dma(5), dma(5), dma(8), dma(8), dma(4, 3, 4), dma(4, 3, 4), dma(4, 4, 4), dma(4, 4, 4), dma(4, 4), dma(4, 4),
        dma(8), dma(8), dma(8), dma(8), dma(8), dma(8), dma(4, 10), dma(4, 10),
        dma(4, 4), dma(4, 4), dma(4, 2), dma(4, 2), dma(4, 2, 2), dma(4, 2, 2),
        dma(6, 4), dma(6, 4), dma(6, 4), dma(6, 4), dma(3, 4), dma(3, 4), dma(2, 9), dma(2, 9), dma(4, 8), dma(4, 8), dma(4, 8), dma(4, 8),
        dma(7), dma(7), dma(7), dma(7), dma(1), dma(1),
    ]
    anywhere = pl.BlockSpec(memory_space=pl.ANY)
    inside = pl.BlockSpec(memory_space=pltpu.VMEM)

    def out(*shape, dtype=BF16):
        return pltpu.VMEM(shape, dtype)

    return pl.pallas_call(
        layer_kernel,
        out_shape=(
            out(PIECE, D), out(PIECE, D), out(8, 2, 4, 16, 2 * FB), out(8, 2, 4, 48, 128), out(8, 2, 64, 128),
            out(8, 2, 4, 16, FB), out(8, 128, dtype=F32),
        ),
        in_specs=[anywhere] * 11 + [inside] * 6,
        out_specs=[inside] * 7,
        scratch_shapes=scratch,
        compiler_params=pltpu.CompilerParams(
            collective_id=0, has_side_effects=True, vmem_limit_bytes=57 * 1024 * 1024
        ),
        name="layer",
    )(*args)


def spread_kernel(
    lo_in, ig_in, gu, dn, wo, qkv, vec,
    lo, ig, d_gain_a, d_q, d_k, d_v, d_bq, d_bk, d_bv, d_o, d_gain_m, d_gate, d_up, d_down,
    ig_v, q_v, k_v, v_v, o_v, gate_v, up_v, down_v, sems,
):
    stores = []

    def store(src, dst):
        copy = pltpu.make_async_copy(src, dst, sems.at[len(stores)])
        copy.start()
        stores.append(copy)

    for ref, row in ((d_gain_a, 0), (d_gain_m, 1), (d_bq, 2), (d_bk, 3), (d_bv, 4)):
        ref[...] = vec[row : row + 1, :]
    store(lo_in, lo)
    for m in range(8):
        first = 128 if m == 7 else 0
        count = 256 if m >= 6 else FB
        start = min(m, 6) * FB + (256 if m == 7 else 0)
        for t in range(8):
            low, high = max(48 * t, first), min(48 * t + 48, first + count)
            if low < high:
                down_v[start + low - first : start + high - first, :] = dn[
                    t, m % 2, m // 2, low - 48 * t : high - 48 * t, :
                ].astype(F32)
    store(down_v, d_down)
    for ref, off, dst in ((gate_v, 0, d_gate), (up_v, FB, d_up)):
        for m in range(8):
            first = 128 if m == 7 else 0
            count = 256 if m >= 6 else FB
            start = min(m, 6) * FB + (256 if m == 7 else 0)
            for t in range(8):
                cut = slice(16 * t, 16 * t + 16)
                ref[cut, start : start + count] = gu[t, m % 2, m // 2, :, off + first : off + first + count].astype(F32)
        store(ref, dst)
    for i, (ref, dst) in enumerate(((q_v, d_q), (k_v, d_k), (v_v, d_v))):
        for t in range(8):
            for m in range(8):
                ref[16 * t : 16 * t + 16, 128 * m : 128 * m + 128] = qkv[
                    t, m % 2, m // 2, :, 128 * i : 128 * i + 128
                ].astype(F32)
        store(ref, dst)
    flip = lax.axis_index("fsdp") % 2
    for t in range(8):
        for core in range(2):
            to = pl.ds(pl.multiple_of(64 * ((core + flip) % 2), 64), 64)
            o_v[to, 128 * t : 128 * t + 128] = wo[t, core].astype(F32)
    store(o_v, d_o)
    ig_v[...] = ig_in[...].astype(F32)
    store(ig_v, ig)
    for copy in stores:
        copy.wait()


def spread(*args):
    def out(*shape, dtype=F32):
        return jax.ShapeDtypeStruct(shape, dtype)

    inside = pl.BlockSpec(memory_space=pltpu.VMEM)
    anywhere = pl.BlockSpec(memory_space=pl.ANY)
    vec, square, wide, tall = out(1, 128), out(128, D), out(128, 2816), out(2816, 128)
    return pl.pallas_call(
        spread_kernel,
        out_shape=(
            out(PIECE, D, dtype=BF16), out(PIECE, D), vec, square, square, square, vec, vec, vec,
            square, vec, wide, wide, tall,
        ),
        in_specs=[inside] * 7,
        out_specs=[anywhere, anywhere, inside, anywhere, anywhere, anywhere, inside, inside, inside]
        + [anywhere, inside, anywhere, anywhere, anywhere],
        scratch_shapes=[pltpu.VMEM(o.shape, o.dtype) for o in (square,) * 5 + (wide, wide, tall)]
        + [pltpu.SemaphoreType.DMA((9,))],
        compiler_params=pltpu.CompilerParams(vmem_limit_bytes=24 * 1024 * 1024),
        name="spread",
    )(*args)


def rotary_tables():
    exponent = np.arange(HEAD_DIM // 2, dtype=np.float32) * np.float32(2.0 / HEAD_DIM)
    inverse = np.exp(np.float32(-math.log(THETA)) * exponent)
    angles = np.arange(D, dtype=np.float32)[:, None] * inverse
    cos, sin = np.cos(angles), np.sin(angles)
    return np.concatenate([cos] * 4, axis=1), np.concatenate([-sin, sin] * 2, axis=1)


def per_device(
    inputs, doc_ids, positions, attn_gain, query_weight, key_weight, value_weight,
    query_bias, key_bias, value_bias, out_weight, mlp_gain, gate_weight, up_weight,
    down_weight, cotangent,
):
    del positions
    cos, sin = rotary_tables()
    vectors = [v.reshape(1, 128) for v in (attn_gain, mlp_gain, query_bias, key_bias, value_bias)]
    blocks = fused_layer(
        inputs.reshape(PIECE, D), cotangent.reshape(PIECE, D),
        query_weight, key_weight, value_weight, out_weight, gate_weight, up_weight, down_weight,
        jnp.asarray(cos), jnp.asarray(sin), *vectors, doc_ids,
    )
    outs = list(spread(*blocks))
    outs[0] = outs[0].reshape(inputs.shape)
    outs[1] = outs[1].reshape(inputs.shape)
    return tuple(o.reshape(128) if o.shape == (1, 128) else o for o in outs)


def solution(mesh):
    rows_spec = P("fsdp", None)
    act = P("seq", "fsdp", None)
    vec = P("fsdp")
    return jax.shard_map(
        per_device,
        mesh=mesh,
        in_specs=(
            act, P(), P("seq", "fsdp"), vec, rows_spec, rows_spec, rows_spec, vec, vec, vec,
            rows_spec, vec, rows_spec, rows_spec, P(None, "fsdp"), act,
        ),
        out_specs=(
            act, act, vec, rows_spec, rows_spec, rows_spec, vec, vec, vec, rows_spec, vec,
            rows_spec, rows_spec, P(None, "fsdp"),
        ),
        check_vma=False,
    )
```

```python
import math

import jax
import jax.numpy as jnp
import numpy as np
from jax import lax
from jax.experimental import pallas as pl
from jax.experimental.pallas import tpu as pltpu
from jax.sharding import PartitionSpec as P

MESH = pl.DeviceIdType.MESH
HEAD_DIM = 64
EPS = 1e-06
THETA = 1000000.0
NEG = -1000000000.0
OTHER_DOC = -(2.0**30)
LOG2_E = math.log2(math.e)
D = 1024
PIECE = 128
BLOCK = 256
FB = 384
F32 = jnp.float32
BF16 = jnp.bfloat16


def nn(a, b):
    return lax.dot_general(a, b, (((1,), (0,)), ((), ())), preferred_element_type=F32)


def nt(a, b):
    return lax.dot_general(a, b, (((1,), (1,)), ((), ())), preferred_element_type=F32)


def tn(a, b):
    return lax.dot_general(a, b, (((0,), (0,)), ((), ())), preferred_element_type=F32)


def rms_scale(value):
    return lax.rsqrt(jnp.mean(value * value, axis=-1, keepdims=True) + EPS)


def rows(start, size):
    return pl.ds(pl.multiple_of(start, size), size)


def half_turn(value):
    lane = lax.broadcasted_iota(jnp.int32, value.shape, 1)
    ahead = pltpu.roll(value, 96, 1)
    behind = pltpu.roll(value, 32, 1)
    return jnp.where(lane % 64 < 32, ahead, behind)


def layer_kernel(
    x_in, cot_in, wq_in, wk_in, wv_in, wo_in, wg_in, wu_in, wd_in, cos_in, sin_in,
    gain_a, gain_m, bias_q, bias_k, bias_v, docs,
    layer_out, in_grad, all_gu, all_dn, all_wo, all_qkv, vec_out,
    cos_ref, sin_ref, vec_in,
    x_own, cot_own, hidden, g_hidden, wo_all, wqkv, wgu, wdn, vall,
    normed_all, cot_all, mlp_all, branch_all,
    q_two, k_all, v_all, k_t, v_t, p_t, inv, mixed_t, mixed, mixed_own, mixed_grad,
    g_act, active, active_t, g_gu, g_mixed, gk_acc, gv_acc, g_qkv,
    part, sib, far_s, far_r, fin_s, fin_r,
    dga, dgb, ddn, dqa, dqb, dwo, ra, rb, rd, rqa, rqb, rw, ha, hb, hd, hqa, hqb, hw, sa, sb, sd, sqa, sqb, sw, wo_send, sum_gu, sum_dn, sum_qkv,
    lo_send, ig_send,
    vs, vr, v2s, v2r, v3s, v3r,
    sem_load, swap_s, swap_r, vec_s, vec_r, wy_s, wy_r, wz_s, wz_r, wx_s, wx_r, wp_s, wp_r, mx_s, mx_r, um_s, um_r, ag_s, ag_r,
    sib_ss, sib_rs, far_ss, far_rs, fin_ss, fin_rs,
    f1_s, f1_r, f2_s, f2_r, ya_s, ya_r, rg_s, rg_r, gd_s, gd_r, gp_s, gp_r, v1_ss, v1_rs, v2_ss, v2_rs, v3_ss, v3_rs,
):
    s = lax.axis_index("seq")
    f = lax.axis_index("fsdp")
    xh = s // 8
    z = (s % 8) // 2
    c = s % 2
    y = f // 2
    xl = f % 2
    x = xh * 2 + xl
    j = y * 2 + c
    place = z * 2 + xh

    def dev(x_, y_, z_, c_):
        x_, y_, z_ = (x_ + 4) % 4, (y_ + 4) % 4, (z_ + 4) % 4
        return ((x_ // 2) * 8 + z_ * 2 + c_, y_ * 2 + x_ % 2)

    sibling = dev(x, y, z, 1 - c)
    y_up = dev(x, y + 1, z, c)
    y_dn = dev(x, y + 3, z, c)
    moves = (c + xl) % 2
    partner = dev(xh * 2 + 1 - xl, y, z, 1 - c)
    x_to = dev(x + 1 + 2 * c, y, z, c)

    def window(m):
        return (3 * m - 2 * (m // 7)) * 128

    def remote(src, dst, ss, rs, to):
        return pltpu.make_async_remote_copy(
            src_ref=src, dst_ref=dst, send_sem=ss, recv_sem=rs, device_id=to, device_id_type=MESH
        )

    def all_in(ref, sem):
        remote(ref, ref, sem, sem, sibling).wait_recv()

    def all_sent(ref, sem):
        remote(ref, ref, sem, sem, sibling).wait_send()

    def at(start, size, unit):
        return pl.ds(pl.multiple_of(start, unit), size)

    own_rows = rows(f * 128, 128)
    own_win = at(window(j), FB, 128)
    loads = [
        pltpu.make_async_copy(wq_in.at[:, rows(j * 128, 128)], wqkv.at[own_rows, pl.ds(0, 128)], sem_load.at[0]),
        pltpu.make_async_copy(wk_in.at[:, rows(j * 128, 128)], wqkv.at[own_rows, pl.ds(128, 128)], sem_load.at[0]),
        pltpu.make_async_copy(wv_in.at[:, rows(j * 128, 128)], wqkv.at[own_rows, pl.ds(256, 128)], sem_load.at[0]),
        pltpu.make_async_copy(wo_in, wo_all.at[own_rows], sem_load.at[1]),
        pltpu.make_async_copy(wg_in.at[:, own_win], wgu.at[own_rows, pl.ds(0, FB)], sem_load.at[2]),
        pltpu.make_async_copy(wu_in.at[:, own_win], wgu.at[own_rows, pl.ds(FB, FB)], sem_load.at[2]),
        pltpu.make_async_copy(wd_in.at[own_win, :], wdn.at[:, own_rows], sem_load.at[3]),
        pltpu.make_async_copy(cos_in, cos_ref, sem_load.at[4]),
        pltpu.make_async_copy(sin_in, sin_ref, sem_load.at[5]),
    ]
    for load in loads:
        load.start()

    barrier = pltpu.get_barrier_semaphore()

    def greet(to):
        pl.semaphore_signal(barrier, inc=1, device_id=to, device_id_type=MESH)

    def greet_near(r, carry):
        greet(dev(x + r, y, z, c))
        greet(dev(x, y, z + r, c))
        greet(dev(x + 2, y, z + r, c))
        return carry

    def greet_fsdp(r, carry):
        greet((s, (f + r) % 8))
        return carry

    def greet_cross(r, carry):
        greet(dev(x, y + r, z, 1 - c))
        return carry

    lax.fori_loop(1, 4, greet_near, 0)
    lax.fori_loop(1, 8, greet_fsdp, 0)
    lax.fori_loop(0, 4, greet_cross, 0)

    @pl.when(moves == 1)
    def _():
        greet(partner)
        pl.semaphore_wait(barrier, 21)

    @pl.when(moves == 0)
    def _():
        pl.semaphore_wait(barrier, 20)

    def swap_start(src, dst, n):
        @pl.when(moves == 1)
        def _():
            remote(src, dst, swap_s.at[n], swap_r.at[n], partner).start()

        @pl.when(moves == 0)
        def _():
            pltpu.make_async_copy(src, dst, swap_r.at[n]).start()

    def swap_wait(src, dst, n):
        @pl.when(moves == 1)
        def _():
            remote(src, dst, swap_s.at[n], swap_r.at[n], partner).wait()

        @pl.when(moves == 0)
        def _():
            pltpu.make_async_copy(src, dst, swap_r.at[n]).wait()

    def vec_copy(r):
        return remote(vec_in, vall.at[f], vec_s.at[0], vec_r.at[0], (s, (f + r) % 8))

    def vec_start(r, carry):
        vec_copy(r).start()
        return carry

    vec_in[...] = jnp.zeros_like(vec_in)
    for i, ref in enumerate((gain_a, gain_m, bias_q, bias_k, bias_v)):
        vec_in[i : i + 1, :] = ref[...].astype(F32)
    lax.fori_loop(1, 8, vec_start, 0)
    swap_start(x_in, x_own, 0)
    vall[pl.ds(f, 1)] = vec_in[...][None]
    doc_row = docs[pl.ds(xh * 8 + z * 2 + xl, 1), :]

    PARTS = (3, 2, 1, 1)

    def shard(r):
        return ((y + 4 - r) % 4) * 2 + xl

    def w_quarter(n, f_, q, p=None):
        if n == 0:
            return wqkv.at[at(f_ * 128 + q * 32, 32, 32), slice(None) if p is None else pl.ds(p * 128, 128)]
        if n == 1:
            return wgu.at[at(f_ * 128 + q * 32, 32, 32), slice(None) if p is None else pl.ds(p * FB, FB)]
        if n == 2:
            return wdn.at[at(q * 96, 96, 32), rows(f_ * 128, 128)]
        return wo_all.at[at(f_ * 128 + c * 64 + q * 16, 16, 16)]

    def w_rows(n, f_):
        if n == 0:
            return wqkv.at[rows(f_ * 128, 128)]
        if n == 1:
            return wgu.at[rows(f_ * 128, 128)]
        if n == 2:
            return wdn.at[:, rows(f_ * 128, 128)]
        return wo_all.at[rows(f_ * 128 + c * 64, 64)]

    def w_y(n, p, r, recv=False):
        m = ((y + r) % 4) * 2 + c
        if n == 0:
            src = (wq_in, wk_in, wv_in)[p].at[at(z * 32, 32, 32), rows(m * 128, 128)]
        elif n == 1:
            src = (wg_in, wu_in)[p].at[at(z * 32, 32, 32), at(window(m), FB, 128)]
        elif n == 2:
            src = wd_in.at[at(window(m) + z * 96, 96, 32), :]
        else:
            src = wo_in.at[at(c * 64 + z * 16, 16, 16)]
        dst = w_quarter(n, shard(r) if recv else f, z, p)
        return remote(src, dst, wy_s.at[n], wy_r.at[n, r - 1], dev(x, y + r, z, c))

    def w_z(n, r, dz, recv=False):
        src = w_quarter(n, shard(r), z)
        dst = w_quarter(n, shard(r), (z + 4 - dz) % 4) if recv else src
        return remote(src, dst, wz_s.at[n], wz_r.at[n, r - 1], dev(x, y, z + dz, c))

    def w_x(n, r, recv=False):
        src = w_rows(n, shard(r))
        dst = w_rows(n, ((y + 4 - r) % 4) * 2 + 1 - xl) if recv else src
        return remote(src, dst, wx_s.at[n], wx_r.at[n], x_to)

    def quarters(n, count):
        if n == 2:
            return wdn.at[pl.ds(0, 96 * count)] if count == 1 else wdn.at[pl.ds(0, 288), pl.ds(0, 128 * (count // 3))]
        return (wqkv, wgu, None, wo_all)[n].at[pl.ds(0, (32, 32, 0, 16)[n] * count)]

    def blocks(n, count):
        if n == 2:
            return wdn.at[:, pl.ds(0, 128 * count)]
        return (wqkv, wgu, None, wo_all)[n].at[pl.ds(0, (128, 128, 0, 64)[n] * count)]

    def w_ystart(n):
        for r in (1, 3, 2):
            for p in range(PARTS[n]):
                w_y(n, p, r).start()

    def w_own(n):
        own = wo_all.at[own_rows] if n == 3 else w_rows(n, f)
        pltpu.make_async_copy(own, own, sem_load.at[(0, 2, 3, 1)[n]]).wait()
        w_x(n, 0).start()

    def w_zstart(n):
        for r in (1, 3, 2):
            all_in(w_quarter(n, shard(r), z), wy_r.at[n, r - 1])
            for dz in (1, 3, 2):
                w_z(n, r, dz).start()

    def w_xstart(n):
        for r in (1, 3, 2):
            all_in(quarters(n, 3), wz_r.at[n, r - 1])
            w_x(n, r).start()
            if n == 3:
                wo_pass(2 * ((4 - r) % 4)).start()

    def w_finish(n):
        all_in(blocks(n, 4), wx_r.at[n])

    def wo_pass(n, recv=False):
        f_ = ((y + n // 2) % 4) * 2 + (xl + n % 2) % 2
        ref = wo_all.at[rows(f_ * 128 + ((1 - c) if recv else c) * 64, 64)]
        return remote(ref, ref, wp_s.at[0], wp_r.at[0], sibling)

    def wo_pass_x():
        all_in(blocks(3, 4), wx_r.at[3])
        for r in range(4):
            wo_pass(2 * ((4 - r) % 4) + 1).start()

    def wo_pass_finish():
        all_in(wo_all.at[pl.ds(0, 448)], wp_r.at[0])

    for n in (0, 3, 2, 1):
        w_ystart(n)
    w_own(0)

    def piece(buf, y_, c_):
        return buf.at[rows((((y_ + 4) % 4) * 2 + c_) * PIECE, PIECE)]

    def half(buf, y_, c_, h):
        return buf.at[rows((((y_ + 4) % 4) * 2 + c_) * PIECE + h * 64, 64)]

    def ag(buf, k, n, recv=False):
        if n in (0, 8):
            h = 0 if n == 0 else 1
            ref, to = (half(buf, y - 1, c, h) if recv else half(buf, y, c, h)), y_up
        elif n in (1, 9):
            h = 1 if n == 1 else 0
            ref, to = (half(buf, y + 1, c, h) if recv else half(buf, y, c, h)), y_dn
        elif n == 2:
            ref, to = (piece(buf, y, 1 - c) if recv else piece(buf, y, c)), sibling
        elif n == 3:
            ref, to = (half(buf, y - 2, c, 0) if recv else half(buf, y - 1, c, 0)), y_up
        elif n == 4:
            ref, to = (piece(buf, y - 1, 1 - c) if recv else piece(buf, y - 1, c)), sibling
        elif n == 5:
            ref, to = (half(buf, y + 2, c, 1) if recv else half(buf, y + 1, c, 1)), y_dn
        elif n == 6:
            ref, to = (piece(buf, y + 1, 1 - c) if recv else piece(buf, y + 1, c)), sibling
        else:
            ref, to = (piece(buf, y + 2, 1 - c) if recv else piece(buf, y + 2, c)), sibling
        return remote(ref, ref, ag_s.at[k], ag_r.at[k, (0, 0, 3, 2, 4, 2, 5, 6, 1, 1)[n]], to)

    def ag_start(buf, k):
        for n in (0, 1, 2, 8, 9):
            ag(buf, k, n).start()

    def ag_near(buf, k):
        all_in(buf.at[pl.ds(0, PIECE)], ag_r.at[k, 0])
        ag(buf, k, 3).start()
        ag(buf, k, 5).start()

    def ag_pass(buf, k):
        all_in(buf.at[pl.ds(0, PIECE)], ag_r.at[k, 1])
        ag(buf, k, 4).start()
        ag(buf, k, 6).start()

    def ag_far(buf, k):
        all_in(buf.at[pl.ds(0, PIECE)], ag_r.at[k, 2])
        ag(buf, k, 7).start()

    def ag_finish(buf, k):
        for n in (2, 4, 6, 7):
            ag(buf, k, n, True).wait_recv()

    def ag_run(buf, k, consume, after_pass=None, after_far=None):
        def step(i, carry):
            @pl.when(i == 0)
            def _():
                ag(buf, k, 2, True).wait_recv()

            @pl.when(i == 1)
            def _():
                ag_pass(buf, k)
                if after_pass is not None:
                    after_pass()
                ag(buf, k, 4, True).wait_recv()

            @pl.when(i == 2)
            def _():
                ag(buf, k, 6, True).wait_recv()
                ag_far(buf, k)

            @pl.when(i == 3)
            def _():
                if after_far is not None:
                    after_far()
                ag(buf, k, 7, True).wait_recv()

            consume((y + (3 * ((i * (i + 1)) // 2)) % 4) % 4)

            @pl.when(i == 0)
            def _():
                if k > 0:
                    ag_near(buf, k)

            return carry

        lax.fori_loop(0, 4, step, 0)

    def held(k):
        return part.at[1 if k == 2 else 0]

    def own_part(k, a):
        return held(k)[a, rows(c * PIECE, PIECE), :].astype(F32)

    def c_sib(k, a):
        src = held(k).at[a, rows((1 - c) * PIECE, PIECE)]
        return remote(src, sib.at[k, a], sib_ss.at[k], sib_rs.at[k, a], sibling)

    def c_far(k, n):
        return remote(far_s.at[k, pl.ds(64 * n, 64)], far_r.at[k, n], far_ss.at[k], far_rs.at[k], y_up if n == 0 else y_dn)

    def c_fin(k, n, h):
        cut = pl.ds(64 * h, 64)
        return remote(fin_s.at[k, n, cut], fin_r.at[k, n, cut], fin_ss.at[k], fin_rs.at[k], y_up if n == 0 else y_dn)

    def rs_put(k, a, value):
        held(k)[a] = value.astype(BF16)
        c_sib(k, a).start()

    def rs_pair(k, a):
        c_sib(k, a).wait_recv()
        return own_part(k, a) + sib[k, a].astype(F32)

    def rs_far(k):
        far_s[k] = rs_pair(k, (y + 2) % 4).astype(BF16)
        c_far(k, 0).start()
        c_far(k, 1).start()

    def rs_near(k, n):
        fin_s[k, n] = rs_pair(k, (y + 1 + 2 * n) % 4).astype(BF16)
        c_fin(k, n, 1 - n).start()

    def rs_mid(k):
        all_in(far_r.at[k], far_rs.at[k])
        for n in (0, 1):
            cut = pl.ds(64 * n, 64)
            fin_s[k, n, cut] = (fin_s[k, n, cut].astype(F32) + far_r[k, n].astype(F32)).astype(BF16)
            c_fin(k, n, n).start()

    def rs_finish(k):
        total = rs_pair(k, y)
        all_in(fin_r.at[k], fin_rs.at[k])
        return total + fin_r[k, 0].astype(F32) + fin_r[k, 1].astype(F32)

    w_zstart(0)
    all_in(vall.at[pl.ds(0, 7)], vec_r.at[0])
    all_sent(vall.at[pl.ds(0, 7)], vec_s.at[0])

    def gathered(row):
        return jnp.concatenate([vall[i, row : row + 1, :] for i in range(8)], axis=1)

    swap_wait(x_in, x_own, 0)
    x32 = x_own[...].astype(F32)
    normed_all[rows(j * PIECE, PIECE), :] = (x32 * rms_scale(x32) * gathered(0)).astype(BF16)
    ag_start(normed_all, 0)
    w_xstart(0)
    swap_start(cot_in, cot_own, 1)
    w_zstart(3)
    w_own(3)
    w_zstart(2)
    w_own(2)
    w_zstart(1)
    w_own(1)
    ag_near(normed_all, 0)
    for load in loads[7:]:
        load.wait()
    w_finish(0)

    doc = jnp.broadcast_to(doc_row, (8, D)).astype(F32).T[:, :1]
    feature = lax.broadcasted_iota(jnp.int32, (D, 128), 1)
    k_all[:, 128:] = jnp.where(
        feature == 0, OTHER_DOC * (1.0 - doc), jnp.where(feature == 1, OTHER_DOC * doc, 0.0)
    ).astype(BF16)
    q_more = jnp.where(feature == 0, doc, jnp.where(feature == 1, 1.0 - doc, 0.0)).astype(BF16)
    for i in range(4):
        for h in range(2):
            q_two[i, BLOCK * h : BLOCK * h + BLOCK, 128:] = q_more[BLOCK * i : BLOCK * i + BLOCK]

    def two_heads(value):
        first_head = lax.broadcasted_iota(jnp.int32, value.shape, 1) < HEAD_DIM
        return jnp.concatenate([jnp.where(first_head, value, 0.0), jnp.where(first_head, 0.0, value)], axis=0)

    def own_quarters(value):
        return jnp.concatenate([value[:HEAD_DIM, :BLOCK], value[HEAD_DIM:, BLOCK:]], axis=0)

    def project(yy):
        cut = rows(yy * BLOCK, BLOCK)
        lin = nn(normed_all[cut, :], wqkv[...])
        cos = cos_ref[cut, :]
        sin = sin_ref[cut, :]
        bias = vall[pl.ds(j, 1)][0]
        q_lin = lin[:, :128] + bias[2:3, :]
        k_lin = lin[:, 128:256] + bias[3:4, :]
        v_lin = lin[:, 256:] + bias[4:5, :]
        q = (q_lin * cos + half_turn(q_lin) * sin) * (0.125 * LOG2_E)
        k32 = k_lin * cos + half_turn(k_lin) * sin
        q_two[pl.ds(yy, 1), :, :128] = two_heads(q).astype(BF16)[None]
        k_all[cut, :128] = k32.astype(BF16)
        v_all[cut, :] = v_lin.astype(BF16)
        k_t[:, cut] = k32.T.astype(BF16)
        v_t[:, cut] = v_lin.T.astype(BF16)

    def cot_start():
        swap_wait(cot_in, cot_own, 1)
        cot_all[rows(j * PIECE, PIECE), :] = cot_own[...]
        ag_start(cot_all, 1)

    ag_run(normed_all, 0, project, lambda: w_xstart(3), cot_start)

    def attend(i):
        width = (i + 1) * BLOCK
        before = i * BLOCK
        cut = slice(before, width)
        scores = nt(k_all[:width, :], q_two[i])
        key_at = lax.broadcasted_iota(jnp.int32, (BLOCK, 2 * BLOCK), 0)
        query_at = lax.broadcasted_iota(jnp.int32, (BLOCK, 2 * BLOCK), 1) % BLOCK
        last = jnp.where(key_at <= query_at, scores[before:], NEG)
        top = jnp.max(last, axis=0, keepdims=True)
        if i > 0:
            top = jnp.maximum(top, jnp.max(scores[:before], axis=0, keepdims=True))
        weights = jnp.exp2(last - top)
        total = jnp.sum(weights, axis=0, keepdims=True)
        p_t[i, before:width, :] = weights.astype(BF16)
        if i > 0:
            weights = jnp.exp2(scores[:before] - top)
            total = total + jnp.sum(weights, axis=0, keepdims=True)
            p_t[i, :before, :] = weights.astype(BF16)
        inverse = 1.0 / total
        inv[i : i + 1, :] = inverse
        both = nn(v_t[:, :width], p_t[i, :width, :]) * inverse
        mixed_t[:, cut] = own_quarters(both)
        mixed[cut, :] = mixed_t[:, cut].T.astype(BF16)
        for m in (2 * i, 2 * i + 1):
            mix_start(m)

    def mix(m, sender):
        return remote(
            mixed.at[rows(m * PIECE, PIECE), :], mixed_own.at[:, rows(sender * 128, 128)],
            mx_s.at[0], mx_r.at[0], dev(x, m // 2, z, m % 2),
        )

    def mix_start(m):
        @pl.when(j != m)
        def _():
            mix(m, j).start()

        @pl.when(j == m)
        def _():
            mixed_own[:, rows(j * 128, 128)] = mixed[m * PIECE : (m + 1) * PIECE, :]

    w_xstart(2)
    attend(0)
    attend(1)
    w_xstart(1)
    ag_near(cot_all, 1)
    attend(2)
    wo_pass_x()
    attend(3)
    ag_pass(cot_all, 1)
    wo_pass_finish()
    all_in(mixed_own.at[:, pl.ds(0, 896)], mx_r.at[0])
    all_sent(mixed.at[pl.ds(0, 896)], mx_s.at[0])

    hidden[...] = x_own[...].astype(F32) + nn(mixed_own[...], wo_all[...])
    hid = hidden[...]
    mlp_all[rows(j * PIECE, PIECE), :] = (hid * rms_scale(hid) * gathered(1)).astype(BF16)
    ag_start(mlp_all, 2)
    ag_far(cot_all, 1)
    w_finish(2)
    ag_finish(cot_all, 1)

    def active_back(i, carry):
        cut = rows(i * BLOCK, BLOCK)
        g_act[cut, :] = nt(cot_all[cut, :], wdn[...])
        return carry

    lax.fori_loop(0, 4, active_back, 0)
    w_finish(1)

    unit = lax.broadcasted_iota(jnp.int32, (1, FB), 1)
    low_edge = 128 * (j // 7)
    high_edge = FB - 128 * ((j // 6) * (1 - j // 7))
    live = (unit >= low_edge) & (unit < high_edge)

    def feed(yy):
        cut = rows(yy * BLOCK, BLOCK)
        both = nn(mlp_all[cut, :], wgu[...])
        gate = both[:, :FB]
        up = both[:, FB:]
        sig = 1.0 / (1.0 + jnp.exp(-gate))
        silu = gate * sig
        back = jnp.where(live, g_act[cut, :], 0.0)
        act = jnp.where(live, silu * up, 0.0)
        active[cut, :] = act.astype(BF16)
        g_gu[cut, :FB] = (back * up * sig * (1.0 + gate * (1.0 - sig))).astype(BF16)
        g_gu[cut, FB:] = (back * silu).astype(BF16)
        rs_put(1, yy, nt(g_gu[cut, :], wgu[...]))

    ag_run(mlp_all, 2, feed)
    rs_far(1)

    terms = (dga, dgb, ddn, dqa, dqb, dwo)
    term_in = (ra, rb, rd, rqa, rqb, rw)
    halfway = (ha, hb, hd, hqa, hqb, hw)
    half_in = (sa, sb, sd, sqa, sqb, sw)

    def first(n, r):
        if n in (0, 3, 5):
            src, to = terms[n].at[(x + r) % 4], dev(x + r, y, z, c)
        else:
            src, to = terms[n].at[:, (z + r) % 4], dev(x, y, z + r, c)
        return remote(src, term_in[n].at[r - 1], f1_s.at[n], f1_r.at[n], to)

    def second(n, r):
        if n in (0, 3, 5):
            src, to = halfway[n].at[(z + r) % 4], dev(x, y, z + r, c)
        else:
            src, to = halfway[n].at[(x + r) % 4], dev(x + r, y, z, c)
        return remote(src, half_in[n].at[r - 1], f2_s.at[n], f2_r.at[n], to)

    def first_start(n):
        for r in (1, 3, 2):
            first(n, r).start()

    def first_sum(n):
        total = (terms[n][x] if n in (0, 3, 5) else terms[n][:, z]).astype(F32)
        all_in(term_in[n], f1_r.at[n])
        for r in (1, 3, 2):
            total = total + term_in[n][r - 1].astype(F32)
        halfway[n][...] = total.astype(BF16)
        for r in (1, 3, 2):
            second(n, r).start()

    def second_sum(n):
        total = halfway[n][z if n in (0, 3, 5) else x].astype(F32)
        all_in(half_in[n], f2_r.at[n])
        for r in (1, 3, 2):
            total = total + half_in[n][r - 1].astype(F32)
        return total.astype(BF16)

    def chunk(t, xl_):
        return (t % 2) * 2 + xl_, t // 2

    def grad_gu(i, carry):
        got = tn(mlp_all[:, rows(i * BLOCK, BLOCK)], g_gu[...]).astype(BF16)
        for xl_ in range(2):
            for t in range(8):
                x_, z_ = chunk(t, xl_)
                share = got[xl_ * 128 + t * 16 : xl_ * 128 + t * 16 + 16]
                dga[x_, z_, i] = share[:, :512]
                dgb[x_, z_, i] = share[:, 512:]
        return carry

    def grad_dn(i, carry):
        got = nn(active_t[...], cot_all[:, rows(i * BLOCK, BLOCK)]).astype(BF16)
        for xl_ in range(2):
            for t in range(8):
                x_, z_ = chunk(t, xl_)
                ddn[x_, z_, i] = got[t * 48 : t * 48 + 48, xl_ * 128 : xl_ * 128 + 128]
        return carry

    def grad_qkv(part_ref, base):
        def go(i, carry):
            got = tn(normed_all[:, rows((base + i) * BLOCK, BLOCK)], g_qkv[...]).astype(BF16)
            for xl_ in range(2):
                for t in range(8):
                    x_, z_ = chunk(t, xl_)
                    part_ref[x_, z_, i] = got[xl_ * 128 + t * 16 : xl_ * 128 + t * 16 + 16]
            return carry

        lax.fori_loop(0, 2, go, 0)

    def grad_wo():
        got = tn(mixed[...], branch_all[...]).astype(BF16)
        for h in range(2):
            for t in range(8):
                x_, z_ = chunk(t, (h + c) % 2)
                dwo[pl.ds(x_, 1), z_] = got[h * 64 : h * 64 + 64, t * 128 : t * 128 + 128][None]

    lax.fori_loop(0, 4, grad_gu, 0)
    rs_near(1, 0)
    rs_near(1, 1)
    first_start(1)
    first_start(0)
    rs_mid(1)
    active_t[...] = active[...].T
    lax.fori_loop(0, 4, grad_dn, 0)
    first_start(2)

    grad = rs_finish(1)
    hid = hidden[...]
    scale = rms_scale(hid)
    scaled = grad * gathered(1)
    back = scale * scaled - hid * (scale * scale * scale) * jnp.mean(scaled * hid, axis=-1, keepdims=True)
    g_hidden[...] = cot_own[...].astype(F32) + back
    branch_all[rows(j * PIECE, PIECE), :] = g_hidden[...].astype(BF16)

    def unmix_term(i, carry):
        cut = rows(i * BLOCK, BLOCK)
        mixed_grad[:, cut] = nt(branch_all[rows(j * PIECE, PIECE), :], wo_all[cut, :]).astype(BF16)
        return carry

    lax.fori_loop(0, 4, unmix_term, 0)
    g_mixed[rows(j * PIECE, PIECE), :] = mixed_grad[:, rows(j * 128, 128)]

    def unmix(m, sender):
        return remote(
            mixed_grad.at[:, rows(m * 128, 128)], g_mixed.at[rows(sender * PIECE, PIECE), :],
            um_s.at[0], um_r.at[0], dev(x, m // 2, z, m % 2),
        )

    def unmix_start(r, carry):
        unmix((j + r) % 8, j).start()
        return carry

    lax.fori_loop(1, 8, unmix_start, 0)
    gain_two = jnp.sum(grad * hid * scale, axis=0, keepdims=True)
    gk_acc[...] = jnp.zeros_like(gk_acc)
    gv_acc[...] = jnp.zeros_like(gv_acc)

    def output_term(i, carry):
        rs_put(2, i, nn(active[rows(i * BLOCK, BLOCK), :], wdn[...]))
        return carry

    lax.fori_loop(0, 4, output_term, 0)
    first_sum(1)
    first_sum(0)
    all_in(g_mixed.at[pl.ds(0, 896)], um_r.at[0])
    all_sent(mixed_grad.at[:, pl.ds(0, 896)], um_s.at[0])
    all_sent(sib.at[1], sib_ss.at[1])
    ag_start(branch_all, 3)

    def along_y(n, r, recv=False):
        src = (sum_gu, sum_dn, sum_qkv)[n].at[(y + r) % 4]
        dst = (all_gu, all_dn, all_qkv)[n].at[place, c, (y + 4 - r) % 4 if recv else y]
        return remote(src, dst, ya_s.at[n], ya_r.at[n], dev(x, y + r, z, c))

    def share(n):
        total, every = ((sum_gu, all_gu), (sum_dn, all_dn), (sum_qkv, all_qkv))[n]
        if n == 0:
            total[:, :, :512] = second_sum(0)
            total[:, :, 512:] = second_sum(1)
        elif n == 1:
            total[...] = second_sum(2)
        else:
            total[:2] = second_sum(3)
            total[2:] = second_sum(4)
        for r in (1, 3, 2):
            along_y(n, r).start()
        every[place, c, y] = total[y]

    arrays = (all_gu, all_dn, all_wo, all_qkv)

    def spot(n, r, c_):
        return arrays[n].at[((z + 4 - r % 4) % 4) * 2 + (xh + r // 4) % 2, c_]

    def gd(n, r, recv=False):
        if n == 2:
            ref = spot(n, r if recv else 0, c)
            return remote(ref, ref, gd_s.at[n - 2], gd_r.at[3 if n == 2 else (0, 1, 1, 1, 0, 2, 2, 2)[r]], dev(x + 2 * (r // 4), y, z + r % 4, c))
        ref = spot(n, r if recv else 4 * (r // 5), c)
        return remote(ref, ref, gd_s.at[n - 2], gd_r.at[3 if n == 2 else (0, 1, 1, 1, 0, 2, 2, 2)[r]], dev(x + 2 * (r == 4), y, z + r % 4, c))

    def gp(n, r, recv=False):
        ref = spot(n, r, (1 - c) if recv else c)
        return remote(ref, ref, gp_s.at[n - 2], gp_r.at[n - 2], sibling)

    def pair(n, z_, c_):
        return arrays[n].at[pl.ds(((z_ + 4) % 4) * 2, 2), c_]

    def single(n, z_, h):
        return arrays[n].at[pl.ds(((z_ + 4) % 4) * 2 + h, 1), c]

    def ring(n, k, recv=False):
        if k == 0:
            ref, to = single(n, z, (1 - xh) if recv else xh), dev(x + 2, y, z, c)
        elif k == 1:
            ref, to = pair(n, z - 1 if recv else z, c), dev(x, y, z + 1, c)
        elif k == 2:
            ref, to = pair(n, z + 1 if recv else z, c), dev(x, y, z + 3, c)
        elif k == 3:
            ref, to = single(n, z - 2 if recv else z - 1, 0), dev(x, y, z + 1, c)
        elif k == 4:
            ref, to = single(n, z + 2 if recv else z + 1, 1), dev(x, y, z + 3, c)
        else:
            ref, to = pair(n, z + (k - 5), (1 - c) if recv else c), sibling
        return remote(ref, ref, rg_s.at[n, k // 5], rg_r.at[n, (0, 1, 1, 2, 2, 3, 3, 3, 3)[k]], to)

    def ring_one(n):
        all_in(arrays[n].at[place, c, pl.ds(0, 3)], ya_r.at[n])
        ring(n, 0).start()

    def ring_two(n):
        ring(n, 0, True).wait_recv()
        for k in (1, 2, 5):
            ring(n, k).start()

    def ring_three(n):
        all_in(arrays[n].at[pl.ds(0, 4), c], rg_r.at[n, 1])
        for k in (3, 4, 8, 6):
            ring(n, k).start()

    def ring_four(n):
        all_in(arrays[n].at[pl.ds(0, 2), c], rg_r.at[n, 2])
        ring(n, 7).start()

    def ring_five(n):
        all_in(arrays[n].at[:, c], rg_r.at[n, 3])

    def spread_start(n):
        if n != 2:
            all_in(arrays[n].at[place, c, pl.ds(0, 3)], ya_r.at[min(n, 2)])
        for r in (6, 4, 5, 7, 2, 1, 3) if n == 2 else (4, 2, 1, 3):
            gd(n, r).start()
        gp(n, 0).start()

    def spread_next(n):
        if n == 3:
            gd(n, 4, True).wait_recv()
            for r in (6, 5, 7):
                gd(n, r).start()
            gp(n, 4).start()

    def spread_pass(n):
        if n == 2:
            all_in(arrays[n].at[pl.ds(0, 7), c], gd_r.at[3])
            for r in range(1, 8):
                gp(n, r).start()
        else:
            for i, steps in ((1, (1, 3, 2)), (2, (5, 7, 6))):
                all_in(arrays[n].at[pl.ds(0, 3), c], gd_r.at[i])
                for r in steps:
                    gp(n, r).start()

    def spread_finish(n):
        all_in(arrays[n].at[:, c], gp_r.at[n - 2])

    def unturn(value, cut):
        value = value.astype(BF16).astype(F32)
        return (value * cos_ref[cut, :] - half_turn(value) * sin_ref[cut, :]).astype(BF16)

    def attend_back(i):
        width = (i + 1) * BLOCK
        cut = slice(i * BLOCK, width)
        inverse = inv[i : i + 1, :]
        grad_t = g_mixed[cut, :].astype(F32).T
        scaled = jnp.concatenate([grad_t[:HEAD_DIM] * inverse[:, :BLOCK], grad_t[HEAD_DIM:] * inverse[:, BLOCK:]], axis=0)
        scaled = scaled.astype(BF16).astype(F32)
        products = scaled * mixed_t[:, cut]
        delta = jnp.concatenate(
            [jnp.sum(products[:HEAD_DIM], axis=0, keepdims=True), jnp.sum(products[HEAD_DIM:], axis=0, keepdims=True)], axis=1
        )
        grad_two = two_heads(scaled.T).astype(BF16)
        weights = p_t[i, :width, :]
        gv_acc[:width, :] += nn(weights, grad_two)
        g_probs = nt(v_all[:width, :], grad_two)
        g_scores = (weights.astype(F32) * (g_probs - delta)).astype(BF16)
        gk_acc[:width, :] += nn(g_scores, q_two[i, :, :128])
        g_query = own_quarters(nn(k_t[:, :width], g_scores)) * 0.125
        g_qkv[cut, :128] = unturn(g_query.T, cut)

    def block_back(i):
        cut = slice(i * BLOCK, (i + 1) * BLOCK)
        attend_back(i)
        g_qkv[cut, 128:256] = unturn(gk_acc[cut, :] * (1.0 / LOG2_E), cut)
        g_qkv[cut, 256:] = gv_acc[cut, :].astype(BF16)
        rs_put(3, i, nt(g_qkv[cut, :], wqkv[...]))

    block_back(3)
    block_back(2)
    share(0)
    first_sum(2)
    ag_near(branch_all, 3)
    block_back(1)
    block_back(0)
    rs_far(3)
    grad_qkv(dqb, 2)
    first_start(4)
    ring_one(0)
    grad_qkv(dqa, 0)
    first_start(3)
    rs_near(3, 0)
    rs_near(3, 1)
    ag_pass(branch_all, 3)
    share(1)
    ag_far(branch_all, 3)
    rs_mid(3)
    ring_two(0)
    first_sum(4)
    first_sum(3)
    ring_one(1)
    rs_far(2)
    ag_finish(branch_all, 3)
    grad_wo()
    first_start(5)
    rs_near(2, 0)
    rs_near(2, 1)

    grad = rs_finish(3)
    scale = rms_scale(x32)
    scaled = grad * gathered(0)
    back = scale * scaled - x32 * (scale * scale * scale) * jnp.mean(scaled * x32, axis=-1, keepdims=True)
    ig_send[...] = (g_hidden[...] + back).astype(BF16)
    swap_start(ig_send, in_grad, 3)
    share(2)
    ring_two(1)
    first_sum(5)

    gain_one = jnp.sum(grad * x32 * scale, axis=0, keepdims=True)
    vs[...] = jnp.zeros_like(vs)
    for i in range(8):
        vs[i, 0:1, :] = gain_one[:, 128 * i : 128 * i + 128]
        vs[i, 1:2, :] = gain_two[:, 128 * i : 128 * i + 128]
    bias_sum = jnp.sum(g_qkv[...].astype(F32), axis=0, keepdims=True)
    for i in range(3):
        vs[pl.ds(j, 1), 2 + i : 3 + i, :] = bias_sum[:, 128 * i : 128 * i + 128][None]

    def v1_copy(r):
        return remote(vs.at[(f + r) % 8], vr.at[r - 1], v1_ss.at[0], v1_rs.at[0], (s, (f + r) % 8))

    def v1_start(r, carry):
        v1_copy(r).start()
        return carry

    lax.fori_loop(1, 8, v1_start, 0)
    ring_three(0)
    spread_start(3)
    ring_three(1)
    rs_mid(2)
    wo_send[...] = second_sum(5)
    swap_start(wo_send, all_wo.at[place, (c + moves) % 2], 4)
    all_in(vr, v1_rs.at[0])
    all_sent(vr, v1_ss.at[0])
    v2s[...] = jnp.sum(vr[...], axis=0) + vs[pl.ds(f, 1)][0]

    def v2_copy(r):
        to = dev(x + 2 * (r // 4), y, z + r % 4, c)
        return remote(v2s, v2r.at[r - 1], v2_ss.at[0], v2_rs.at[0], to)

    def v2_start(r, carry):
        v2_copy(r).start()
        return carry

    lax.fori_loop(1, 8, v2_start, 0)
    spread_next(3)
    swap_wait(wo_send, all_wo.at[place, c], 4)
    spread_start(2)
    lo_send[...] = (hidden[...] + rs_finish(2)).astype(BF16)
    swap_start(lo_send, layer_out, 2)
    all_in(v2r, v2_rs.at[0])
    all_sent(v2r, v2_ss.at[0])
    v3s[...] = jnp.sum(v2r[...], axis=0) + v2s[...]
    v3_copy = remote(v3s, v3r, v3_ss.at[0], v3_rs.at[0], sibling)
    v3_copy.start()
    ring_four(0)
    spread_pass(3)
    ring_four(1)
    spread_next(2)
    spread_pass(2)
    v3_copy.wait()
    vec_out[...] = v3s[...] + v3r[...]
    swap_wait(lo_send, layer_out, 2)
    swap_wait(ig_send, in_grad, 3)
    for n in (0, 1):
        ring_five(n)
    for n in (3, 2):
        spread_finish(n)

    for n in range(4):
        all_sent(quarters(n, 3), wy_s.at[n])
        all_sent(quarters(n, 9), wz_s.at[n])
        all_sent(blocks(n, 4), wx_s.at[n])
    all_sent(wo_all.at[pl.ds(0, 448)], wp_s.at[0])
    for k, buf in enumerate((normed_all, cot_all, mlp_all, branch_all)):
        all_sent(buf.at[pl.ds(0, 896)], ag_s.at[k])
    for k in range(1, 4):
        if k > 1:
            all_sent(sib.at[k], sib_ss.at[k])
        all_sent(far_s.at[k], far_ss.at[k])
        all_sent(fin_s.at[k], fin_ss.at[k])
    for n in range(6):
        all_sent(term_in[n], f1_s.at[n])
        all_sent(half_in[n], f2_s.at[n])
    for n in (0, 1, 3):
        all_sent(arrays[n].at[place, c, pl.ds(0, 3)], ya_s.at[min(n, 2)])
    for n in (0, 1):
        all_sent(arrays[n].at[pl.ds(0, 7), c], rg_s.at[n, 0])
        all_sent(arrays[n].at[:, c], rg_s.at[n, 1])
    for n in (2, 3):
        all_sent(arrays[n].at[pl.ds(0, 7), c], gd_s.at[n - 2])
        all_sent(arrays[n].at[:, c], gp_s.at[n - 2])


def fused_layer(*args):
    def vmem(*shape, dtype=BF16):
        return pltpu.VMEM(shape, dtype)

    def dma(*shape):
        return pltpu.SemaphoreType.DMA(shape)

    full = vmem(D, D)
    shares = ((4, 16, 512), (4, 16, 256), (4, 48, 128), (2, 16, FB), (2, 16, FB), (64, 128))
    scratch = [
        vmem(D, 128, dtype=F32), vmem(D, 128, dtype=F32), vmem(8, 128, dtype=F32),
        vmem(PIECE, D), vmem(PIECE, D), vmem(PIECE, D, dtype=F32), vmem(PIECE, D, dtype=F32),
        full, vmem(D, FB), vmem(D, 2 * FB), vmem(FB, D), vmem(8, 8, 128, dtype=F32),
        full, full, full, full,
        vmem(4, 2 * BLOCK, 256), vmem(D, 256), vmem(D, 128), vmem(128, D), vmem(128, D),
        vmem(4, D, 2 * BLOCK), vmem(8, 2 * BLOCK, dtype=F32), vmem(128, D, dtype=F32), vmem(D, 128), vmem(PIECE, D), vmem(PIECE, D),
        vmem(D, FB, dtype=F32), vmem(D, FB), vmem(FB, D), vmem(D, 2 * FB), vmem(D, 128),
        vmem(D, 128, dtype=F32), vmem(D, 128, dtype=F32), vmem(D, FB),
        vmem(2, 4, BLOCK, D), vmem(4, 4, PIECE, D), vmem(4, PIECE, D), vmem(4, 2, 64, D), vmem(4, 2, PIECE, D), vmem(4, 2, PIECE, D),
        *(vmem(4, 4, *dims) for dims in shares),
        *(vmem(3, 4, *dims) for dims in shares),
        *(vmem(4, *dims) for dims in shares),
        *(vmem(3, *dims) for dims in shares),
        vmem(64, 128), vmem(4, 16, 2 * FB), vmem(4, 48, 128), vmem(4, 16, FB),
        vmem(PIECE, D), vmem(PIECE, D),
        vmem(8, 8, 128, dtype=F32), vmem(7, 8, 128, dtype=F32), vmem(8, 128, dtype=F32), vmem(7, 8, 128, dtype=F32),
        vmem(8, 128, dtype=F32), vmem(8, 128, dtype=F32),
        dma(6), dma(5), dma(5), dma(1), dma(1), dma(4), dma(4, 3), dma(4), dma(4, 3), dma(4), dma(4),
        dma(1), dma(1), dma(1), dma(1), dma(1), dma(1), dma(4), dma(4, 7),
        dma(4), dma(4, 4), dma(4), dma(4), dma(4), dma(4),
        dma(6), dma(6), dma(6), dma(6), dma(3), dma(3), dma(2, 2), dma(2, 4), dma(2), dma(4), dma(2), dma(2),
        dma(1), dma(1), dma(1), dma(1), dma(1), dma(1),
    ]
    anywhere = pl.BlockSpec(memory_space=pl.ANY)
    inside = pl.BlockSpec(memory_space=pltpu.VMEM)

    def out(*shape, dtype=BF16):
        return pltpu.VMEM(shape, dtype)

    return pl.pallas_call(
        layer_kernel,
        out_shape=(
            out(PIECE, D), out(PIECE, D), out(8, 2, 4, 16, 2 * FB), out(8, 2, 4, 48, 128), out(8, 2, 64, 128),
            out(8, 2, 4, 16, FB), out(8, 128, dtype=F32),
        ),
        in_specs=[anywhere] * 11 + [inside] * 6,
        out_specs=[inside] * 7,
        scratch_shapes=scratch,
        compiler_params=pltpu.CompilerParams(
            collective_id=0, has_side_effects=True, vmem_limit_bytes=57 * 1024 * 1024
        ),
        name="layer",
    )(*args)


def spread_kernel(
    lo_in, ig_in, gu, dn, wo, qkv, vec,
    lo, ig, d_gain_a, d_q, d_k, d_v, d_bq, d_bk, d_bv, d_o, d_gain_m, d_gate, d_up, d_down,
    ig_v, q_v, k_v, v_v, o_v, gate_v, up_v, down_v, sems,
):
    stores = []

    def store(src, dst):
        copy = pltpu.make_async_copy(src, dst, sems.at[len(stores)])
        copy.start()
        stores.append(copy)

    for ref, row in ((d_gain_a, 0), (d_gain_m, 1), (d_bq, 2), (d_bk, 3), (d_bv, 4)):
        ref[...] = vec[row : row + 1, :]
    store(lo_in, lo)
    for m in range(8):
        first = 128 if m == 7 else 0
        count = 256 if m >= 6 else FB
        start = min(m, 6) * FB + (256 if m == 7 else 0)
        for t in range(8):
            low, high = max(48 * t, first), min(48 * t + 48, first + count)
            if low < high:
                down_v[start + low - first : start + high - first, :] = dn[
                    t, m % 2, m // 2, low - 48 * t : high - 48 * t, :
                ].astype(F32)
    store(down_v, d_down)
    for ref, off, dst in ((gate_v, 0, d_gate), (up_v, FB, d_up)):
        for m in range(8):
            first = 128 if m == 7 else 0
            count = 256 if m >= 6 else FB
            start = min(m, 6) * FB + (256 if m == 7 else 0)
            for t in range(8):
                cut = slice(16 * t, 16 * t + 16)
                ref[cut, start : start + count] = gu[t, m % 2, m // 2, :, off + first : off + first + count].astype(F32)
        store(ref, dst)
    for i, (ref, dst) in enumerate(((q_v, d_q), (k_v, d_k), (v_v, d_v))):
        for t in range(8):
            for m in range(8):
                ref[16 * t : 16 * t + 16, 128 * m : 128 * m + 128] = qkv[
                    t, m % 2, m // 2, :, 128 * i : 128 * i + 128
                ].astype(F32)
        store(ref, dst)
    flip = lax.axis_index("fsdp") % 2
    for t in range(8):
        for core in range(2):
            to = pl.ds(pl.multiple_of(64 * ((core + flip) % 2), 64), 64)
            o_v[to, 128 * t : 128 * t + 128] = wo[t, core].astype(F32)
    store(o_v, d_o)
    ig_v[...] = ig_in[...].astype(F32)
    store(ig_v, ig)
    for copy in stores:
        copy.wait()


def spread(*args):
    def out(*shape, dtype=F32):
        return jax.ShapeDtypeStruct(shape, dtype)

    inside = pl.BlockSpec(memory_space=pltpu.VMEM)
    anywhere = pl.BlockSpec(memory_space=pl.ANY)
    vec, square, wide, tall = out(1, 128), out(128, D), out(128, 2816), out(2816, 128)
    return pl.pallas_call(
        spread_kernel,
        out_shape=(
            out(PIECE, D, dtype=BF16), out(PIECE, D), vec, square, square, square, vec, vec, vec,
            square, vec, wide, wide, tall,
        ),
        in_specs=[inside] * 7,
        out_specs=[anywhere, anywhere, inside, anywhere, anywhere, anywhere, inside, inside, inside]
        + [anywhere, inside, anywhere, anywhere, anywhere],
        scratch_shapes=[pltpu.VMEM(o.shape, o.dtype) for o in (square,) * 5 + (wide, wide, tall)]
        + [pltpu.SemaphoreType.DMA((9,))],
        compiler_params=pltpu.CompilerParams(vmem_limit_bytes=24 * 1024 * 1024),
        name="spread",
    )(*args)


def rotary_tables():
    exponent = np.arange(HEAD_DIM // 2, dtype=np.float32) * np.float32(2.0 / HEAD_DIM)
    inverse = np.exp(np.float32(-math.log(THETA)) * exponent)
    angles = np.arange(D, dtype=np.float32)[:, None] * inverse
    cos, sin = np.cos(angles), np.sin(angles)
    return np.concatenate([cos] * 4, axis=1), np.concatenate([-sin, sin] * 2, axis=1)


def per_device(
    inputs, doc_ids, positions, attn_gain, query_weight, key_weight, value_weight,
    query_bias, key_bias, value_bias, out_weight, mlp_gain, gate_weight, up_weight,
    down_weight, cotangent,
):
    del positions
    cos, sin = rotary_tables()
    vectors = [v.reshape(1, 128) for v in (attn_gain, mlp_gain, query_bias, key_bias, value_bias)]
    blocks = fused_layer(
        inputs.reshape(PIECE, D), cotangent.reshape(PIECE, D),
        query_weight, key_weight, value_weight, out_weight, gate_weight, up_weight, down_weight,
        jnp.asarray(cos), jnp.asarray(sin), *vectors, doc_ids,
    )
    outs = list(spread(*blocks))
    outs[0] = outs[0].reshape(inputs.shape)
    outs[1] = outs[1].reshape(inputs.shape)
    return tuple(o.reshape(128) if o.shape == (1, 128) else o for o in outs)


def solution(mesh):
    rows_spec = P("fsdp", None)
    act = P("seq", "fsdp", None)
    vec = P("fsdp")
    return jax.shard_map(
        per_device,
        mesh=mesh,
        in_specs=(
            act, P(), P("seq", "fsdp"), vec, rows_spec, rows_spec, rows_spec, vec, vec, vec,
            rows_spec, vec, rows_spec, rows_spec, P(None, "fsdp"), act,
        ),
        out_specs=(
            act, act, vec, rows_spec, rows_spec, rows_spec, vec, vec, vec, rows_spec, vec,
            rows_spec, rows_spec, P(None, "fsdp"),
        ),
        check_vma=False,
    )
```

```python
import math

import jax
import jax.numpy as jnp
import numpy as np
from jax import lax
from jax.experimental import pallas as pl
from jax.experimental.pallas import tpu as pltpu
from jax.sharding import PartitionSpec as P

MESH = pl.DeviceIdType.MESH
HEAD_DIM = 64
EPS = 1e-06
THETA = 1000000.0
NEG = -1000000000.0
OTHER_DOC = -(2.0**30)
LOG2_E = math.log2(math.e)
D = 1024
PIECE = 128
BLOCK = 256
FB = 384
F32 = jnp.float32
BF16 = jnp.bfloat16


def nn(a, b):
    return lax.dot_general(a, b, (((1,), (0,)), ((), ())), preferred_element_type=F32)


def nt(a, b):
    return lax.dot_general(a, b, (((1,), (1,)), ((), ())), preferred_element_type=F32)


def tn(a, b):
    return lax.dot_general(a, b, (((0,), (0,)), ((), ())), preferred_element_type=F32)


def rms_scale(value):
    return lax.rsqrt(jnp.mean(value * value, axis=-1, keepdims=True) + EPS)


def rows(start, size):
    return pl.ds(pl.multiple_of(start, size), size)


def half_turn(value):
    lane = lax.broadcasted_iota(jnp.int32, value.shape, 1)
    ahead = pltpu.roll(value, 96, 1)
    behind = pltpu.roll(value, 32, 1)
    return jnp.where(lane % 64 < 32, ahead, behind)


def layer_kernel(
    x_in, cot_in, wq_in, wk_in, wv_in, wo_in, wg_in, wu_in, wd_in, cos_in, sin_in,
    gain_a, gain_m, bias_q, bias_k, bias_v, docs,
    layer_out, in_grad, all_gu, all_dn, all_wo, all_qkv, vec_out,
    cos_ref, sin_ref, vec_in,
    x_own, cot_own, hidden, g_hidden, wo_all, wqkv, wgu, wdn, vall,
    normed_all, cot_all, mlp_all, branch_all,
    q_two, k_all, v_all, k_t, v_t, p_t, inv, mixed_t, mixed, mixed_own, mixed_grad,
    g_act, active, active_t, g_gu, g_mixed, gk_acc, gv_acc, g_qkv,
    part, sib, far_s, far_r, fin_s, fin_r,
    dga, dgb, ddn, dqa, dqb, dwo, ra, rb, rd, rqa, rqb, rw, ha, hb, hd, hqa, hqb, hw, sa, sb, sd, sqa, sqb, sw, wo_send, sum_gu, sum_dn, sum_qkv,
    lo_send, ig_send,
    vs, vr, v2s, v2r, v3s, v3r,
    sem_load, swap_s, swap_r, vec_s, vec_r, wy_s, wy_r, wz_s, wz_r, wx_s, wx_r, wp_s, wp_r, mx_s, mx_r, um_s, um_r, ag_s, ag_r,
    sib_ss, sib_rs, far_ss, far_rs, fin_ss, fin_rs,
    f1_s, f1_r, f2_s, f2_r, ya_s, ya_r, rg_s, rg_r, gd_s, gd_r, gp_s, gp_r, v1_ss, v1_rs, v2_ss, v2_rs, v3_ss, v3_rs,
):
    s = lax.axis_index("seq")
    f = lax.axis_index("fsdp")
    xh = s // 8
    z = (s % 8) // 2
    c = s % 2
    y = f // 2
    xl = f % 2
    x = xh * 2 + xl
    j = y * 2 + c
    place = z * 2 + xh

    def dev(x_, y_, z_, c_):
        x_, y_, z_ = (x_ + 4) % 4, (y_ + 4) % 4, (z_ + 4) % 4
        return ((x_ // 2) * 8 + z_ * 2 + c_, y_ * 2 + x_ % 2)

    sibling = dev(x, y, z, 1 - c)
    y_up = dev(x, y + 1, z, c)
    y_dn = dev(x, y + 3, z, c)
    moves = (c + xl) % 2
    partner = dev(xh * 2 + 1 - xl, y, z, 1 - c)
    x_to = dev(x + 1 + 2 * c, y, z, c)

    def window(m):
        return (3 * m - 2 * (m // 7)) * 128

    def remote(src, dst, ss, rs, to):
        return pltpu.make_async_remote_copy(
            src_ref=src, dst_ref=dst, send_sem=ss, recv_sem=rs, device_id=to, device_id_type=MESH
        )

    def all_in(ref, sem):
        remote(ref, ref, sem, sem, sibling).wait_recv()

    def all_sent(ref, sem):
        remote(ref, ref, sem, sem, sibling).wait_send()

    def at(start, size, unit):
        return pl.ds(pl.multiple_of(start, unit), size)

    own_rows = rows(f * 128, 128)
    own_win = at(window(j), FB, 128)
    loads = [
        pltpu.make_async_copy(wq_in.at[:, rows(j * 128, 128)], wqkv.at[own_rows, pl.ds(0, 128)], sem_load.at[0]),
        pltpu.make_async_copy(wk_in.at[:, rows(j * 128, 128)], wqkv.at[own_rows, pl.ds(128, 128)], sem_load.at[0]),
        pltpu.make_async_copy(wv_in.at[:, rows(j * 128, 128)], wqkv.at[own_rows, pl.ds(256, 128)], sem_load.at[0]),
        pltpu.make_async_copy(wo_in, wo_all.at[own_rows], sem_load.at[1]),
        pltpu.make_async_copy(wg_in.at[:, own_win], wgu.at[own_rows, pl.ds(0, FB)], sem_load.at[2]),
        pltpu.make_async_copy(wu_in.at[:, own_win], wgu.at[own_rows, pl.ds(FB, FB)], sem_load.at[2]),
        pltpu.make_async_copy(wd_in.at[own_win, :], wdn.at[:, own_rows], sem_load.at[3]),
        pltpu.make_async_copy(cos_in, cos_ref, sem_load.at[4]),
        pltpu.make_async_copy(sin_in, sin_ref, sem_load.at[5]),
    ]
    for load in loads:
        load.start()

    barrier = pltpu.get_barrier_semaphore()

    def greet(to):
        pl.semaphore_signal(barrier, inc=1, device_id=to, device_id_type=MESH)

    def greet_near(r, carry):
        greet(dev(x + r, y, z, c))
        greet(dev(x, y, z + r, c))
        greet(dev(x + 2, y, z + r, c))
        return carry

    def greet_fsdp(r, carry):
        greet((s, (f + r) % 8))
        return carry

    def greet_cross(r, carry):
        greet(dev(x, y + r, z, 1 - c))
        return carry

    lax.fori_loop(1, 4, greet_near, 0)
    lax.fori_loop(1, 8, greet_fsdp, 0)
    lax.fori_loop(0, 4, greet_cross, 0)

    @pl.when(moves == 1)
    def _():
        greet(partner)
        pl.semaphore_wait(barrier, 21)

    @pl.when(moves == 0)
    def _():
        pl.semaphore_wait(barrier, 20)

    def swap_start(src, dst, n):
        @pl.when(moves == 1)
        def _():
            remote(src, dst, swap_s.at[n], swap_r.at[n], partner).start()

        @pl.when(moves == 0)
        def _():
            pltpu.make_async_copy(src, dst, swap_r.at[n]).start()

    def swap_wait(src, dst, n):
        @pl.when(moves == 1)
        def _():
            remote(src, dst, swap_s.at[n], swap_r.at[n], partner).wait()

        @pl.when(moves == 0)
        def _():
            pltpu.make_async_copy(src, dst, swap_r.at[n]).wait()

    def vec_copy(r):
        return remote(vec_in, vall.at[f], vec_s.at[0], vec_r.at[0], (s, (f + r) % 8))

    def vec_start(r, carry):
        vec_copy(r).start()
        return carry

    vec_in[...] = jnp.zeros_like(vec_in)
    for i, ref in enumerate((gain_a, gain_m, bias_q, bias_k, bias_v)):
        vec_in[i : i + 1, :] = ref[...].astype(F32)
    lax.fori_loop(1, 8, vec_start, 0)
    swap_start(x_in, x_own, 0)
    vall[pl.ds(f, 1)] = vec_in[...][None]
    doc_row = docs[pl.ds(xh * 8 + z * 2 + xl, 1), :]

    PARTS = (3, 2, 1, 1)

    def shard(r):
        return ((y + 4 - r) % 4) * 2 + xl

    def w_quarter(n, f_, q, p=None):
        if n == 0:
            return wqkv.at[at(f_ * 128 + q * 32, 32, 32), slice(None) if p is None else pl.ds(p * 128, 128)]
        if n == 1:
            return wgu.at[at(f_ * 128 + q * 32, 32, 32), slice(None) if p is None else pl.ds(p * FB, FB)]
        if n == 2:
            return wdn.at[at(q * 96, 96, 32), rows(f_ * 128, 128)]
        return wo_all.at[at(f_ * 128 + c * 64 + q * 16, 16, 16)]

    def w_rows(n, f_):
        if n == 0:
            return wqkv.at[rows(f_ * 128, 128)]
        if n == 1:
            return wgu.at[rows(f_ * 128, 128)]
        if n == 2:
            return wdn.at[:, rows(f_ * 128, 128)]
        return wo_all.at[rows(f_ * 128 + c * 64, 64)]

    def w_y(n, p, r, recv=False):
        m = ((y + r) % 4) * 2 + c
        if n == 0:
            src = (wq_in, wk_in, wv_in)[p].at[at(z * 32, 32, 32), rows(m * 128, 128)]
        elif n == 1:
            src = (wg_in, wu_in)[p].at[at(z * 32, 32, 32), at(window(m), FB, 128)]
        elif n == 2:
            src = wd_in.at[at(window(m) + z * 96, 96, 32), :]
        else:
            src = wo_in.at[at(c * 64 + z * 16, 16, 16)]
        dst = w_quarter(n, shard(r) if recv else f, z, p)
        return remote(src, dst, wy_s.at[n], wy_r.at[n, r - 1], dev(x, y + r, z, c))

    def w_z(n, r, dz, recv=False):
        src = w_quarter(n, shard(r), z)
        dst = w_quarter(n, shard(r), (z + 4 - dz) % 4) if recv else src
        return remote(src, dst, wz_s.at[n], wz_r.at[n, r - 1], dev(x, y, z + dz, c))

    def w_x(n, r, recv=False):
        src = w_rows(n, shard(r))
        dst = w_rows(n, ((y + 4 - r) % 4) * 2 + 1 - xl) if recv else src
        return remote(src, dst, wx_s.at[n], wx_r.at[n], x_to)

    def quarters(n, count):
        if n == 2:
            return wdn.at[pl.ds(0, 96 * count)] if count == 1 else wdn.at[pl.ds(0, 288), pl.ds(0, 128 * (count // 3))]
        return (wqkv, wgu, None, wo_all)[n].at[pl.ds(0, (32, 32, 0, 16)[n] * count)]

    def blocks(n, count):
        if n == 2:
            return wdn.at[:, pl.ds(0, 128 * count)]
        return (wqkv, wgu, None, wo_all)[n].at[pl.ds(0, (128, 128, 0, 64)[n] * count)]

    def w_ystart(n):
        for r in (1, 3, 2):
            for p in range(PARTS[n]):
                w_y(n, p, r).start()

    def w_own(n):
        own = wo_all.at[own_rows] if n == 3 else w_rows(n, f)
        pltpu.make_async_copy(own, own, sem_load.at[(0, 2, 3, 1)[n]]).wait()
        w_x(n, 0).start()

    def w_zstart(n):
        for r in (1, 3, 2):
            all_in(w_quarter(n, shard(r), z), wy_r.at[n, r - 1])
            for dz in (1, 3, 2):
                w_z(n, r, dz).start()

    def w_xstart(n):
        for r in (1, 3, 2):
            all_in(quarters(n, 3), wz_r.at[n, r - 1])
            w_x(n, r).start()
            if n == 3:
                wo_pass(2 * ((4 - r) % 4)).start()

    def w_finish(n):
        all_in(blocks(n, 4), wx_r.at[n])

    def wo_pass(n, recv=False):
        f_ = ((y + n // 2) % 4) * 2 + (xl + n % 2) % 2
        ref = wo_all.at[rows(f_ * 128 + ((1 - c) if recv else c) * 64, 64)]
        return remote(ref, ref, wp_s.at[0], wp_r.at[0], sibling)

    def wo_pass_x():
        all_in(blocks(3, 4), wx_r.at[3])
        for r in range(4):
            wo_pass(2 * ((4 - r) % 4) + 1).start()

    def wo_pass_finish():
        all_in(wo_all.at[pl.ds(0, 448)], wp_r.at[0])

    for n in (0, 3, 2, 1):
        w_ystart(n)
    w_own(0)

    def piece(buf, y_, c_):
        return buf.at[rows((((y_ + 4) % 4) * 2 + c_) * PIECE, PIECE)]

    def half(buf, y_, c_, h):
        return buf.at[rows((((y_ + 4) % 4) * 2 + c_) * PIECE + h * 64, 64)]

    def ag(buf, k, n, recv=False):
        if n in (0, 8):
            h = 0 if n == 0 else 1
            ref, to = (half(buf, y - 1, c, h) if recv else half(buf, y, c, h)), y_up
        elif n in (1, 9):
            h = 1 if n == 1 else 0
            ref, to = (half(buf, y + 1, c, h) if recv else half(buf, y, c, h)), y_dn
        elif n == 2:
            ref, to = (piece(buf, y, 1 - c) if recv else piece(buf, y, c)), sibling
        elif n == 3:
            ref, to = (half(buf, y - 2, c, 0) if recv else half(buf, y - 1, c, 0)), y_up
        elif n == 4:
            ref, to = (piece(buf, y - 1, 1 - c) if recv else piece(buf, y - 1, c)), sibling
        elif n == 5:
            ref, to = (half(buf, y + 2, c, 1) if recv else half(buf, y + 1, c, 1)), y_dn
        elif n == 6:
            ref, to = (piece(buf, y + 1, 1 - c) if recv else piece(buf, y + 1, c)), sibling
        else:
            ref, to = (piece(buf, y + 2, 1 - c) if recv else piece(buf, y + 2, c)), sibling
        return remote(ref, ref, ag_s.at[k], ag_r.at[k, (0, 0, 3, 2, 4, 2, 5, 6, 1, 1)[n]], to)

    def ag_start(buf, k):
        for n in (0, 1, 2, 8, 9):
            ag(buf, k, n).start()

    def ag_near(buf, k):
        all_in(buf.at[pl.ds(0, PIECE)], ag_r.at[k, 0])
        ag(buf, k, 3).start()
        ag(buf, k, 5).start()

    def ag_pass(buf, k):
        all_in(buf.at[pl.ds(0, PIECE)], ag_r.at[k, 1])
        ag(buf, k, 4).start()
        ag(buf, k, 6).start()

    def ag_far(buf, k):
        all_in(buf.at[pl.ds(0, PIECE)], ag_r.at[k, 2])
        ag(buf, k, 7).start()

    def ag_finish(buf, k):
        for n in (2, 4, 6, 7):
            ag(buf, k, n, True).wait_recv()

    def ag_run(buf, k, consume, after_pass=None, after_far=None):
        def step(i, carry):
            @pl.when(i == 0)
            def _():
                ag(buf, k, 2, True).wait_recv()

            @pl.when(i == 1)
            def _():
                ag_pass(buf, k)
                if after_pass is not None:
                    after_pass()
                ag(buf, k, 4, True).wait_recv()

            @pl.when(i == 2)
            def _():
                ag(buf, k, 6, True).wait_recv()
                ag_far(buf, k)

            @pl.when(i == 3)
            def _():
                if after_far is not None:
                    after_far()
                ag(buf, k, 7, True).wait_recv()

            consume((y + (3 * ((i * (i + 1)) // 2)) % 4) % 4)

            @pl.when(i == 0)
            def _():
                if k > 0:
                    ag_near(buf, k)

            return carry

        lax.fori_loop(0, 4, step, 0)

    def held(k):
        return part.at[1 if k == 2 else 0]

    def own_part(k, a):
        return held(k)[a, rows(c * PIECE, PIECE), :].astype(F32)

    def c_sib(k, a):
        src = held(k).at[a, rows((1 - c) * PIECE, PIECE)]
        return remote(src, sib.at[k, a], sib_ss.at[k], sib_rs.at[k, a], sibling)

    def c_far(k, n):
        return remote(far_s.at[k, pl.ds(64 * n, 64)], far_r.at[k, n], far_ss.at[k], far_rs.at[k], y_up if n == 0 else y_dn)

    def c_fin(k, n, h):
        cut = pl.ds(64 * h, 64)
        return remote(fin_s.at[k, n, cut], fin_r.at[k, n, cut], fin_ss.at[k], fin_rs.at[k], y_up if n == 0 else y_dn)

    def rs_put(k, a, value):
        held(k)[a] = value.astype(BF16)
        c_sib(k, a).start()

    def rs_pair(k, a):
        c_sib(k, a).wait_recv()
        return own_part(k, a) + sib[k, a].astype(F32)

    def rs_far(k):
        far_s[k] = rs_pair(k, (y + 2) % 4).astype(BF16)
        c_far(k, 0).start()
        c_far(k, 1).start()

    def rs_near(k, n):
        fin_s[k, n] = rs_pair(k, (y + 1 + 2 * n) % 4).astype(BF16)
        c_fin(k, n, 1 - n).start()

    def rs_mid(k):
        all_in(far_r.at[k], far_rs.at[k])
        for n in (0, 1):
            cut = pl.ds(64 * n, 64)
            fin_s[k, n, cut] = (fin_s[k, n, cut].astype(F32) + far_r[k, n].astype(F32)).astype(BF16)
            c_fin(k, n, n).start()

    def rs_finish(k):
        total = rs_pair(k, y)
        all_in(fin_r.at[k], fin_rs.at[k])
        return total + fin_r[k, 0].astype(F32) + fin_r[k, 1].astype(F32)

    w_zstart(0)
    all_in(vall.at[pl.ds(0, 7)], vec_r.at[0])
    all_sent(vall.at[pl.ds(0, 7)], vec_s.at[0])

    def gathered(row):
        return jnp.concatenate([vall[i, row : row + 1, :] for i in range(8)], axis=1)

    swap_wait(x_in, x_own, 0)
    x32 = x_own[...].astype(F32)
    normed_all[rows(j * PIECE, PIECE), :] = (x32 * rms_scale(x32) * gathered(0)).astype(BF16)
    ag_start(normed_all, 0)
    w_xstart(0)
    swap_start(cot_in, cot_own, 1)
    w_zstart(3)
    w_own(3)
    w_zstart(2)
    w_own(2)
    w_zstart(1)
    w_own(1)
    ag_near(normed_all, 0)
    for load in loads[7:]:
        load.wait()
    w_finish(0)

    doc = jnp.broadcast_to(doc_row, (8, D)).astype(F32).T[:, :1]
    feature = lax.broadcasted_iota(jnp.int32, (D, 128), 1)
    k_all[:, 128:] = jnp.where(
        feature == 0, OTHER_DOC * (1.0 - doc), jnp.where(feature == 1, OTHER_DOC * doc, 0.0)
    ).astype(BF16)
    q_more = jnp.where(feature == 0, doc, jnp.where(feature == 1, 1.0 - doc, 0.0)).astype(BF16)
    for i in range(4):
        for h in range(2):
            q_two[i, BLOCK * h : BLOCK * h + BLOCK, 128:] = q_more[BLOCK * i : BLOCK * i + BLOCK]

    def two_heads(value):
        first_head = lax.broadcasted_iota(jnp.int32, value.shape, 1) < HEAD_DIM
        return jnp.concatenate([jnp.where(first_head, value, 0.0), jnp.where(first_head, 0.0, value)], axis=0)

    def own_quarters(value):
        return jnp.concatenate([value[:HEAD_DIM, :BLOCK], value[HEAD_DIM:, BLOCK:]], axis=0)

    def project(yy):
        cut = rows(yy * BLOCK, BLOCK)
        lin = nn(normed_all[cut, :], wqkv[...])
        cos = cos_ref[cut, :]
        sin = sin_ref[cut, :]
        bias = vall[pl.ds(j, 1)][0]
        q_lin = lin[:, :128] + bias[2:3, :]
        k_lin = lin[:, 128:256] + bias[3:4, :]
        v_lin = lin[:, 256:] + bias[4:5, :]
        q = (q_lin * cos + half_turn(q_lin) * sin) * (0.125 * LOG2_E)
        k32 = k_lin * cos + half_turn(k_lin) * sin
        q_two[pl.ds(yy, 1), :, :128] = two_heads(q).astype(BF16)[None]
        k_all[cut, :128] = k32.astype(BF16)
        v_all[cut, :] = v_lin.astype(BF16)
        k_t[:, cut] = k32.T.astype(BF16)
        v_t[:, cut] = v_lin.T.astype(BF16)

    def cot_start():
        swap_wait(cot_in, cot_own, 1)
        cot_all[rows(j * PIECE, PIECE), :] = cot_own[...]
        ag_start(cot_all, 1)

    ag_run(normed_all, 0, project, lambda: w_xstart(3), cot_start)

    def attend(i):
        width = (i + 1) * BLOCK
        before = i * BLOCK
        cut = slice(before, width)
        scores = nt(k_all[:width, :], q_two[i])
        key_at = lax.broadcasted_iota(jnp.int32, (BLOCK, 2 * BLOCK), 0)
        query_at = lax.broadcasted_iota(jnp.int32, (BLOCK, 2 * BLOCK), 1) % BLOCK
        last = jnp.where(key_at <= query_at, scores[before:], NEG)
        top = jnp.max(last, axis=0, keepdims=True)
        if i > 0:
            top = jnp.maximum(top, jnp.max(scores[:before], axis=0, keepdims=True))
        weights = jnp.exp2(last - top)
        total = jnp.sum(weights, axis=0, keepdims=True)
        p_t[i, before:width, :] = weights.astype(BF16)
        if i > 0:
            weights = jnp.exp2(scores[:before] - top)
            total = total + jnp.sum(weights, axis=0, keepdims=True)
            p_t[i, :before, :] = weights.astype(BF16)
        inverse = 1.0 / total
        inv[i : i + 1, :] = inverse
        both = nn(v_t[:, :width], p_t[i, :width, :]) * inverse
        mixed_t[:, cut] = own_quarters(both)
        mixed[cut, :] = mixed_t[:, cut].T.astype(BF16)
        for m in (2 * i, 2 * i + 1):
            mix_start(m)

    def mix(m, sender):
        return remote(
            mixed.at[rows(m * PIECE, PIECE), :], mixed_own.at[:, rows(sender * 128, 128)],
            mx_s.at[0], mx_r.at[0], dev(x, m // 2, z, m % 2),
        )

    def mix_start(m):
        @pl.when(j != m)
        def _():
            mix(m, j).start()

        @pl.when(j == m)
        def _():
            mixed_own[:, rows(j * 128, 128)] = mixed[m * PIECE : (m + 1) * PIECE, :]

    w_xstart(2)
    attend(0)
    attend(1)
    w_xstart(1)
    attend(2)
    wo_pass_x()
    attend(3)
    ag_near(cot_all, 1)
    ag_pass(cot_all, 1)
    wo_pass_finish()
    all_in(mixed_own.at[:, pl.ds(0, 896)], mx_r.at[0])
    all_sent(mixed.at[pl.ds(0, 896)], mx_s.at[0])

    hidden[...] = x_own[...].astype(F32) + nn(mixed_own[...], wo_all[...])
    hid = hidden[...]
    mlp_all[rows(j * PIECE, PIECE), :] = (hid * rms_scale(hid) * gathered(1)).astype(BF16)
    ag_start(mlp_all, 2)
    ag_far(cot_all, 1)
    w_finish(2)
    ag_finish(cot_all, 1)

    def active_back(i, carry):
        cut = rows(i * BLOCK, BLOCK)
        g_act[cut, :] = nt(cot_all[cut, :], wdn[...])
        return carry

    lax.fori_loop(0, 4, active_back, 0)
    w_finish(1)

    unit = lax.broadcasted_iota(jnp.int32, (1, FB), 1)
    low_edge = 128 * (j // 7)
    high_edge = FB - 128 * ((j // 6) * (1 - j // 7))
    live = (unit >= low_edge) & (unit < high_edge)

    def feed(yy):
        cut = rows(yy * BLOCK, BLOCK)
        both = nn(mlp_all[cut, :], wgu[...])
        gate = both[:, :FB]
        up = both[:, FB:]
        sig = 1.0 / (1.0 + jnp.exp(-gate))
        silu = gate * sig
        back = jnp.where(live, g_act[cut, :], 0.0)
        act = jnp.where(live, silu * up, 0.0)
        active[cut, :] = act.astype(BF16)
        g_gu[cut, :FB] = (back * up * sig * (1.0 + gate * (1.0 - sig))).astype(BF16)
        g_gu[cut, FB:] = (back * silu).astype(BF16)
        rs_put(1, yy, nt(g_gu[cut, :], wgu[...]))

    ag_run(mlp_all, 2, feed)
    rs_far(1)

    terms = (dga, dgb, ddn, dqa, dqb, dwo)
    term_in = (ra, rb, rd, rqa, rqb, rw)
    halfway = (ha, hb, hd, hqa, hqb, hw)
    half_in = (sa, sb, sd, sqa, sqb, sw)

    def first(n, r):
        if n in (0, 3, 5):
            src, to = terms[n].at[(x + r) % 4], dev(x + r, y, z, c)
        else:
            src, to = terms[n].at[:, (z + r) % 4], dev(x, y, z + r, c)
        return remote(src, term_in[n].at[r - 1], f1_s.at[n], f1_r.at[n], to)

    def second(n, r):
        if n in (0, 3, 5):
            src, to = halfway[n].at[(z + r) % 4], dev(x, y, z + r, c)
        else:
            src, to = halfway[n].at[(x + r) % 4], dev(x + r, y, z, c)
        return remote(src, half_in[n].at[r - 1], f2_s.at[n], f2_r.at[n], to)

    def first_start(n):
        for r in (1, 3, 2):
            first(n, r).start()

    def first_sum(n):
        total = (terms[n][x] if n in (0, 3, 5) else terms[n][:, z]).astype(F32)
        all_in(term_in[n], f1_r.at[n])
        for r in (1, 3, 2):
            total = total + term_in[n][r - 1].astype(F32)
        halfway[n][...] = total.astype(BF16)
        for r in (1, 3, 2):
            second(n, r).start()

    def second_sum(n):
        total = halfway[n][z if n in (0, 3, 5) else x].astype(F32)
        all_in(half_in[n], f2_r.at[n])
        for r in (1, 3, 2):
            total = total + half_in[n][r - 1].astype(F32)
        return total.astype(BF16)

    def chunk(t, xl_):
        return (t % 2) * 2 + xl_, t // 2

    def grad_gu(i, carry):
        got = tn(mlp_all[:, rows(i * BLOCK, BLOCK)], g_gu[...]).astype(BF16)
        for xl_ in range(2):
            for t in range(8):
                x_, z_ = chunk(t, xl_)
                share = got[xl_ * 128 + t * 16 : xl_ * 128 + t * 16 + 16]
                dga[x_, z_, i] = share[:, :512]
                dgb[x_, z_, i] = share[:, 512:]
        return carry

    def grad_dn(i, carry):
        got = nn(active_t[...], cot_all[:, rows(i * BLOCK, BLOCK)]).astype(BF16)
        for xl_ in range(2):
            for t in range(8):
                x_, z_ = chunk(t, xl_)
                ddn[x_, z_, i] = got[t * 48 : t * 48 + 48, xl_ * 128 : xl_ * 128 + 128]
        return carry

    def grad_qkv(part_ref, base):
        def go(i, carry):
            got = tn(normed_all[:, rows((base + i) * BLOCK, BLOCK)], g_qkv[...]).astype(BF16)
            for xl_ in range(2):
                for t in range(8):
                    x_, z_ = chunk(t, xl_)
                    part_ref[x_, z_, i] = got[xl_ * 128 + t * 16 : xl_ * 128 + t * 16 + 16]
            return carry

        lax.fori_loop(0, 2, go, 0)

    def grad_wo():
        got = tn(mixed[...], branch_all[...]).astype(BF16)
        for h in range(2):
            for t in range(8):
                x_, z_ = chunk(t, (h + c) % 2)
                dwo[pl.ds(x_, 1), z_] = got[h * 64 : h * 64 + 64, t * 128 : t * 128 + 128][None]

    lax.fori_loop(0, 4, grad_gu, 0)
    rs_near(1, 0)
    rs_near(1, 1)
    first_start(1)
    first_start(0)
    rs_mid(1)
    active_t[...] = active[...].T
    lax.fori_loop(0, 4, grad_dn, 0)
    first_start(2)

    grad = rs_finish(1)
    hid = hidden[...]
    scale = rms_scale(hid)
    scaled = grad * gathered(1)
    back = scale * scaled - hid * (scale * scale * scale) * jnp.mean(scaled * hid, axis=-1, keepdims=True)
    g_hidden[...] = cot_own[...].astype(F32) + back
    branch_all[rows(j * PIECE, PIECE), :] = g_hidden[...].astype(BF16)

    def unmix_term(i, carry):
        cut = rows(i * BLOCK, BLOCK)
        mixed_grad[:, cut] = nt(branch_all[rows(j * PIECE, PIECE), :], wo_all[cut, :]).astype(BF16)
        return carry

    lax.fori_loop(0, 4, unmix_term, 0)
    g_mixed[rows(j * PIECE, PIECE), :] = mixed_grad[:, rows(j * 128, 128)]

    def unmix(m, sender):
        return remote(
            mixed_grad.at[:, rows(m * 128, 128)], g_mixed.at[rows(sender * PIECE, PIECE), :],
            um_s.at[0], um_r.at[0], dev(x, m // 2, z, m % 2),
        )

    def unmix_start(r, carry):
        unmix((j + r) % 8, j).start()
        return carry

    lax.fori_loop(1, 8, unmix_start, 0)
    gain_two = jnp.sum(grad * hid * scale, axis=0, keepdims=True)
    gk_acc[...] = jnp.zeros_like(gk_acc)
    gv_acc[...] = jnp.zeros_like(gv_acc)

    def output_term(i, carry):
        rs_put(2, i, nn(active[rows(i * BLOCK, BLOCK), :], wdn[...]))
        return carry

    lax.fori_loop(0, 4, output_term, 0)
    first_sum(1)
    first_sum(0)
    all_in(g_mixed.at[pl.ds(0, 896)], um_r.at[0])
    all_sent(mixed_grad.at[:, pl.ds(0, 896)], um_s.at[0])
    all_sent(sib.at[1], sib_ss.at[1])
    ag_start(branch_all, 3)

    def along_y(n, r, recv=False):
        src = (sum_gu, sum_dn, sum_qkv)[n].at[(y + r) % 4]
        dst = (all_gu, all_dn, all_qkv)[n].at[place, c, (y + 4 - r) % 4 if recv else y]
        return remote(src, dst, ya_s.at[n], ya_r.at[n], dev(x, y + r, z, c))

    def share(n):
        total, every = ((sum_gu, all_gu), (sum_dn, all_dn), (sum_qkv, all_qkv))[n]
        if n == 0:
            total[:, :, :512] = second_sum(0)
            total[:, :, 512:] = second_sum(1)
        elif n == 1:
            total[...] = second_sum(2)
        else:
            total[:2] = second_sum(3)
            total[2:] = second_sum(4)
        for r in (1, 3, 2):
            along_y(n, r).start()
        every[place, c, y] = total[y]

    arrays = (all_gu, all_dn, all_wo, all_qkv)

    def spot(n, r, c_):
        return arrays[n].at[((z + 4 - r % 4) % 4) * 2 + (xh + r // 4) % 2, c_]

    def gd(n, r, recv=False):
        if n == 2:
            ref = spot(n, r if recv else 0, c)
            return remote(ref, ref, gd_s.at[n - 2], gd_r.at[3 if n == 2 else (0, 1, 1, 1, 0, 2, 2, 2)[r]], dev(x + 2 * (r // 4), y, z + r % 4, c))
        ref = spot(n, r if recv else 4 * (r // 5), c)
        return remote(ref, ref, gd_s.at[n - 2], gd_r.at[3 if n == 2 else (0, 1, 1, 1, 0, 2, 2, 2)[r]], dev(x + 2 * (r == 4), y, z + r % 4, c))

    def gp(n, r, recv=False):
        ref = spot(n, r, (1 - c) if recv else c)
        return remote(ref, ref, gp_s.at[n - 2], gp_r.at[n - 2], sibling)

    def pair(n, z_, c_):
        return arrays[n].at[pl.ds(((z_ + 4) % 4) * 2, 2), c_]

    def single(n, z_, h):
        return arrays[n].at[pl.ds(((z_ + 4) % 4) * 2 + h, 1), c]

    def ring(n, k, recv=False):
        if k == 0:
            ref, to = single(n, z, (1 - xh) if recv else xh), dev(x + 2, y, z, c)
        elif k == 1:
            ref, to = pair(n, z - 1 if recv else z, c), dev(x, y, z + 1, c)
        elif k == 2:
            ref, to = pair(n, z + 1 if recv else z, c), dev(x, y, z + 3, c)
        elif k == 3:
            ref, to = single(n, z - 2 if recv else z - 1, 0), dev(x, y, z + 1, c)
        elif k == 4:
            ref, to = single(n, z + 2 if recv else z + 1, 1), dev(x, y, z + 3, c)
        else:
            ref, to = pair(n, z + (k - 5), (1 - c) if recv else c), sibling
        return remote(ref, ref, rg_s.at[n, k // 5], rg_r.at[n, (0, 1, 1, 2, 2, 3, 3, 3, 3)[k]], to)

    def ring_one(n):
        all_in(arrays[n].at[place, c, pl.ds(0, 3)], ya_r.at[n])
        ring(n, 0).start()

    def ring_two(n):
        ring(n, 0, True).wait_recv()
        for k in (1, 2, 5):
            ring(n, k).start()

    def ring_three(n):
        all_in(arrays[n].at[pl.ds(0, 4), c], rg_r.at[n, 1])
        for k in (3, 4, 8, 6):
            ring(n, k).start()

    def ring_four(n):
        all_in(arrays[n].at[pl.ds(0, 2), c], rg_r.at[n, 2])
        ring(n, 7).start()

    def ring_five(n):
        all_in(arrays[n].at[:, c], rg_r.at[n, 3])

    def spread_start(n):
        if n != 2:
            all_in(arrays[n].at[place, c, pl.ds(0, 3)], ya_r.at[min(n, 2)])
        for r in (6, 4, 5, 7, 2, 1, 3) if n == 2 else (4, 2, 1, 3):
            gd(n, r).start()
        gp(n, 0).start()

    def spread_next(n):
        if n == 3:
            gd(n, 4, True).wait_recv()
            for r in (6, 5, 7):
                gd(n, r).start()
            gp(n, 4).start()

    def spread_pass(n):
        if n == 2:
            all_in(arrays[n].at[pl.ds(0, 7), c], gd_r.at[3])
            for r in range(1, 8):
                gp(n, r).start()
        else:
            for i, steps in ((1, (1, 3, 2)), (2, (5, 7, 6))):
                all_in(arrays[n].at[pl.ds(0, 3), c], gd_r.at[i])
                for r in steps:
                    gp(n, r).start()

    def spread_finish(n):
        all_in(arrays[n].at[:, c], gp_r.at[n - 2])

    def unturn(value, cut):
        value = value.astype(BF16).astype(F32)
        return (value * cos_ref[cut, :] - half_turn(value) * sin_ref[cut, :]).astype(BF16)

    def attend_back(i):
        width = (i + 1) * BLOCK
        cut = slice(i * BLOCK, width)
        inverse = inv[i : i + 1, :]
        grad_t = g_mixed[cut, :].astype(F32).T
        scaled = jnp.concatenate([grad_t[:HEAD_DIM] * inverse[:, :BLOCK], grad_t[HEAD_DIM:] * inverse[:, BLOCK:]], axis=0)
        scaled = scaled.astype(BF16).astype(F32)
        products = scaled * mixed_t[:, cut]
        delta = jnp.concatenate(
            [jnp.sum(products[:HEAD_DIM], axis=0, keepdims=True), jnp.sum(products[HEAD_DIM:], axis=0, keepdims=True)], axis=1
        )
        grad_two = two_heads(scaled.T).astype(BF16)
        weights = p_t[i, :width, :]
        gv_acc[:width, :] += nn(weights, grad_two)
        g_probs = nt(v_all[:width, :], grad_two)
        g_scores = (weights.astype(F32) * (g_probs - delta)).astype(BF16)
        gk_acc[:width, :] += nn(g_scores, q_two[i, :, :128])
        g_query = own_quarters(nn(k_t[:, :width], g_scores)) * 0.125
        g_qkv[cut, :128] = unturn(g_query.T, cut)

    def block_back(i):
        cut = slice(i * BLOCK, (i + 1) * BLOCK)
        attend_back(i)
        g_qkv[cut, 128:256] = unturn(gk_acc[cut, :] * (1.0 / LOG2_E), cut)
        g_qkv[cut, 256:] = gv_acc[cut, :].astype(BF16)
        rs_put(3, i, nt(g_qkv[cut, :], wqkv[...]))

    block_back(3)
    block_back(2)
    share(0)
    first_sum(2)
    ag_near(branch_all, 3)
    block_back(1)
    block_back(0)
    rs_far(3)
    grad_qkv(dqb, 2)
    first_start(4)
    ring_one(0)
    grad_qkv(dqa, 0)
    first_start(3)
    rs_near(3, 0)
    rs_near(3, 1)
    ag_pass(branch_all, 3)
    share(1)
    ag_far(branch_all, 3)
    rs_mid(3)
    ring_two(0)
    first_sum(4)
    first_sum(3)
    ring_one(1)
    rs_far(2)
    ag_finish(branch_all, 3)
    grad_wo()
    first_start(5)
    rs_near(2, 0)
    rs_near(2, 1)

    grad = rs_finish(3)
    scale = rms_scale(x32)
    scaled = grad * gathered(0)
    back = scale * scaled - x32 * (scale * scale * scale) * jnp.mean(scaled * x32, axis=-1, keepdims=True)
    ig_send[...] = (g_hidden[...] + back).astype(BF16)
    swap_start(ig_send, in_grad, 3)
    share(2)
    ring_two(1)
    first_sum(5)

    gain_one = jnp.sum(grad * x32 * scale, axis=0, keepdims=True)
    vs[...] = jnp.zeros_like(vs)
    for i in range(8):
        vs[i, 0:1, :] = gain_one[:, 128 * i : 128 * i + 128]
        vs[i, 1:2, :] = gain_two[:, 128 * i : 128 * i + 128]
    bias_sum = jnp.sum(g_qkv[...].astype(F32), axis=0, keepdims=True)
    for i in range(3):
        vs[pl.ds(j, 1), 2 + i : 3 + i, :] = bias_sum[:, 128 * i : 128 * i + 128][None]

    def v1_copy(r):
        return remote(vs.at[(f + r) % 8], vr.at[r - 1], v1_ss.at[0], v1_rs.at[0], (s, (f + r) % 8))

    def v1_start(r, carry):
        v1_copy(r).start()
        return carry

    lax.fori_loop(1, 8, v1_start, 0)
    ring_three(0)
    spread_start(3)
    ring_three(1)
    rs_mid(2)
    wo_send[...] = second_sum(5)
    swap_start(wo_send, all_wo.at[place, (c + moves) % 2], 4)
    all_in(vr, v1_rs.at[0])
    all_sent(vr, v1_ss.at[0])
    v2s[...] = jnp.sum(vr[...], axis=0) + vs[pl.ds(f, 1)][0]

    def v2_copy(r):
        to = dev(x + 2 * (r // 4), y, z + r % 4, c)
        return remote(v2s, v2r.at[r - 1], v2_ss.at[0], v2_rs.at[0], to)

    def v2_start(r, carry):
        v2_copy(r).start()
        return carry

    lax.fori_loop(1, 8, v2_start, 0)
    spread_next(3)
    swap_wait(wo_send, all_wo.at[place, c], 4)
    spread_start(2)
    lo_send[...] = (hidden[...] + rs_finish(2)).astype(BF16)
    swap_start(lo_send, layer_out, 2)
    all_in(v2r, v2_rs.at[0])
    all_sent(v2r, v2_ss.at[0])
    v3s[...] = jnp.sum(v2r[...], axis=0) + v2s[...]
    v3_copy = remote(v3s, v3r, v3_ss.at[0], v3_rs.at[0], sibling)
    v3_copy.start()
    ring_four(0)
    spread_pass(3)
    ring_four(1)
    spread_next(2)
    spread_pass(2)
    v3_copy.wait()
    vec_out[...] = v3s[...] + v3r[...]
    swap_wait(lo_send, layer_out, 2)
    swap_wait(ig_send, in_grad, 3)
    for n in (0, 1):
        ring_five(n)
    for n in (3, 2):
        spread_finish(n)

    for n in range(4):
        all_sent(quarters(n, 3), wy_s.at[n])
        all_sent(quarters(n, 9), wz_s.at[n])
        all_sent(blocks(n, 4), wx_s.at[n])
    all_sent(wo_all.at[pl.ds(0, 448)], wp_s.at[0])
    for k, buf in enumerate((normed_all, cot_all, mlp_all, branch_all)):
        all_sent(buf.at[pl.ds(0, 896)], ag_s.at[k])
    for k in range(1, 4):
        if k > 1:
            all_sent(sib.at[k], sib_ss.at[k])
        all_sent(far_s.at[k], far_ss.at[k])
        all_sent(fin_s.at[k], fin_ss.at[k])
    for n in range(6):
        all_sent(term_in[n], f1_s.at[n])
        all_sent(half_in[n], f2_s.at[n])
    for n in (0, 1, 3):
        all_sent(arrays[n].at[place, c, pl.ds(0, 3)], ya_s.at[min(n, 2)])
    for n in (0, 1):
        all_sent(arrays[n].at[pl.ds(0, 7), c], rg_s.at[n, 0])
        all_sent(arrays[n].at[:, c], rg_s.at[n, 1])
    for n in (2, 3):
        all_sent(arrays[n].at[pl.ds(0, 7), c], gd_s.at[n - 2])
        all_sent(arrays[n].at[:, c], gp_s.at[n - 2])


def fused_layer(*args):
    def vmem(*shape, dtype=BF16):
        return pltpu.VMEM(shape, dtype)

    def dma(*shape):
        return pltpu.SemaphoreType.DMA(shape)

    full = vmem(D, D)
    shares = ((4, 16, 512), (4, 16, 256), (4, 48, 128), (2, 16, FB), (2, 16, FB), (64, 128))
    scratch = [
        vmem(D, 128, dtype=F32), vmem(D, 128, dtype=F32), vmem(8, 128, dtype=F32),
        vmem(PIECE, D), vmem(PIECE, D), vmem(PIECE, D, dtype=F32), vmem(PIECE, D, dtype=F32),
        full, vmem(D, FB), vmem(D, 2 * FB), vmem(FB, D), vmem(8, 8, 128, dtype=F32),
        full, full, full, full,
        vmem(4, 2 * BLOCK, 256), vmem(D, 256), vmem(D, 128), vmem(128, D), vmem(128, D),
        vmem(4, D, 2 * BLOCK), vmem(8, 2 * BLOCK, dtype=F32), vmem(128, D, dtype=F32), vmem(D, 128), vmem(PIECE, D), vmem(PIECE, D),
        vmem(D, FB, dtype=F32), vmem(D, FB), vmem(FB, D), vmem(D, 2 * FB), vmem(D, 128),
        vmem(D, 128, dtype=F32), vmem(D, 128, dtype=F32), vmem(D, FB),
        vmem(2, 4, BLOCK, D), vmem(4, 4, PIECE, D), vmem(4, PIECE, D), vmem(4, 2, 64, D), vmem(4, 2, PIECE, D), vmem(4, 2, PIECE, D),
        *(vmem(4, 4, *dims) for dims in shares),
        *(vmem(3, 4, *dims) for dims in shares),
        *(vmem(4, *dims) for dims in shares),
        *(vmem(3, *dims) for dims in shares),
        vmem(64, 128), vmem(4, 16, 2 * FB), vmem(4, 48, 128), vmem(4, 16, FB),
        vmem(PIECE, D), vmem(PIECE, D),
        vmem(8, 8, 128, dtype=F32), vmem(7, 8, 128, dtype=F32), vmem(8, 128, dtype=F32), vmem(7, 8, 128, dtype=F32),
        vmem(8, 128, dtype=F32), vmem(8, 128, dtype=F32),
        dma(6), dma(5), dma(5), dma(1), dma(1), dma(4), dma(4, 3), dma(4), dma(4, 3), dma(4), dma(4),
        dma(1), dma(1), dma(1), dma(1), dma(1), dma(1), dma(4), dma(4, 7),
        dma(4), dma(4, 4), dma(4), dma(4), dma(4), dma(4),
        dma(6), dma(6), dma(6), dma(6), dma(3), dma(3), dma(2, 2), dma(2, 4), dma(2), dma(4), dma(2), dma(2),
        dma(1), dma(1), dma(1), dma(1), dma(1), dma(1),
    ]
    anywhere = pl.BlockSpec(memory_space=pl.ANY)
    inside = pl.BlockSpec(memory_space=pltpu.VMEM)

    def out(*shape, dtype=BF16):
        return pltpu.VMEM(shape, dtype)

    return pl.pallas_call(
        layer_kernel,
        out_shape=(
            out(PIECE, D), out(PIECE, D), out(8, 2, 4, 16, 2 * FB), out(8, 2, 4, 48, 128), out(8, 2, 64, 128),
            out(8, 2, 4, 16, FB), out(8, 128, dtype=F32),
        ),
        in_specs=[anywhere] * 11 + [inside] * 6,
        out_specs=[inside] * 7,
        scratch_shapes=scratch,
        compiler_params=pltpu.CompilerParams(
            collective_id=0, has_side_effects=True, vmem_limit_bytes=57 * 1024 * 1024
        ),
        name="layer",
    )(*args)


def spread_kernel(
    lo_in, ig_in, gu, dn, wo, qkv, vec,
    lo, ig, d_gain_a, d_q, d_k, d_v, d_bq, d_bk, d_bv, d_o, d_gain_m, d_gate, d_up, d_down,
    ig_v, q_v, k_v, v_v, o_v, gate_v, up_v, down_v, sems,
):
    stores = []

    def store(src, dst):
        copy = pltpu.make_async_copy(src, dst, sems.at[len(stores)])
        copy.start()
        stores.append(copy)

    for ref, row in ((d_gain_a, 0), (d_gain_m, 1), (d_bq, 2), (d_bk, 3), (d_bv, 4)):
        ref[...] = vec[row : row + 1, :]
    store(lo_in, lo)
    for m in range(8):
        first = 128 if m == 7 else 0
        count = 256 if m >= 6 else FB
        start = min(m, 6) * FB + (256 if m == 7 else 0)
        for t in range(8):
            low, high = max(48 * t, first), min(48 * t + 48, first + count)
            if low < high:
                down_v[start + low - first : start + high - first, :] = dn[
                    t, m % 2, m // 2, low - 48 * t : high - 48 * t, :
                ].astype(F32)
    store(down_v, d_down)
    for ref, off, dst in ((gate_v, 0, d_gate), (up_v, FB, d_up)):
        for m in range(8):
            first = 128 if m == 7 else 0
            count = 256 if m >= 6 else FB
            start = min(m, 6) * FB + (256 if m == 7 else 0)
            for t in range(8):
                cut = slice(16 * t, 16 * t + 16)
                ref[cut, start : start + count] = gu[t, m % 2, m // 2, :, off + first : off + first + count].astype(F32)
        store(ref, dst)
    for i, (ref, dst) in enumerate(((q_v, d_q), (k_v, d_k), (v_v, d_v))):
        for t in range(8):
            for m in range(8):
                ref[16 * t : 16 * t + 16, 128 * m : 128 * m + 128] = qkv[
                    t, m % 2, m // 2, :, 128 * i : 128 * i + 128
                ].astype(F32)
        store(ref, dst)
    flip = lax.axis_index("fsdp") % 2
    for t in range(8):
        for core in range(2):
            to = pl.ds(pl.multiple_of(64 * ((core + flip) % 2), 64), 64)
            o_v[to, 128 * t : 128 * t + 128] = wo[t, core].astype(F32)
    store(o_v, d_o)
    ig_v[...] = ig_in[...].astype(F32)
    store(ig_v, ig)
    for copy in stores:
        copy.wait()


def spread(*args):
    def out(*shape, dtype=F32):
        return jax.ShapeDtypeStruct(shape, dtype)

    inside = pl.BlockSpec(memory_space=pltpu.VMEM)
    anywhere = pl.BlockSpec(memory_space=pl.ANY)
    vec, square, wide, tall = out(1, 128), out(128, D), out(128, 2816), out(2816, 128)
    return pl.pallas_call(
        spread_kernel,
        out_shape=(
            out(PIECE, D, dtype=BF16), out(PIECE, D), vec, square, square, square, vec, vec, vec,
            square, vec, wide, wide, tall,
        ),
        in_specs=[inside] * 7,
        out_specs=[anywhere, anywhere, inside, anywhere, anywhere, anywhere, inside, inside, inside]
        + [anywhere, inside, anywhere, anywhere, anywhere],
        scratch_shapes=[pltpu.VMEM(o.shape, o.dtype) for o in (square,) * 5 + (wide, wide, tall)]
        + [pltpu.SemaphoreType.DMA((9,))],
        compiler_params=pltpu.CompilerParams(vmem_limit_bytes=24 * 1024 * 1024),
        name="spread",
    )(*args)


def rotary_tables():
    exponent = np.arange(HEAD_DIM // 2, dtype=np.float32) * np.float32(2.0 / HEAD_DIM)
    inverse = np.exp(np.float32(-math.log(THETA)) * exponent)
    angles = np.arange(D, dtype=np.float32)[:, None] * inverse
    cos, sin = np.cos(angles), np.sin(angles)
    return np.concatenate([cos] * 4, axis=1), np.concatenate([-sin, sin] * 2, axis=1)


def per_device(
    inputs, doc_ids, positions, attn_gain, query_weight, key_weight, value_weight,
    query_bias, key_bias, value_bias, out_weight, mlp_gain, gate_weight, up_weight,
    down_weight, cotangent,
):
    del positions
    cos, sin = rotary_tables()
    vectors = [v.reshape(1, 128) for v in (attn_gain, mlp_gain, query_bias, key_bias, value_bias)]
    blocks = fused_layer(
        inputs.reshape(PIECE, D), cotangent.reshape(PIECE, D),
        query_weight, key_weight, value_weight, out_weight, gate_weight, up_weight, down_weight,
        jnp.asarray(cos), jnp.asarray(sin), *vectors, doc_ids,
    )
    outs = list(spread(*blocks))
    outs[0] = outs[0].reshape(inputs.shape)
    outs[1] = outs[1].reshape(inputs.shape)
    return tuple(o.reshape(128) if o.shape == (1, 128) else o for o in outs)


def solution(mesh):
    rows_spec = P("fsdp", None)
    act = P("seq", "fsdp", None)
    vec = P("fsdp")
    return jax.shard_map(
        per_device,
        mesh=mesh,
        in_specs=(
            act, P(), P("seq", "fsdp"), vec, rows_spec, rows_spec, rows_spec, vec, vec, vec,
            rows_spec, vec, rows_spec, rows_spec, P(None, "fsdp"), act,
        ),
        out_specs=(
            act, act, vec, rows_spec, rows_spec, rows_spec, vec, vec, vec, rows_spec, vec,
            rows_spec, rows_spec, P(None, "fsdp"),
        ),
        check_vma=False,
    )
```

```python
import math

import jax
import jax.numpy as jnp
import numpy as np
from jax import lax
from jax.experimental import pallas as pl
from jax.experimental.pallas import tpu as pltpu
from jax.sharding import PartitionSpec as P

MESH = pl.DeviceIdType.MESH
HEAD_DIM = 64
EPS = 1e-06
THETA = 1000000.0
NEG = -1000000000.0
OTHER_DOC = -(2.0**30)
LOG2_E = math.log2(math.e)
D = 1024
PIECE = 128
BLOCK = 256
FB = 384
F32 = jnp.float32
BF16 = jnp.bfloat16


def nn(a, b):
    return lax.dot_general(a, b, (((1,), (0,)), ((), ())), preferred_element_type=F32)


def nt(a, b):
    return lax.dot_general(a, b, (((1,), (1,)), ((), ())), preferred_element_type=F32)


def tn(a, b):
    return lax.dot_general(a, b, (((0,), (0,)), ((), ())), preferred_element_type=F32)


def rms_scale(value):
    return lax.rsqrt(jnp.mean(value * value, axis=-1, keepdims=True) + EPS)


def rows(start, size):
    return pl.ds(pl.multiple_of(start, size), size)


def half_turn(value):
    lane = lax.broadcasted_iota(jnp.int32, value.shape, 1)
    ahead = pltpu.roll(value, 96, 1)
    behind = pltpu.roll(value, 32, 1)
    return jnp.where(lane % 64 < 32, ahead, behind)


def layer_kernel(
    x_in, cot_in, wq_in, wk_in, wv_in, wo_in, wg_in, wu_in, wd_in, cos_in, sin_in,
    gain_a, gain_m, bias_q, bias_k, bias_v, docs,
    layer_out, in_grad, all_gu, all_dn, all_wo, all_qkv, vec_out,
    cos_ref, sin_ref, vec_in,
    x_own, cot_own, hidden, g_hidden, wo_all, wqkv, wgu, wdn, vall,
    normed_all, cot_all, mlp_all, branch_all,
    q_two, k_all, v_all, k_t, v_t, p_t, inv, mixed_t, mixed, mixed_own, mixed_grad,
    g_act, active, active_t, g_gu, g_mixed, gk_acc, gv_acc, g_qkv,
    part, sib, far_s, far_r, fin_s, fin_r,
    dga, dgb, ddn, dqa, dqb, dwo, ra, rb, rd, rqa, rqb, rw, ha, hb, hd, hqa, hqb, hw, sa, sb, sd, sqa, sqb, sw, wo_send, sum_gu, sum_dn, sum_qkv,
    lo_send, ig_send,
    vs, vr, v2s, v2r, v3s, v3r,
    sem_load, swap_s, swap_r, vec_s, vec_r, wy_s, wy_r, wz_s, wz_r, wx_s, wx_r, wp_s, wp_r, mx_s, mx_r, um_s, um_r, ag_s, ag_r,
    sib_ss, sib_rs, far_ss, far_rs, fin_ss, fin_rs,
    f1_s, f1_r, f2_s, f2_r, ya_s, ya_r, rg_s, rg_r, gd_s, gd_r, gp_s, gp_r, v1_ss, v1_rs, v2_ss, v2_rs, v3_ss, v3_rs,
):
    s = lax.axis_index("seq")
    f = lax.axis_index("fsdp")
    xh = s // 8
    z = (s % 8) // 2
    c = s % 2
    y = f // 2
    xl = f % 2
    x = xh * 2 + xl
    j = y * 2 + c
    place = z * 2 + xh

    def dev(x_, y_, z_, c_):
        x_, y_, z_ = (x_ + 4) % 4, (y_ + 4) % 4, (z_ + 4) % 4
        return ((x_ // 2) * 8 + z_ * 2 + c_, y_ * 2 + x_ % 2)

    sibling = dev(x, y, z, 1 - c)
    y_up = dev(x, y + 1, z, c)
    y_dn = dev(x, y + 3, z, c)
    moves = (c + xl) % 2
    partner = dev(xh * 2 + 1 - xl, y, z, 1 - c)
    x_to = dev(x + 1 + 2 * c, y, z, c)

    def window(m):
        return (3 * m - 2 * (m // 7)) * 128

    def remote(src, dst, ss, rs, to):
        return pltpu.make_async_remote_copy(
            src_ref=src, dst_ref=dst, send_sem=ss, recv_sem=rs, device_id=to, device_id_type=MESH
        )

    def all_in(ref, sem):
        remote(ref, ref, sem, sem, sibling).wait_recv()

    def all_sent(ref, sem):
        remote(ref, ref, sem, sem, sibling).wait_send()

    def at(start, size, unit):
        return pl.ds(pl.multiple_of(start, unit), size)

    own_rows = rows(f * 128, 128)
    own_win = at(window(j), FB, 128)
    loads = [
        pltpu.make_async_copy(wq_in.at[:, rows(j * 128, 128)], wqkv.at[own_rows, pl.ds(0, 128)], sem_load.at[0]),
        pltpu.make_async_copy(wk_in.at[:, rows(j * 128, 128)], wqkv.at[own_rows, pl.ds(128, 128)], sem_load.at[0]),
        pltpu.make_async_copy(wv_in.at[:, rows(j * 128, 128)], wqkv.at[own_rows, pl.ds(256, 128)], sem_load.at[0]),
        pltpu.make_async_copy(wo_in, wo_all.at[own_rows], sem_load.at[1]),
        pltpu.make_async_copy(wg_in.at[:, own_win], wgu.at[own_rows, pl.ds(0, FB)], sem_load.at[2]),
        pltpu.make_async_copy(wu_in.at[:, own_win], wgu.at[own_rows, pl.ds(FB, FB)], sem_load.at[2]),
        pltpu.make_async_copy(wd_in.at[own_win, :], wdn.at[:, own_rows], sem_load.at[3]),
        pltpu.make_async_copy(cos_in, cos_ref, sem_load.at[4]),
        pltpu.make_async_copy(sin_in, sin_ref, sem_load.at[5]),
    ]
    for load in loads:
        load.start()

    barrier = pltpu.get_barrier_semaphore()

    def greet(to):
        pl.semaphore_signal(barrier, inc=1, device_id=to, device_id_type=MESH)

    def greet_near(r, carry):
        greet(dev(x + r, y, z, c))
        greet(dev(x, y, z + r, c))
        greet(dev(x + 2, y, z + r, c))
        return carry

    def greet_fsdp(r, carry):
        greet((s, (f + r) % 8))
        return carry

    def greet_cross(r, carry):
        greet(dev(x, y + r, z, 1 - c))
        return carry

    lax.fori_loop(1, 4, greet_near, 0)
    lax.fori_loop(1, 8, greet_fsdp, 0)
    lax.fori_loop(0, 4, greet_cross, 0)

    @pl.when(moves == 1)
    def _():
        greet(partner)
        pl.semaphore_wait(barrier, 21)

    @pl.when(moves == 0)
    def _():
        pl.semaphore_wait(barrier, 20)

    def swap_start(src, dst, n):
        @pl.when(moves == 1)
        def _():
            remote(src, dst, swap_s.at[n], swap_r.at[n], partner).start()

        @pl.when(moves == 0)
        def _():
            pltpu.make_async_copy(src, dst, swap_r.at[n]).start()

    def swap_wait(src, dst, n):
        @pl.when(moves == 1)
        def _():
            remote(src, dst, swap_s.at[n], swap_r.at[n], partner).wait()

        @pl.when(moves == 0)
        def _():
            pltpu.make_async_copy(src, dst, swap_r.at[n]).wait()

    def vec_copy(r):
        return remote(vec_in, vall.at[f], vec_s.at[0], vec_r.at[0], (s, (f + r) % 8))

    def vec_start(r, carry):
        vec_copy(r).start()
        return carry

    vec_in[...] = jnp.zeros_like(vec_in)
    for i, ref in enumerate((gain_a, gain_m, bias_q, bias_k, bias_v)):
        vec_in[i : i + 1, :] = ref[...].astype(F32)
    lax.fori_loop(1, 8, vec_start, 0)
    swap_start(x_in, x_own, 0)
    vall[pl.ds(f, 1)] = vec_in[...][None]
    doc_row = docs[pl.ds(xh * 8 + z * 2 + xl, 1), :]

    PARTS = (3, 2, 1, 1)

    def shard(r):
        return ((y + 4 - r) % 4) * 2 + xl

    def w_quarter(n, f_, q, p=None):
        if n == 0:
            return wqkv.at[at(f_ * 128 + q * 32, 32, 32), slice(None) if p is None else pl.ds(p * 128, 128)]
        if n == 1:
            return wgu.at[at(f_ * 128 + q * 32, 32, 32), slice(None) if p is None else pl.ds(p * FB, FB)]
        if n == 2:
            return wdn.at[at(q * 96, 96, 32), rows(f_ * 128, 128)]
        return wo_all.at[at(f_ * 128 + c * 64 + q * 16, 16, 16)]

    def w_rows(n, f_):
        if n == 0:
            return wqkv.at[rows(f_ * 128, 128)]
        if n == 1:
            return wgu.at[rows(f_ * 128, 128)]
        if n == 2:
            return wdn.at[:, rows(f_ * 128, 128)]
        return wo_all.at[rows(f_ * 128 + c * 64, 64)]

    def w_y(n, p, r, recv=False):
        m = ((y + r) % 4) * 2 + c
        if n == 0:
            src = (wq_in, wk_in, wv_in)[p].at[at(z * 32, 32, 32), rows(m * 128, 128)]
        elif n == 1:
            src = (wg_in, wu_in)[p].at[at(z * 32, 32, 32), at(window(m), FB, 128)]
        elif n == 2:
            src = wd_in.at[at(window(m) + z * 96, 96, 32), :]
        else:
            src = wo_in.at[at(c * 64 + z * 16, 16, 16)]
        dst = w_quarter(n, shard(r) if recv else f, z, p)
        return remote(src, dst, wy_s.at[0], wy_r.at[r - 1 if n == 0 else n + 2], dev(x, y + r, z, c))

    def w_z(n, r, dz, recv=False):
        src = w_quarter(n, shard(r), z)
        dst = w_quarter(n, shard(r), (z + 4 - dz) % 4) if recv else src
        return remote(src, dst, wz_s.at[0], wz_r.at[r - 1 if n == 0 else n + 2], dev(x, y, z + dz, c))

    def w_x(n, r, recv=False):
        src = w_rows(n, shard(r))
        dst = w_rows(n, ((y + 4 - r) % 4) * 2 + 1 - xl) if recv else src
        return remote(src, dst, wx_s.at[0], wx_r.at[n], x_to)

    def quarters(n, count):
        if n == 2:
            return wdn.at[pl.ds(0, 96 * count)] if count == 1 else wdn.at[pl.ds(0, 288), pl.ds(0, 128 * (count // 3))]
        return (wqkv, wgu, None, wo_all)[n].at[pl.ds(0, (32, 32, 0, 16)[n] * count)]

    def blocks(n, count):
        if n == 2:
            return wdn.at[:, pl.ds(0, 128 * count)]
        return (wqkv, wgu, None, wo_all)[n].at[pl.ds(0, (128, 128, 0, 64)[n] * count)]

    def w_ystart(n):
        for r in (1, 3, 2):
            for p in range(PARTS[n]):
                w_y(n, p, r).start()

    def w_own(n):
        own = wo_all.at[own_rows] if n == 3 else w_rows(n, f)
        pltpu.make_async_copy(own, own, sem_load.at[(0, 2, 3, 1)[n]]).wait()
        w_x(n, 0).start()

    def w_zstart(n):
        if n > 0:
            all_in(quarters(n, 3), wy_r.at[n + 2])
        for r in (1, 3, 2):
            if n == 0:
                all_in(w_quarter(n, shard(r), z), wy_r.at[r - 1])
            for dz in (1, 3, 2):
                w_z(n, r, dz).start()

    def w_xstart(n):
        if n > 0:
            all_in(quarters(n, 9), wz_r.at[n + 2])
        for r in (1, 3, 2):
            if n == 0:
                all_in(quarters(n, 3), wz_r.at[r - 1])
            w_x(n, r).start()
            if n == 3:
                wo_pass(2 * ((4 - r) % 4)).start()

    def w_finish(n):
        all_in(blocks(n, 4), wx_r.at[n])

    def wo_pass(n, recv=False):
        f_ = ((y + n // 2) % 4) * 2 + (xl + n % 2) % 2
        ref = wo_all.at[rows(f_ * 128 + ((1 - c) if recv else c) * 64, 64)]
        return remote(ref, ref, wp_s.at[0], wp_r.at[0], sibling)

    def wo_pass_x():
        all_in(blocks(3, 4), wx_r.at[3])
        for r in range(4):
            wo_pass(2 * ((4 - r) % 4) + 1).start()

    def wo_pass_finish():
        all_in(wo_all.at[pl.ds(0, 448)], wp_r.at[0])

    for n in (0, 3, 2, 1):
        w_ystart(n)
    w_own(0)

    def piece(buf, y_, c_):
        return buf.at[rows((((y_ + 4) % 4) * 2 + c_) * PIECE, PIECE)]

    def half(buf, y_, c_, h):
        return buf.at[rows((((y_ + 4) % 4) * 2 + c_) * PIECE + h * 64, 64)]

    def ag(buf, k, n, recv=False):
        if n in (0, 8):
            h = 0 if n == 0 else 1
            ref, to = (half(buf, y - 1, c, h) if recv else half(buf, y, c, h)), y_up
        elif n in (1, 9):
            h = 1 if n == 1 else 0
            ref, to = (half(buf, y + 1, c, h) if recv else half(buf, y, c, h)), y_dn
        elif n == 2:
            ref, to = (piece(buf, y, 1 - c) if recv else piece(buf, y, c)), sibling
        elif n == 3:
            ref, to = (half(buf, y - 2, c, 0) if recv else half(buf, y - 1, c, 0)), y_up
        elif n == 4:
            ref, to = (piece(buf, y - 1, 1 - c) if recv else piece(buf, y - 1, c)), sibling
        elif n == 5:
            ref, to = (half(buf, y + 2, c, 1) if recv else half(buf, y + 1, c, 1)), y_dn
        elif n == 6:
            ref, to = (piece(buf, y + 1, 1 - c) if recv else piece(buf, y + 1, c)), sibling
        else:
            ref, to = (piece(buf, y + 2, 1 - c) if recv else piece(buf, y + 2, c)), sibling
        return remote(ref, ref, ag_s.at[k], ag_r.at[k, (0, 0, 3, 2, 4, 2, 5, 6, 1, 1)[n]], to)

    def ag_start(buf, k):
        for n in (0, 1, 2, 8, 9):
            ag(buf, k, n).start()

    def ag_near(buf, k):
        all_in(buf.at[pl.ds(0, PIECE)], ag_r.at[k, 0])
        ag(buf, k, 3).start()
        ag(buf, k, 5).start()

    def ag_pass(buf, k):
        all_in(buf.at[pl.ds(0, PIECE)], ag_r.at[k, 1])
        ag(buf, k, 4).start()
        ag(buf, k, 6).start()

    def ag_far(buf, k):
        all_in(buf.at[pl.ds(0, PIECE)], ag_r.at[k, 2])
        ag(buf, k, 7).start()

    def ag_finish(buf, k):
        for n in (2, 4, 6, 7):
            ag(buf, k, n, True).wait_recv()

    def ag_run(buf, k, consume, after_pass=None, after_far=None):
        def step(i, carry):
            @pl.when(i == 0)
            def _():
                ag(buf, k, 2, True).wait_recv()

            @pl.when(i == 1)
            def _():
                ag_pass(buf, k)
                if after_pass is not None:
                    after_pass()
                ag(buf, k, 4, True).wait_recv()

            @pl.when(i == 2)
            def _():
                ag(buf, k, 6, True).wait_recv()
                ag_far(buf, k)

            @pl.when(i == 3)
            def _():
                if after_far is not None:
                    after_far()
                ag(buf, k, 7, True).wait_recv()

            consume((y + (3 * ((i * (i + 1)) // 2)) % 4) % 4)

            @pl.when(i == 0)
            def _():
                if k > 0:
                    ag_near(buf, k)

            return carry

        lax.fori_loop(0, 4, step, 0)

    def held(k):
        return part.at[1 if k == 2 else 0]

    def own_part(k, a):
        return held(k)[a, rows(c * PIECE, PIECE), :].astype(F32)

    def c_sib(k, a):
        src = held(k).at[a, rows((1 - c) * PIECE, PIECE)]
        return remote(src, sib.at[k, a], sib_ss.at[k - 1], sib_rs.at[k - 1, a], sibling)

    def c_far(k, n):
        return remote(far_s.at[k, pl.ds(64 * n, 64)], far_r.at[k, n], far_ss.at[k - 1], far_rs.at[k - 1], y_up if n == 0 else y_dn)

    def c_fin(k, n, h):
        cut = pl.ds(64 * h, 64)
        return remote(fin_s.at[k, n, cut], fin_r.at[k, n, cut], fin_ss.at[k - 1], fin_rs.at[k - 1], y_up if n == 0 else y_dn)

    def rs_put(k, a, value):
        held(k)[a] = value.astype(BF16)
        c_sib(k, a).start()

    def rs_pair(k, a):
        c_sib(k, a).wait_recv()
        return own_part(k, a) + sib[k, a].astype(F32)

    def rs_far(k):
        far_s[k] = rs_pair(k, (y + 2) % 4).astype(BF16)
        c_far(k, 0).start()
        c_far(k, 1).start()

    def rs_near(k, n):
        fin_s[k, n] = rs_pair(k, (y + 1 + 2 * n) % 4).astype(BF16)
        c_fin(k, n, 1 - n).start()

    def rs_mid(k):
        all_in(far_r.at[k], far_rs.at[k - 1])
        for n in (0, 1):
            cut = pl.ds(64 * n, 64)
            fin_s[k, n, cut] = (fin_s[k, n, cut].astype(F32) + far_r[k, n].astype(F32)).astype(BF16)
            c_fin(k, n, n).start()

    def rs_finish(k):
        total = rs_pair(k, y)
        all_in(fin_r.at[k], fin_rs.at[k - 1])
        return total + fin_r[k, 0].astype(F32) + fin_r[k, 1].astype(F32)

    w_zstart(0)
    all_in(vall.at[pl.ds(0, 7)], vec_r.at[0])
    all_sent(vall.at[pl.ds(0, 7)], vec_s.at[0])

    def gathered(row):
        return jnp.concatenate([vall[i, row : row + 1, :] for i in range(8)], axis=1)

    swap_wait(x_in, x_own, 0)
    x32 = x_own[...].astype(F32)
    normed_all[rows(j * PIECE, PIECE), :] = (x32 * rms_scale(x32) * gathered(0)).astype(BF16)
    ag_start(normed_all, 0)
    w_xstart(0)
    swap_start(cot_in, cot_own, 1)
    w_zstart(3)
    w_own(3)
    w_zstart(2)
    w_own(2)
    w_zstart(1)
    w_own(1)
    ag_near(normed_all, 0)
    for load in loads[7:]:
        load.wait()
    w_finish(0)

    doc = jnp.broadcast_to(doc_row, (8, D)).astype(F32).T[:, :1]
    feature = lax.broadcasted_iota(jnp.int32, (D, 128), 1)
    k_all[:, 128:] = jnp.where(
        feature == 0, OTHER_DOC * (1.0 - doc), jnp.where(feature == 1, OTHER_DOC * doc, 0.0)
    ).astype(BF16)
    q_more = jnp.where(feature == 0, doc, jnp.where(feature == 1, 1.0 - doc, 0.0)).astype(BF16)
    for i in range(4):
        for h in range(2):
            q_two[i, BLOCK * h : BLOCK * h + BLOCK, 128:] = q_more[BLOCK * i : BLOCK * i + BLOCK]

    def two_heads(value):
        first_head = lax.broadcasted_iota(jnp.int32, value.shape, 1) < HEAD_DIM
        return jnp.concatenate([jnp.where(first_head, value, 0.0), jnp.where(first_head, 0.0, value)], axis=0)

    def own_quarters(value):
        return jnp.concatenate([value[:HEAD_DIM, :BLOCK], value[HEAD_DIM:, BLOCK:]], axis=0)

    def project(yy):
        cut = rows(yy * BLOCK, BLOCK)
        lin = nn(normed_all[cut, :], wqkv[...])
        cos = cos_ref[cut, :]
        sin = sin_ref[cut, :]
        bias = vall[pl.ds(j, 1)][0]
        q_lin = lin[:, :128] + bias[2:3, :]
        k_lin = lin[:, 128:256] + bias[3:4, :]
        v_lin = lin[:, 256:] + bias[4:5, :]
        q = (q_lin * cos + half_turn(q_lin) * sin) * (0.125 * LOG2_E)
        k32 = k_lin * cos + half_turn(k_lin) * sin
        q_two[pl.ds(yy, 1), :, :128] = two_heads(q).astype(BF16)[None]
        k_all[cut, :128] = k32.astype(BF16)
        v_all[cut, :] = v_lin.astype(BF16)
        k_t[:, cut] = k32.T.astype(BF16)
        v_t[:, cut] = v_lin.T.astype(BF16)

    def cot_start():
        swap_wait(cot_in, cot_own, 1)
        cot_all[rows(j * PIECE, PIECE), :] = cot_own[...]
        ag_start(cot_all, 1)

    ag_run(normed_all, 0, project, lambda: w_xstart(3), cot_start)

    def attend(i):
        width = (i + 1) * BLOCK
        before = i * BLOCK
        cut = slice(before, width)
        scores = nt(k_all[:width, :], q_two[i])
        key_at = lax.broadcasted_iota(jnp.int32, (BLOCK, 2 * BLOCK), 0)
        query_at = lax.broadcasted_iota(jnp.int32, (BLOCK, 2 * BLOCK), 1) % BLOCK
        last = jnp.where(key_at <= query_at, scores[before:], NEG)
        top = jnp.max(last, axis=0, keepdims=True)
        if i > 0:
            top = jnp.maximum(top, jnp.max(scores[:before], axis=0, keepdims=True))
        weights = jnp.exp2(last - top)
        total = jnp.sum(weights, axis=0, keepdims=True)
        p_t[i, before:width, :] = weights.astype(BF16)
        if i > 0:
            weights = jnp.exp2(scores[:before] - top)
            total = total + jnp.sum(weights, axis=0, keepdims=True)
            p_t[i, :before, :] = weights.astype(BF16)
        inverse = 1.0 / total
        inv[i : i + 1, :] = inverse
        both = nn(v_t[:, :width], p_t[i, :width, :]) * inverse
        mixed_t[:, cut] = own_quarters(both)
        mixed[cut, :] = mixed_t[:, cut].T.astype(BF16)
        for m in (2 * i, 2 * i + 1):
            mix_start(m)

    def mix(m, sender):
        return remote(
            mixed.at[rows(m * PIECE, PIECE), :], mixed_own.at[:, rows(sender * 128, 128)],
            mx_s.at[0], mx_r.at[0], dev(x, m // 2, z, m % 2),
        )

    def mix_start(m):
        @pl.when(j != m)
        def _():
            mix(m, j).start()

        @pl.when(j == m)
        def _():
            mixed_own[:, rows(j * 128, 128)] = mixed[m * PIECE : (m + 1) * PIECE, :]

    w_xstart(2)
    attend(0)
    attend(1)
    w_xstart(1)
    attend(2)
    wo_pass_x()
    attend(3)
    ag_near(cot_all, 1)
    ag_pass(cot_all, 1)
    wo_pass_finish()
    all_in(mixed_own.at[:, pl.ds(0, 896)], mx_r.at[0])
    all_sent(mixed.at[pl.ds(0, 896)], mx_s.at[0])

    hidden[...] = x_own[...].astype(F32) + nn(mixed_own[...], wo_all[...])
    hid = hidden[...]
    mlp_all[rows(j * PIECE, PIECE), :] = (hid * rms_scale(hid) * gathered(1)).astype(BF16)
    ag_start(mlp_all, 2)
    ag_far(cot_all, 1)
    w_finish(2)
    ag_finish(cot_all, 1)

    def active_back(i, carry):
        cut = rows(i * BLOCK, BLOCK)
        g_act[cut, :] = nt(cot_all[cut, :], wdn[...])
        return carry

    lax.fori_loop(0, 4, active_back, 0)
    w_finish(1)

    unit = lax.broadcasted_iota(jnp.int32, (1, FB), 1)
    low_edge = 128 * (j // 7)
    high_edge = FB - 128 * ((j // 6) * (1 - j // 7))
    live = (unit >= low_edge) & (unit < high_edge)

    def feed(yy):
        cut = rows(yy * BLOCK, BLOCK)
        both = nn(mlp_all[cut, :], wgu[...])
        gate = both[:, :FB]
        up = both[:, FB:]
        sig = 1.0 / (1.0 + jnp.exp(-gate))
        silu = gate * sig
        back = jnp.where(live, g_act[cut, :], 0.0)
        act = jnp.where(live, silu * up, 0.0)
        active[cut, :] = act.astype(BF16)
        g_gu[cut, :FB] = (back * up * sig * (1.0 + gate * (1.0 - sig))).astype(BF16)
        g_gu[cut, FB:] = (back * silu).astype(BF16)
        rs_put(1, yy, nt(g_gu[cut, :], wgu[...]))

    ag_run(mlp_all, 2, feed)
    rs_far(1)

    terms = (dga, dgb, ddn, dqa, dqb, dwo)
    term_in = (ra, rb, rd, rqa, rqb, rw)
    halfway = (ha, hb, hd, hqa, hqb, hw)
    half_in = (sa, sb, sd, sqa, sqb, sw)

    def first(n, r):
        if n in (0, 3, 5):
            src, to = terms[n].at[(x + r) % 4], dev(x + r, y, z, c)
        else:
            src, to = terms[n].at[:, (z + r) % 4], dev(x, y, z + r, c)
        return remote(src, term_in[n].at[r - 1], f1_s.at[0], f1_r.at[n], to)

    def second(n, r):
        if n in (0, 3, 5):
            src, to = halfway[n].at[(z + r) % 4], dev(x, y, z + r, c)
        else:
            src, to = halfway[n].at[(x + r) % 4], dev(x + r, y, z, c)
        return remote(src, half_in[n].at[r - 1], f2_s.at[0], f2_r.at[n], to)

    def first_start(n):
        for r in (1, 3, 2):
            first(n, r).start()

    def first_sum(n):
        total = (terms[n][x] if n in (0, 3, 5) else terms[n][:, z]).astype(F32)
        all_in(term_in[n], f1_r.at[n])
        for r in (1, 3, 2):
            total = total + term_in[n][r - 1].astype(F32)
        halfway[n][...] = total.astype(BF16)
        for r in (1, 3, 2):
            second(n, r).start()

    def second_sum(n):
        total = halfway[n][z if n in (0, 3, 5) else x].astype(F32)
        all_in(half_in[n], f2_r.at[n])
        for r in (1, 3, 2):
            total = total + half_in[n][r - 1].astype(F32)
        return total.astype(BF16)

    def chunk(t, xl_):
        return (t % 2) * 2 + xl_, t // 2

    def grad_gu(i, carry):
        got = tn(mlp_all[:, rows(i * BLOCK, BLOCK)], g_gu[...]).astype(BF16)
        for xl_ in range(2):
            for t in range(8):
                x_, z_ = chunk(t, xl_)
                share = got[xl_ * 128 + t * 16 : xl_ * 128 + t * 16 + 16]
                dga[x_, z_, i] = share[:, :512]
                dgb[x_, z_, i] = share[:, 512:]
        return carry

    def grad_dn(i, carry):
        got = nn(active_t[...], cot_all[:, rows(i * BLOCK, BLOCK)]).astype(BF16)
        for xl_ in range(2):
            for t in range(8):
                x_, z_ = chunk(t, xl_)
                ddn[x_, z_, i] = got[t * 48 : t * 48 + 48, xl_ * 128 : xl_ * 128 + 128]
        return carry

    def grad_qkv(part_ref, base):
        def go(i, carry):
            got = tn(normed_all[:, rows((base + i) * BLOCK, BLOCK)], g_qkv[...]).astype(BF16)
            for xl_ in range(2):
                for t in range(8):
                    x_, z_ = chunk(t, xl_)
                    part_ref[x_, z_, i] = got[xl_ * 128 + t * 16 : xl_ * 128 + t * 16 + 16]
            return carry

        lax.fori_loop(0, 2, go, 0)

    def grad_wo():
        got = tn(mixed[...], branch_all[...]).astype(BF16)
        for h in range(2):
            for t in range(8):
                x_, z_ = chunk(t, (h + c) % 2)
                dwo[pl.ds(x_, 1), z_] = got[h * 64 : h * 64 + 64, t * 128 : t * 128 + 128][None]

    lax.fori_loop(0, 4, grad_gu, 0)
    rs_near(1, 0)
    rs_near(1, 1)
    first_start(1)
    first_start(0)
    rs_mid(1)
    active_t[...] = active[...].T
    lax.fori_loop(0, 4, grad_dn, 0)
    first_start(2)

    grad = rs_finish(1)
    hid = hidden[...]
    scale = rms_scale(hid)
    scaled = grad * gathered(1)
    back = scale * scaled - hid * (scale * scale * scale) * jnp.mean(scaled * hid, axis=-1, keepdims=True)
    g_hidden[...] = cot_own[...].astype(F32) + back
    branch_all[rows(j * PIECE, PIECE), :] = g_hidden[...].astype(BF16)

    def unmix_term(i, carry):
        cut = rows(i * BLOCK, BLOCK)
        mixed_grad[:, cut] = nt(branch_all[rows(j * PIECE, PIECE), :], wo_all[cut, :]).astype(BF16)
        return carry

    lax.fori_loop(0, 4, unmix_term, 0)
    g_mixed[rows(j * PIECE, PIECE), :] = mixed_grad[:, rows(j * 128, 128)]

    def unmix(m, sender):
        return remote(
            mixed_grad.at[:, rows(m * 128, 128)], g_mixed.at[rows(sender * PIECE, PIECE), :],
            um_s.at[0], um_r.at[0], dev(x, m // 2, z, m % 2),
        )

    def unmix_start(r, carry):
        unmix((j + r) % 8, j).start()
        return carry

    lax.fori_loop(1, 8, unmix_start, 0)
    gain_two = jnp.sum(grad * hid * scale, axis=0, keepdims=True)
    gk_acc[...] = jnp.zeros_like(gk_acc)
    gv_acc[...] = jnp.zeros_like(gv_acc)

    def output_term(i, carry):
        rs_put(2, i, nn(active[rows(i * BLOCK, BLOCK), :], wdn[...]))
        return carry

    lax.fori_loop(0, 4, output_term, 0)
    first_sum(1)
    first_sum(0)
    all_in(g_mixed.at[pl.ds(0, 896)], um_r.at[0])
    all_sent(mixed_grad.at[:, pl.ds(0, 896)], um_s.at[0])
    all_sent(sib.at[1], sib_ss.at[0])
    ag_start(branch_all, 3)

    def along_y(n, r, recv=False):
        src = (sum_gu, sum_dn, sum_qkv)[n].at[(y + r) % 4]
        dst = (all_gu, all_dn, all_qkv)[n].at[place, c, (y + 4 - r) % 4 if recv else y]
        return remote(src, dst, ya_s.at[n], ya_r.at[n], dev(x, y + r, z, c))

    def share(n):
        total, every = ((sum_gu, all_gu), (sum_dn, all_dn), (sum_qkv, all_qkv))[n]
        if n == 0:
            total[:, :, :512] = second_sum(0)
            total[:, :, 512:] = second_sum(1)
        elif n == 1:
            total[...] = second_sum(2)
        else:
            total[:2] = second_sum(3)
            total[2:] = second_sum(4)
        for r in (1, 3, 2):
            along_y(n, r).start()
        every[place, c, y] = total[y]

    arrays = (all_gu, all_dn, all_wo, all_qkv)

    def spot(n, r, c_):
        return arrays[n].at[((z + 4 - r % 4) % 4) * 2 + (xh + r // 4) % 2, c_]

    def gd(n, r, recv=False):
        if n == 2:
            ref = spot(n, r if recv else 0, c)
            return remote(ref, ref, gd_s.at[n - 2], gd_r.at[3 if n == 2 else (0, 1, 1, 1, 0, 2, 2, 2)[r]], dev(x + 2 * (r // 4), y, z + r % 4, c))
        ref = spot(n, r if recv else 4 * (r // 5), c)
        return remote(ref, ref, gd_s.at[n - 2], gd_r.at[3 if n == 2 else (0, 1, 1, 1, 0, 2, 2, 2)[r]], dev(x + 2 * (r == 4), y, z + r % 4, c))

    def gp(n, r, recv=False):
        ref = spot(n, r, (1 - c) if recv else c)
        return remote(ref, ref, gp_s.at[n - 2], gp_r.at[n - 2], sibling)

    def pair(n, z_, c_):
        return arrays[n].at[pl.ds(((z_ + 4) % 4) * 2, 2), c_]

    def single(n, z_, h):
        return arrays[n].at[pl.ds(((z_ + 4) % 4) * 2 + h, 1), c]

    def ring(n, k, recv=False):
        if k == 0:
            ref, to = single(n, z, (1 - xh) if recv else xh), dev(x + 2, y, z, c)
        elif k == 1:
            ref, to = pair(n, z - 1 if recv else z, c), dev(x, y, z + 1, c)
        elif k == 2:
            ref, to = pair(n, z + 1 if recv else z, c), dev(x, y, z + 3, c)
        elif k == 3:
            ref, to = single(n, z - 2 if recv else z - 1, 0), dev(x, y, z + 1, c)
        elif k == 4:
            ref, to = single(n, z + 2 if recv else z + 1, 1), dev(x, y, z + 3, c)
        else:
            ref, to = pair(n, z + (k - 5), (1 - c) if recv else c), sibling
        return remote(ref, ref, rg_s.at[n, k // 5], rg_r.at[n, (0, 1, 1, 2, 2, 3, 3, 3, 3)[k]], to)

    def ring_one(n):
        all_in(arrays[n].at[place, c, pl.ds(0, 3)], ya_r.at[n])
        ring(n, 0).start()

    def ring_two(n):
        ring(n, 0, True).wait_recv()
        for k in (1, 2, 5):
            ring(n, k).start()

    def ring_three(n):
        all_in(arrays[n].at[pl.ds(0, 4), c], rg_r.at[n, 1])
        for k in (3, 4, 8, 6):
            ring(n, k).start()

    def ring_four(n):
        all_in(arrays[n].at[pl.ds(0, 2), c], rg_r.at[n, 2])
        ring(n, 7).start()

    def ring_five(n):
        all_in(arrays[n].at[:, c], rg_r.at[n, 3])

    def spread_start(n):
        if n != 2:
            all_in(arrays[n].at[place, c, pl.ds(0, 3)], ya_r.at[min(n, 2)])
        for r in (6, 4, 5, 7, 2, 1, 3) if n == 2 else (4, 2, 1, 3):
            gd(n, r).start()
        gp(n, 0).start()

    def spread_next(n):
        if n == 3:
            gd(n, 4, True).wait_recv()
            for r in (6, 5, 7):
                gd(n, r).start()
            gp(n, 4).start()

    def spread_pass(n):
        if n == 2:
            all_in(arrays[n].at[pl.ds(0, 7), c], gd_r.at[3])
            for r in range(1, 8):
                gp(n, r).start()
        else:
            for i, steps in ((1, (1, 3, 2)), (2, (5, 7, 6))):
                all_in(arrays[n].at[pl.ds(0, 3), c], gd_r.at[i])
                for r in steps:
                    gp(n, r).start()

    def spread_finish(n):
        all_in(arrays[n].at[:, c], gp_r.at[n - 2])

    def unturn(value, cut):
        value = value.astype(BF16).astype(F32)
        return (value * cos_ref[cut, :] - half_turn(value) * sin_ref[cut, :]).astype(BF16)

    def attend_back(i):
        width = (i + 1) * BLOCK
        cut = slice(i * BLOCK, width)
        inverse = inv[i : i + 1, :]
        grad_t = g_mixed[cut, :].astype(F32).T
        scaled = jnp.concatenate([grad_t[:HEAD_DIM] * inverse[:, :BLOCK], grad_t[HEAD_DIM:] * inverse[:, BLOCK:]], axis=0)
        scaled = scaled.astype(BF16).astype(F32)
        products = scaled * mixed_t[:, cut]
        delta = jnp.concatenate(
            [jnp.sum(products[:HEAD_DIM], axis=0, keepdims=True), jnp.sum(products[HEAD_DIM:], axis=0, keepdims=True)], axis=1
        )
        grad_two = two_heads(scaled.T).astype(BF16)
        weights = p_t[i, :width, :]
        gv_acc[:width, :] += nn(weights, grad_two)
        g_probs = nt(v_all[:width, :], grad_two)
        g_scores = (weights.astype(F32) * (g_probs - delta)).astype(BF16)
        gk_acc[:width, :] += nn(g_scores, q_two[i, :, :128])
        g_query = own_quarters(nn(k_t[:, :width], g_scores)) * 0.125
        g_qkv[cut, :128] = unturn(g_query.T, cut)

    def block_back(i):
        cut = slice(i * BLOCK, (i + 1) * BLOCK)
        attend_back(i)
        g_qkv[cut, 128:256] = unturn(gk_acc[cut, :] * (1.0 / LOG2_E), cut)
        g_qkv[cut, 256:] = gv_acc[cut, :].astype(BF16)
        rs_put(3, i, nt(g_qkv[cut, :], wqkv[...]))

    block_back(3)
    block_back(2)
    share(0)
    first_sum(2)
    ag_near(branch_all, 3)
    block_back(1)
    block_back(0)
    rs_far(3)
    grad_qkv(dqb, 2)
    first_start(4)
    ring_one(0)
    grad_qkv(dqa, 0)
    first_start(3)
    rs_near(3, 0)
    rs_near(3, 1)
    ag_pass(branch_all, 3)
    share(1)
    ag_far(branch_all, 3)
    rs_mid(3)
    ring_two(0)
    first_sum(4)
    first_sum(3)
    ring_one(1)
    rs_far(2)
    ag_finish(branch_all, 3)
    grad_wo()
    first_start(5)
    rs_near(2, 0)
    rs_near(2, 1)

    grad = rs_finish(3)
    scale = rms_scale(x32)
    scaled = grad * gathered(0)
    back = scale * scaled - x32 * (scale * scale * scale) * jnp.mean(scaled * x32, axis=-1, keepdims=True)
    ig_send[...] = (g_hidden[...] + back).astype(BF16)
    swap_start(ig_send, in_grad, 3)
    share(2)
    ring_two(1)
    first_sum(5)

    gain_one = jnp.sum(grad * x32 * scale, axis=0, keepdims=True)
    vs[...] = jnp.zeros_like(vs)
    for i in range(8):
        vs[i, 0:1, :] = gain_one[:, 128 * i : 128 * i + 128]
        vs[i, 1:2, :] = gain_two[:, 128 * i : 128 * i + 128]
    bias_sum = jnp.sum(g_qkv[...].astype(F32), axis=0, keepdims=True)
    for i in range(3):
        vs[pl.ds(j, 1), 2 + i : 3 + i, :] = bias_sum[:, 128 * i : 128 * i + 128][None]

    def v1_copy(r):
        return remote(vs.at[(f + r) % 8], vr.at[r - 1], v1_ss.at[0], v1_rs.at[0], (s, (f + r) % 8))

    def v1_start(r, carry):
        v1_copy(r).start()
        return carry

    lax.fori_loop(1, 8, v1_start, 0)
    ring_three(0)
    spread_start(3)
    ring_three(1)
    rs_mid(2)
    wo_send[...] = second_sum(5)
    swap_start(wo_send, all_wo.at[place, (c + moves) % 2], 4)
    all_in(vr, v1_rs.at[0])
    all_sent(vr, v1_ss.at[0])
    v2s[...] = jnp.sum(vr[...], axis=0) + vs[pl.ds(f, 1)][0]

    def v2_copy(r):
        to = dev(x + 2 * (r // 4), y, z + r % 4, c)
        return remote(v2s, v2r.at[r - 1], v2_ss.at[0], v2_rs.at[0], to)

    def v2_start(r, carry):
        v2_copy(r).start()
        return carry

    lax.fori_loop(1, 8, v2_start, 0)
    spread_next(3)
    swap_wait(wo_send, all_wo.at[place, c], 4)
    spread_start(2)
    lo_send[...] = (hidden[...] + rs_finish(2)).astype(BF16)
    swap_start(lo_send, layer_out, 2)
    all_in(v2r, v2_rs.at[0])
    all_sent(v2r, v2_ss.at[0])
    v3s[...] = jnp.sum(v2r[...], axis=0) + v2s[...]
    v3_copy = remote(v3s, v3r, v3_ss.at[0], v3_rs.at[0], sibling)
    v3_copy.start()
    ring_four(0)
    spread_pass(3)
    ring_four(1)
    spread_next(2)
    spread_pass(2)
    v3_copy.wait()
    vec_out[...] = v3s[...] + v3r[...]
    swap_wait(lo_send, layer_out, 2)
    swap_wait(ig_send, in_grad, 3)
    for n in (0, 1):
        ring_five(n)
    for n in (3, 2):
        spread_finish(n)

    all_sent(wo_all.at[pl.ds(0, 3 * 64)], wy_s.at[0])
    all_sent(wo_all.at[pl.ds(0, 9 * 64)], wz_s.at[0])
    all_sent(wo_all, wx_s.at[0])
    all_sent(wo_all.at[pl.ds(0, 448)], wp_s.at[0])
    for k, buf in enumerate((normed_all, cot_all, mlp_all, branch_all)):
        all_sent(buf.at[pl.ds(0, 896)], ag_s.at[k])
    for k in range(1, 4):
        if k > 1:
            all_sent(sib.at[k], sib_ss.at[k - 1])
        all_sent(far_s.at[k], far_ss.at[k - 1])
        all_sent(fin_s.at[k], fin_ss.at[k - 1])
    all_sent(p_t.at[:, pl.ds(0, 624)], f1_s.at[0])
    all_sent(p_t.at[0, pl.ds(0, 624)], f2_s.at[0])
    for n in (0, 1, 3):
        all_sent(arrays[n].at[place, c, pl.ds(0, 3)], ya_s.at[min(n, 2)])
    for n in (0, 1):
        all_sent(arrays[n].at[pl.ds(0, 7), c], rg_s.at[n, 0])
        all_sent(arrays[n].at[:, c], rg_s.at[n, 1])
    for n in (2, 3):
        all_sent(arrays[n].at[pl.ds(0, 7), c], gd_s.at[n - 2])
        all_sent(arrays[n].at[:, c], gp_s.at[n - 2])


def fused_layer(*args):
    def vmem(*shape, dtype=BF16):
        return pltpu.VMEM(shape, dtype)

    def dma(*shape):
        return pltpu.SemaphoreType.DMA(shape)

    full = vmem(D, D)
    shares = ((4, 16, 512), (4, 16, 256), (4, 48, 128), (2, 16, FB), (2, 16, FB), (64, 128))
    scratch = [
        vmem(D, 128, dtype=F32), vmem(D, 128, dtype=F32), vmem(8, 128, dtype=F32),
        vmem(PIECE, D), vmem(PIECE, D), vmem(PIECE, D, dtype=F32), vmem(PIECE, D, dtype=F32),
        full, vmem(D, FB), vmem(D, 2 * FB), vmem(FB, D), vmem(8, 8, 128, dtype=F32),
        full, full, full, full,
        vmem(4, 2 * BLOCK, 256), vmem(D, 256), vmem(D, 128), vmem(128, D), vmem(128, D),
        vmem(4, D, 2 * BLOCK), vmem(8, 2 * BLOCK, dtype=F32), vmem(128, D, dtype=F32), vmem(D, 128), vmem(PIECE, D), vmem(PIECE, D),
        vmem(D, FB, dtype=F32), vmem(D, FB), vmem(FB, D), vmem(D, 2 * FB), vmem(D, 128),
        vmem(D, 128, dtype=F32), vmem(D, 128, dtype=F32), vmem(D, FB),
        vmem(2, 4, BLOCK, D), vmem(4, 4, PIECE, D), vmem(4, PIECE, D), vmem(4, 2, 64, D), vmem(4, 2, PIECE, D), vmem(4, 2, PIECE, D),
        *(vmem(4, 4, *dims) for dims in shares),
        *(vmem(3, 4, *dims) for dims in shares),
        *(vmem(4, *dims) for dims in shares),
        *(vmem(3, *dims) for dims in shares),
        vmem(64, 128), vmem(4, 16, 2 * FB), vmem(4, 48, 128), vmem(4, 16, FB),
        vmem(PIECE, D), vmem(PIECE, D),
        vmem(8, 8, 128, dtype=F32), vmem(7, 8, 128, dtype=F32), vmem(8, 128, dtype=F32), vmem(7, 8, 128, dtype=F32),
        vmem(8, 128, dtype=F32), vmem(8, 128, dtype=F32),
        dma(6), dma(5), dma(5), dma(1), dma(1), dma(1), dma(6), dma(1), dma(6), dma(1), dma(4),
        dma(1), dma(1), dma(1), dma(1), dma(1), dma(1), dma(4), dma(4, 7),
        dma(3), dma(3, 4), dma(3), dma(3), dma(3), dma(3),
        dma(1), dma(6), dma(1), dma(6), dma(3), dma(3), dma(2, 2), dma(2, 4), dma(2), dma(4), dma(2), dma(2),
        dma(1), dma(1), dma(1), dma(1), dma(1), dma(1),
    ]
    anywhere = pl.BlockSpec(memory_space=pl.ANY)
    inside = pl.BlockSpec(memory_space=pltpu.VMEM)

    def out(*shape, dtype=BF16):
        return pltpu.VMEM(shape, dtype)

    return pl.pallas_call(
        layer_kernel,
        out_shape=(
            out(PIECE, D), out(PIECE, D), out(8, 2, 4, 16, 2 * FB), out(8, 2, 4, 48, 128), out(8, 2, 64, 128),
            out(8, 2, 4, 16, FB), out(8, 128, dtype=F32),
        ),
        in_specs=[anywhere] * 11 + [inside] * 6,
        out_specs=[inside] * 7,
        scratch_shapes=scratch,
        compiler_params=pltpu.CompilerParams(
            collective_id=0, has_side_effects=True, vmem_limit_bytes=57 * 1024 * 1024
        ),
        name="layer",
    )(*args)


def spread_kernel(
    lo_in, ig_in, gu, dn, wo, qkv, vec,
    lo, ig, d_gain_a, d_q, d_k, d_v, d_bq, d_bk, d_bv, d_o, d_gain_m, d_gate, d_up, d_down,
    ig_v, q_v, k_v, v_v, o_v, gate_v, up_v, down_v, sems,
):
    stores = []

    def store(src, dst):
        copy = pltpu.make_async_copy(src, dst, sems.at[len(stores)])
        copy.start()
        stores.append(copy)

    for ref, row in ((d_gain_a, 0), (d_gain_m, 1), (d_bq, 2), (d_bk, 3), (d_bv, 4)):
        ref[...] = vec[row : row + 1, :]
    store(lo_in, lo)
    for m in range(8):
        first = 128 if m == 7 else 0
        count = 256 if m >= 6 else FB
        start = min(m, 6) * FB + (256 if m == 7 else 0)
        for t in range(8):
            low, high = max(48 * t, first), min(48 * t + 48, first + count)
            if low < high:
                down_v[start + low - first : start + high - first, :] = dn[
                    t, m % 2, m // 2, low - 48 * t : high - 48 * t, :
                ].astype(F32)
    store(down_v, d_down)
    for ref, off, dst in ((gate_v, 0, d_gate), (up_v, FB, d_up)):
        for m in range(8):
            first = 128 if m == 7 else 0
            count = 256 if m >= 6 else FB
            start = min(m, 6) * FB + (256 if m == 7 else 0)
            for t in range(8):
                cut = slice(16 * t, 16 * t + 16)
                ref[cut, start : start + count] = gu[t, m % 2, m // 2, :, off + first : off + first + count].astype(F32)
        store(ref, dst)
    for i, (ref, dst) in enumerate(((q_v, d_q), (k_v, d_k), (v_v, d_v))):
        for t in range(8):
            for m in range(8):
                ref[16 * t : 16 * t + 16, 128 * m : 128 * m + 128] = qkv[
                    t, m % 2, m // 2, :, 128 * i : 128 * i + 128
                ].astype(F32)
        store(ref, dst)
    flip = lax.axis_index("fsdp") % 2
    for t in range(8):
        for core in range(2):
            to = pl.ds(pl.multiple_of(64 * ((core + flip) % 2), 64), 64)
            o_v[to, 128 * t : 128 * t + 128] = wo[t, core].astype(F32)
    store(o_v, d_o)
    ig_v[...] = ig_in[...].astype(F32)
    store(ig_v, ig)
    for copy in stores:
        copy.wait()


def spread(*args):
    def out(*shape, dtype=F32):
        return jax.ShapeDtypeStruct(shape, dtype)

    inside = pl.BlockSpec(memory_space=pltpu.VMEM)
    anywhere = pl.BlockSpec(memory_space=pl.ANY)
    vec, square, wide, tall = out(1, 128), out(128, D), out(128, 2816), out(2816, 128)
    return pl.pallas_call(
        spread_kernel,
        out_shape=(
            out(PIECE, D, dtype=BF16), out(PIECE, D), vec, square, square, square, vec, vec, vec,
            square, vec, wide, wide, tall,
        ),
        in_specs=[inside] * 7,
        out_specs=[anywhere, anywhere, inside, anywhere, anywhere, anywhere, inside, inside, inside]
        + [anywhere, inside, anywhere, anywhere, anywhere],
        scratch_shapes=[pltpu.VMEM(o.shape, o.dtype) for o in (square,) * 5 + (wide, wide, tall)]
        + [pltpu.SemaphoreType.DMA((9,))],
        compiler_params=pltpu.CompilerParams(vmem_limit_bytes=24 * 1024 * 1024),
        name="spread",
    )(*args)


def rotary_tables():
    exponent = np.arange(HEAD_DIM // 2, dtype=np.float32) * np.float32(2.0 / HEAD_DIM)
    inverse = np.exp(np.float32(-math.log(THETA)) * exponent)
    angles = np.arange(D, dtype=np.float32)[:, None] * inverse
    cos, sin = np.cos(angles), np.sin(angles)
    return np.concatenate([cos] * 4, axis=1), np.concatenate([-sin, sin] * 2, axis=1)


def per_device(
    inputs, doc_ids, positions, attn_gain, query_weight, key_weight, value_weight,
    query_bias, key_bias, value_bias, out_weight, mlp_gain, gate_weight, up_weight,
    down_weight, cotangent,
):
    del positions
    cos, sin = rotary_tables()
    vectors = [v.reshape(1, 128) for v in (attn_gain, mlp_gain, query_bias, key_bias, value_bias)]
    blocks = fused_layer(
        inputs.reshape(PIECE, D), cotangent.reshape(PIECE, D),
        query_weight, key_weight, value_weight, out_weight, gate_weight, up_weight, down_weight,
        jnp.asarray(cos), jnp.asarray(sin), *vectors, doc_ids,
    )
    outs = list(spread(*blocks))
    outs[0] = outs[0].reshape(inputs.shape)
    outs[1] = outs[1].reshape(inputs.shape)
    return tuple(o.reshape(128) if o.shape == (1, 128) else o for o in outs)


def solution(mesh):
    rows_spec = P("fsdp", None)
    act = P("seq", "fsdp", None)
    vec = P("fsdp")
    return jax.shard_map(
        per_device,
        mesh=mesh,
        in_specs=(
            act, P(), P("seq", "fsdp"), vec, rows_spec, rows_spec, rows_spec, vec, vec, vec,
            rows_spec, vec, rows_spec, rows_spec, P(None, "fsdp"), act,
        ),
        out_specs=(
            act, act, vec, rows_spec, rows_spec, rows_spec, vec, vec, vec, rows_spec, vec,
            rows_spec, rows_spec, P(None, "fsdp"),
        ),
        check_vma=False,
    )
```
